128 devices in a mesh: gx: 8 (over z_lo, y), gy: 4 (over z_hi, core), gz: 4 (over x).
Axes of the slice: x: 4, y: 4, z: 4 (z_hi: 2, z_lo: 2; z = z_hi * 2 + z_lo), core: 2. Of those that a mesh axis runs over, the one named last changes fastest.
Arguments:
- positions: float32 [16, 4, 4, 3, 32], P('gx', 'gy', 'gz'), may hold values from 0 to 5, as said below
- counts: int32 [16, 4, 4], P('gx', 'gy', 'gz'), may hold values from 1 to 32, as said below
- scalars: bfloat16 [16, 4, 4, 32, 128], P('gx', 'gy', 'gz'), may hold values from -6 to 6
- vectors: bfloat16 [16, 4, 4, 32, 3, 128], P('gx', 'gy', 'gz'), may hold values from -6 to 6
- radial_in: bfloat16 [2, 8, 64], replicated, may hold values from -2 to 2
- radial_bias: float32 [2, 64], replicated, may hold values from -3 to 3
- radial_out: bfloat16 [2, 64, 512], replicated, may hold values from -0.75 to 0.75
- atom_in: bfloat16 [2, 128, 128], replicated, may hold values from -0.5 to 0.5
- atom_bias: float32 [2, 128], replicated, may hold values from -3 to 3
- atom_out: bfloat16 [2, 128, 512], replicated, may hold values from -0.5 to 0.5
- readout_in: bfloat16 [128, 64], replicated, may hold values from -0.5 to 0.5
- readout_out: float32 [64], replicated, may hold values from -0.75 to 0.75
Outputs:
- scalars_out: bfloat16 [16, 4, 4, 32, 128], P('gx', 'gy', 'gz')
- vectors_out: bfloat16 [16, 4, 4, 32, 3, 128], P('gx', 'gy', 'gz')
- energy: float32 [1], replicated
The draws below stay inside these ranges and needn't reach their ends.
Inputs may be any that keep to these rules, and one draw needn't show every extreme that they name: `counts`: some cell of every draw holds 32 atoms and some other cell one atom. `positions`: the slots of a cell sit on distinct sites of a jittered lattice, so that any two slots, also of neighbouring cells, lie at least 0.5 apart.
All inputs are finite; a program needn't handle non-finite values.
Results may differ from the reference program's by a relative error of at most 0.0075.
Values may be sent and summed in bfloat16 or wider, within the bound.
No kernel may reach another device: no remote copies, remote signals or barrier semaphores. Data moves between devices by JAX's collectives and lax.ppermute only.
A program may use at most 64 MiB of HBM per device.

```python
import math
import jax
import jax.numpy as jnp
from jax import lax

CHAN = 128
RADIAL = 64
BASIS = 8
FILTERS = 512
READOUT = 64
SLOTS = 32
LAYERS = 2
NX = 16
NY = 4
NZ = 4


def draw_counts(key, part):
    total = NX * NY * NZ
    key_extra, key_full, key_sparse = jax.random.split(key, 3)
    along = lax.broadcasted_iota(jnp.int32, (NX, NY, NZ), 0)
    level = along * (3 * SLOTS // 4) // NX
    extra = jax.random.randint(key_extra, (NX, NY, NZ), 1, SLOTS // 4 + 1)
    flat = jnp.minimum(level + extra, SLOTS).reshape(total)
    full_cell = jax.random.randint(key_full, (), 0, total)
    sparse_cell = (full_cell + 1 + jax.random.randint(key_sparse, (), 0, total - 1)) % total
    flat = flat.at[full_cell].set(SLOTS).at[sparse_cell].set(1)
    return flat.reshape(NX, NY, NZ).astype(jnp.int32)


def draw_positions(key, part):
    total = NX * NY * NZ
    key_order, key_shift = jax.random.split(key)

    def one_order(one_key):
        return jax.random.permutation(one_key, SLOTS)
    orders = jax.vmap(one_order)(jax.random.split(key_order, total))
    layers_z = SLOTS // 16
    site_x = (orders % 4).astype(jnp.float32)
    site_y = (orders // 4 % 4).astype(jnp.float32)
    site_z = (orders // 16).astype(jnp.float32)
    shift = jax.random.uniform(key_shift, (total, 3, SLOTS), jnp.float32, -0.3, 0.3)
    coords = jnp.stack([(site_x + 0.5 + shift[:, 0]) / 4.0, (site_y + 0.5 + shift[:, 1]) / 4.0, (site_z + 0.5 + shift[:, 2]) / layers_z], axis=1) * 5.0
    return coords.reshape(NX, NY, NZ, 3, SLOTS).astype(jnp.float32)


def level_of(key, shape, cuts, low, largest):
    def one(position, blocks):
        steps = jax.random.uniform(jax.random.fold_in(jax.random.fold_in(key, 6), position), (blocks,), jnp.float32, low / len(cuts), largest / len(cuts))
        return jnp.repeat(jnp.exp(steps), shape[position] // blocks).reshape((-1,) + (1,) * (len(shape) - position - 1))

    level = one(*cuts[0])
    for cut in cuts[1:]:
        level = level * one(*cut)
    return level


def normal_values(own_key, dims, scale, reach, pieces=(), kind=jnp.bfloat16):
    loudness = level_of(own_key, dims, pieces, -0.22, 0.18) if pieces else 1.0
    drawn = jax.random.normal(own_key, dims, jnp.float32) * scale * loudness
    return jnp.minimum(jnp.maximum(drawn, -reach), reach).astype(kind)


def setup_inputs(seed: int = 0) -> dict:
    keys = jax.random.split(jax.random.key(seed), 13)
    positions = draw_positions(jax.random.fold_in(keys[12], 71), 0)
    counts = draw_counts(jax.random.fold_in(keys[12], 71), 0)
    scalars = normal_values(keys[2], (NX, NY, NZ, SLOTS, CHAN), 1.0, 6.0, ((0, 8), (1, 4), (2, 4)))
    vectors = normal_values(keys[3], (NX, NY, NZ, SLOTS, 3, CHAN), 1.0, 6.0, ((0, 8), (1, 4), (2, 4)))
    radial_in = normal_values(keys[4], (LAYERS, BASIS, RADIAL), BASIS ** -0.5, 2.0)
    radial_bias = normal_values(keys[5], (LAYERS, RADIAL), 0.5, 3.0, (), jnp.float32)
    radial_out = normal_values(keys[6], (LAYERS, RADIAL, FILTERS), RADIAL ** -0.5, 0.75)
    atom_in = normal_values(keys[7], (LAYERS, CHAN, CHAN), CHAN ** -0.5, 0.5)
    atom_bias = normal_values(keys[8], (LAYERS, CHAN), 0.5, 3.0, (), jnp.float32)
    atom_out = normal_values(keys[9], (LAYERS, CHAN, FILTERS), CHAN ** -0.5, 0.5)
    readout_in = normal_values(keys[10], (CHAN, READOUT), CHAN ** -0.5, 0.5)
    readout_out = normal_values(keys[11], (READOUT,), READOUT ** -0.5, 0.75, (), jnp.float32)
    return {"positions": positions, "counts": counts, "scalars": scalars, "vectors": vectors, "radial_in": radial_in, "radial_bias": radial_bias, "radial_out": radial_out, "atom_in": atom_in, "atom_bias": atom_bias, "atom_out": atom_out, "readout_in": readout_in, "readout_out": readout_out}


cutoff = 5.0
message_scale = 0.5

def offsets_table():
    index = lax.broadcasted_iota(jnp.int32, (27, 3), 0)
    column = lax.broadcasted_iota(jnp.int32, (27, 3), 1)
    digit = jnp.where(column == 0, index // 9, jnp.where(column == 1, index // 3 % 3, index % 3))
    return (digit - 1).astype(jnp.float32)

def wrap_cells(field):
    widths = ((1, 1), (1, 1), (1, 1)) + ((0, 0),) * (field.ndim - 3)
    return jnp.pad(field, widths, mode='wrap')

def atom_gates(states, atom_in, atom_bias, atom_out):
    lead = states.shape[:-1]
    width = states.shape[-1]
    flat = states.reshape(-1, width)
    hidden = jax.nn.silu(jnp.dot(flat, atom_in, preferred_element_type=jnp.float32) + atom_bias).astype(jnp.bfloat16)
    gates = jnp.dot(hidden, atom_out, preferred_element_type=jnp.float32).astype(jnp.bfloat16)
    return gates.reshape(lead + (4, width))

def receiver_block(start, row_count, near_pos, near_live, own_pos, plain_side, gate_c, pair_g, radial_in, radial_bias, radial_out):
    slots = own_pos.shape[1]
    near_count = near_pos.shape[0]
    width = gate_c.shape[-1]
    mine = lax.dynamic_slice_in_dim(own_pos, start, row_count, 1).T
    displace = near_pos[None, :, :] - mine[:, None, :]
    row_index = start + lax.broadcasted_iota(jnp.int32, (row_count, near_count), 0)
    col_index = lax.broadcasted_iota(jnp.int32, (row_count, near_count), 1)
    itself = (col_index == row_index + 13 * slots).astype(jnp.float32)
    distance = jnp.sqrt(lax.optimization_barrier(jnp.sum(displace * displace, axis=-1)) + itself)
    unit = displace / distance[:, :, None]
    smooth = jnp.where(distance < cutoff, 0.5 * (jnp.cos(math.pi * distance / cutoff) + 1.0), 0.0)
    weight = smooth * near_live[None, :] * (1.0 - itself)
    basis_count = radial_in.shape[0]
    centers = lax.broadcasted_iota(jnp.float32, (basis_count,), 0) * (cutoff / (basis_count - 1))
    sharpness = 0.5 * ((basis_count - 1) / cutoff) ** 2
    basis = jnp.exp(-sharpness * (distance[:, :, None] - centers) ** 2).astype(jnp.bfloat16)
    hidden = jnp.dot(basis.reshape(-1, basis_count), radial_in, preferred_element_type=jnp.float32) + radial_bias
    hidden = jax.nn.silu(hidden).reshape(row_count, near_count, -1) * weight[:, :, None]
    edge = jnp.concatenate([hidden[:, :, None, :], hidden[:, :, None, :] * unit[:, :, :, None]], axis=2).astype(jnp.bfloat16)
    edge_plain = edge[:, :, 0, :].astype(jnp.float32)
    edge_turned = edge[:, :, 1:, :].astype(jnp.float32)
    scalar_part = jnp.einsum('rjh,jc->rhc', edge_plain, plain_side.astype(jnp.float32))
    along_part = jnp.einsum('rjkh,jf->rkhf', edge_turned, gate_c.astype(jnp.float32))
    project_part = jnp.einsum('rjkh,jkf->rhf', edge_turned, pair_g.astype(jnp.float32))
    filters = radial_out.astype(jnp.float32).reshape(-1, 4, width)
    term_a = scalar_part[:, :, :width]
    term_b = scalar_part[:, :, width:].reshape(row_count, -1, 3, width)
    scalar_delta = message_scale * (lax.optimization_barrier(jnp.sum(term_a * filters[None, :, 0, :], axis=1)) + lax.optimization_barrier(jnp.sum(project_part * filters[None, :, 3, :], axis=1)))
    vector_delta = message_scale * (lax.optimization_barrier(jnp.sum(term_b * filters[None, :, None, 1, :], axis=1)) + lax.optimization_barrier(jnp.sum(along_part * filters[None, None, :, 2, :], axis=2)))
    return (scalar_delta, vector_delta)

def cell_update(cell, geo_pad, feat_pad, scalar_state, vector_state, layer_params):
    radial_in, radial_bias, radial_out, atom_in, atom_bias, atom_out = layer_params
    grid_x, grid_y, grid_z, slots, width = scalar_state.shape
    at_x = cell // (grid_y * grid_z)
    at_y = cell // grid_z % grid_y
    at_z = cell % grid_z
    zero = jnp.zeros((), jnp.int32)
    geo_near = lax.dynamic_slice(geo_pad, (at_x, at_y, at_z, zero, zero), (3, 3, 3) + geo_pad.shape[3:]).reshape((27,) + geo_pad.shape[3:])
    feat_near = lax.dynamic_slice(feat_pad, (at_x, at_y, at_z, zero, zero, zero), (3, 3, 3) + feat_pad.shape[3:]).reshape((27 * slots,) + feat_pad.shape[4:])
    own_scalar = lax.dynamic_slice(scalar_state, (at_x, at_y, at_z, zero, zero), (1, 1, 1, slots, width)).reshape(slots, width)
    own_vector = lax.dynamic_slice(vector_state, (at_x, at_y, at_z, zero, zero, zero), (1, 1, 1, slots, 3, width)).reshape(slots, 3, width)
    near_pos = (geo_near[:, :3, :] + offsets_table()[:, :, None] * cutoff).transpose(0, 2, 1).reshape(27 * slots, 3)
    near_live = geo_near[:, 3, :].reshape(27 * slots)
    own_pos = geo_near[13, :3, :]
    own_live = geo_near[13, 3, :]
    gates = atom_gates(feat_near[:, 0, :], atom_in, atom_bias, atom_out)
    near_vectors = feat_near[:, 1:, :].astype(jnp.float32)
    pair_b = (gates[:, 1, None, :].astype(jnp.float32) * near_vectors).astype(jnp.bfloat16)
    pair_g = (gates[:, 3, None, :].astype(jnp.float32) * near_vectors).astype(jnp.bfloat16)
    plain_side = jnp.concatenate([gates[:, 0, :], pair_b.reshape(27 * slots, 3 * width)], axis=1)
    gate_c = gates[:, 2, :]
    row_count = slots // 8

    def one_block(block):
        start = block * row_count
        return receiver_block(start, row_count, near_pos, near_live, own_pos, plain_side, gate_c, pair_g, radial_in, radial_bias, radial_out)
    scalar_delta, vector_delta = lax.map(one_block, jnp.arange(8, dtype=jnp.int32))
    new_scalar = ((own_scalar.astype(jnp.float32) + scalar_delta.reshape(slots, width)) * own_live[:, None]).astype(jnp.bfloat16)
    new_vector = ((own_vector.astype(jnp.float32) + vector_delta.reshape(slots, 3, width)) * own_live[:, None, None]).astype(jnp.bfloat16)
    return (new_scalar, new_vector)

def reference(positions, counts, scalars, vectors, radial_in, radial_bias, radial_out, atom_in, atom_bias, atom_out, readout_in, readout_out):
    live = (lax.broadcasted_iota(jnp.int32, (NX, NY, NZ, SLOTS), 3) < counts[:, :, :, None]).astype(jnp.float32)
    geometry = jnp.concatenate([positions, live[:, :, :, None, :]], axis=3)
    geo_pad = wrap_cells(geometry)
    scalar_state, vector_state = (scalars, vectors)
    for layer in range(LAYERS):
        stacked = jnp.concatenate([scalar_state[:, :, :, :, None, :], vector_state], axis=4)
        feat_pad = wrap_cells(stacked)
        layer_params = (radial_in[layer], radial_bias[layer], radial_out[layer], atom_in[layer], atom_bias[layer], atom_out[layer])

        def one_cell(cell, feat_pad=feat_pad, scalar_state=scalar_state, vector_state=vector_state, layer_params=layer_params):
            return cell_update(cell, geo_pad, feat_pad, scalar_state, vector_state, layer_params)
        new_scalar, new_vector = lax.map(one_cell, jnp.arange(NX * NY * NZ, dtype=jnp.int32))
        scalar_state = new_scalar.reshape(NX, NY, NZ, SLOTS, CHAN)
        vector_state = new_vector.reshape(NX, NY, NZ, SLOTS, 3, CHAN)
    readout_hidden = jax.nn.silu(jnp.dot(scalar_state.reshape(-1, CHAN), readout_in, preferred_element_type=jnp.float32))
    atom_energy = lax.optimization_barrier(jnp.sum(readout_hidden * readout_out, axis=-1)) * live.reshape(-1)
    energy = jnp.sum(atom_energy).reshape(1)
    return (scalar_state, vector_state, energy)
```

```python
import functools
import math

import jax
import jax.numpy as jnp
from jax import lax
from jax.experimental import pallas as pl
from jax.experimental.pallas import tpu as pltpu
from jax.sharding import PartitionSpec as P

cutoff = 5.0
message_scale = 0.5
slots = 32
chan = 128
hidden = 64
planes = 4
columns = 9
near = planes * columns * slots
span = 896
starts = (0, 256)
block = 8
f32 = jnp.float32
bf16 = jnp.bfloat16


def pieces(value):
    high = lax.reduce_precision(value, 8, 7)
    rest = value - high
    middle = lax.reduce_precision(rest, 8, 7)
    low = lax.reduce_precision(rest - middle, 8, 7)
    return high.astype(bf16), middle.astype(bf16), low.astype(bf16)


def dot(a, b):
    return jnp.dot(a, b, preferred_element_type=f32)


def half_silu(y):
    return y + y * jnp.tanh(y)


def layer_kernel(
    last,
    counts_ref,
    offs_ref,
    *refs,
):
    cols = refs[:columns]
    geo_in = None
    refs = refs[columns:]
    if last:
        geo_in = refs[0]
        refs = refs[1:]
    (rin_ref, rout_ref, ain_ref, abias_ref, aout_ref), refs = refs[:5], refs[5:]
    if last:
        (read_in_ref, read_out_ref), refs = refs[:2], refs[2:]
        state_ref, energy_ref = refs[:2]
        refs = refs[2:]
    else:
        state_ref, geo_out = refs[:2]
        refs = refs[2:]
    f0, f1, f2, f3, gall, pos, own, basis_s, wts_s, e0, e1, e2, e3, delta = refs
    fk = (f1, f2, f3)
    ek = (e1, e2, e3)

    for c in range(columns):
        x = cols[c][...].reshape(planes * slots, -1)
        s = x[:, :chan]
        hid = half_silu(0.5 * (dot(s, ain_ref[...]) + abias_ref[...])).astype(bf16)
        gates = dot(hid, aout_ref[...]).astype(bf16)
        ga, gb = gates[:, :chan], gates[:, chan : 2 * chan]
        gc, gg = gates[:, 2 * chan : 3 * chan], gates[:, 3 * chan :]
        vec = [x[:, (k + 1) * chan : (k + 2) * chan] for k in range(3)]
        row0 = jnp.concatenate([ga] + [gb * v for v in vec], axis=1)
        rows = [jnp.concatenate([gc, gg * v], axis=1) for v in vec]
        for p in range(planes):
            at = pl.ds((p * columns + c) * slots, slots)
            part = slice(p * slots, (p + 1) * slots)
            f0[at, :] = row0[part]
            for k in range(3):
                fk[k][at, :] = rows[k][part]
            if not last:
                gall[at, :] = x[part, 4 * chan :]
    if last:
        pos[...] = geo_in[0:8, :]
        own[...] = geo_in[8:72, :chan]
    else:
        lane = lax.broadcasted_iota(jnp.int32, (8, chan), 1)
        row = lax.broadcasted_iota(jnp.int32, (8, chan), 0)
        pick = (lane == row) | (lane == row + 8) | (lane == row + 16)
        pick = jnp.where(pick, 1.0, 0.0).astype(bf16)
        contract = (((1,), (1,)), ((), ()))
        pos[...] = lax.dot_general(pick, gall[...], contract, preferred_element_type=f32)
        lane = lax.broadcasted_iota(jnp.int32, (chan, chan), 1)
        row = lax.broadcasted_iota(jnp.int32, (chan, chan), 0)
        pick = (lane == row) | (lane + 8 == row) | (lane + 16 == row)
        pick = jnp.where(pick, 1.0, 0.0).astype(bf16)
        mine = cols[4][1:3].reshape(2 * slots, -1)[:, 4 * chan :]
        own[...] = dot(mine, pick)
        geo_out[0:8, :] = pos[...]
        geo_out[8:72, :chan] = own[...]
        geo_out[8:72, chan:] = jnp.zeros((2 * slots, near - chan), f32)
    delta[...] = jnp.zeros_like(delta)

    for q in range(2):
        window = slice(starts[q], starts[q] + span)
        dist2 = None
        disp = []
        for k in range(3):
            other = pos[k : k + 1, window] + offs_ref[q * 3 + k : q * 3 + k + 1, window]
            d = other - own[q * slots : (q + 1) * slots, k : k + 1]
            disp.append(d)
            dist2 = d * d if k == 0 else dist2 + d * d
        lane = lax.broadcasted_iota(jnp.int32, (slots, span), 1) + starts[q]
        row = lax.broadcasted_iota(jnp.int32, (slots, span), 0)
        self_at = ((1 + q) * columns + 4) * slots
        itself = jnp.where(lane == row + self_at, 1.0, 0.0)
        dist = jnp.sqrt(dist2 + itself)
        smooth = jnp.where(
            dist < cutoff, 0.5 * (jnp.cos(math.pi * dist / cutoff) + 1.0), 0.0
        )
        weight = smooth * pos[3:4, window] * (1.0 - itself)
        scaled = weight / dist
        wts_s[:, 0, :] = weight
        for k in range(3):
            wts_s[:, 1 + k, :] = scaled * disp[k]
        sharp = 0.5 * (7.0 / cutoff) ** 2
        for k in range(8):
            away = dist - k * (cutoff / 7.0)
            basis_s[:, k, :] = jnp.exp(-sharp * (away * away))

        def one_block(b, carry, q=q, window=window):
            for r in range(block):
                i = b * block + r
                wide = jnp.concatenate(
                    [basis_s[i], jnp.ones((8, span), f32)], axis=0
                ).astype(bf16)
                s = half_silu(dot(rin_ref[...], wide))
                part = slice(r * hidden, (r + 1) * hidden)
                w = wts_s[i]
                e0[part, :] = (s * w[0:1, :]).astype(bf16)
                for k in range(3):
                    ek[k][part, :] = (s * w[1 + k : 2 + k, :]).astype(bf16)
            plain = dot(e0[...], f0[window, :])
            turned = [dot(ek[k][...], fk[k][window, :]) for k in range(3)]
            radial = [rout_ref[:, g * chan : (g + 1) * chan][None] for g in range(4)]
            split = (block, hidden, chan)
            proj = turned[0][:, chan:] + turned[1][:, chan:] + turned[2][:, chan:]
            totals = [
                plain[:, :chan].reshape(split) * radial[0] + proj.reshape(split) * radial[3]
            ]
            for k in range(3):
                totals.append(
                    plain[:, (k + 1) * chan : (k + 2) * chan].reshape(split) * radial[1]
                    + turned[k][:, :chan].reshape(split) * radial[2]
                )
            at = pl.ds(pl.multiple_of(q * slots + b * block, block), block)
            for g in range(4):
                delta[at, g * chan : (g + 1) * chan] = jnp.sum(totals[g], axis=1)
            return carry

        blocks = (counts_ref[q] + block - 1) // block
        lax.fori_loop(0, blocks, one_block, 0)

    slot = lax.broadcasted_iota(jnp.int32, (2 * slots, 1), 0)
    limit = jnp.where(slot < slots, counts_ref[0], counts_ref[1] + slots)
    live = jnp.where(slot < limit, 1.0, 0.0)
    mine = cols[4][1:3].reshape(2 * slots, -1)[:, : 4 * chan].astype(f32)
    state = ((mine + message_scale * delta[...]) * live).astype(bf16)
    state_ref[...] = state
    if last:
        x = dot(state[:, :chan], read_in_ref[...])
        each = half_silu(0.5 * x) * read_out_ref[...] * live
        energy_ref[...] = jnp.broadcast_to(jnp.sum(each, keepdims=True), energy_ref.shape)


def layer_call(last, counts, offs, cols, geo, weights):
    vmem = pl.BlockSpec(memory_space=pltpu.VMEM)
    smem = pl.BlockSpec(memory_space=pltpu.SMEM)
    operands = [counts, offs] + list(cols) + ([geo] if last else []) + list(weights)
    state = jax.ShapeDtypeStruct((2 * slots, 4 * chan), bf16)
    if last:
        out = (state, jax.ShapeDtypeStruct((chan, chan), f32))
    else:
        out = (state, jax.ShapeDtypeStruct((72, near), f32))
    return pl.pallas_call(
        functools.partial(layer_kernel, last),
        out_shape=out,
        in_specs=[smem] + [vmem] * (len(operands) - 1),
        out_specs=(vmem, vmem),
        scratch_shapes=[
            pltpu.VMEM((near, 4 * chan), bf16),
            pltpu.VMEM((near, 2 * chan), bf16),
            pltpu.VMEM((near, 2 * chan), bf16),
            pltpu.VMEM((near, 2 * chan), bf16),
            pltpu.VMEM((near, chan), bf16),
            pltpu.VMEM((8, near), f32),
            pltpu.VMEM((2 * slots, chan), f32),
            pltpu.VMEM((slots, 8, span), f32),
            pltpu.VMEM((slots, 8, span), f32),
            pltpu.VMEM((block * hidden, span), bf16),
            pltpu.VMEM((block * hidden, span), bf16),
            pltpu.VMEM((block * hidden, span), bf16),
            pltpu.VMEM((block * hidden, span), bf16),
            pltpu.VMEM((2 * slots, 4 * chan), f32),
        ],
        compiler_params=pltpu.CompilerParams(vmem_limit_bytes=48 * 1024 * 1024),
        name="layer_last" if last else "layer_first",
    )(*operands)


def exchange(own):
    count = lax.axis_size("gx")
    up = [(i, (i + 1) % count) for i in range(count)]
    down = [(i, (i - 1) % count) for i in range(count)]
    low = lax.ppermute(own[1:2], "gx", up)
    high = lax.ppermute(own[0:1], "gx", down)
    column = jnp.concatenate([low, own, high], axis=0)
    deep, tall = lax.axis_size("gy"), lax.axis_size("gz")
    cols = []
    for dy in (-1, 0, 1):
        for dz in (-1, 0, 1):
            if dy == 0 and dz == 0:
                cols.append(column)
                continue
            pairs = [
                (((y + dy) % deep) * tall + (z + dz) % tall, y * tall + z)
                for y in range(deep)
                for z in range(tall)
            ]
            cols.append(lax.ppermute(column, ("gy", "gz"), pairs))
    return cols


def offsets():
    rows = []
    lane = lax.broadcasted_iota(jnp.int32, (near,), 0) // slots
    plane, col = lane // columns, lane % columns
    for q in range(2):
        rows += [plane - 1 - q, col // 3 - 1, col % 3 - 1]
    rows += [plane * 0, plane * 0]
    return jnp.stack(rows).astype(f32) * cutoff


def on_device(
    positions,
    counts,
    scalars,
    vectors,
    radial_in,
    radial_bias,
    radial_out,
    atom_in,
    atom_bias,
    atom_out,
    readout_in,
    readout_out,
):
    counts = counts.reshape(2)
    live = (lax.broadcasted_iota(jnp.int32, (2, slots), 1) < counts[:, None]).astype(f32)
    geo = jnp.concatenate([positions.reshape(2, 3, slots), live[:, None, :]], axis=1)
    geo = jnp.pad(geo.transpose(0, 2, 1), ((0, 0), (0, 0), (0, 4)))
    geo = jnp.concatenate(pieces(geo), axis=2)
    geo = jnp.pad(geo, ((0, 0), (0, 0), (0, chan - 24)))
    own = jnp.concatenate(
        [
            scalars.reshape(2, slots, chan),
            vectors.reshape(2, slots, 3 * chan),
            geo,
        ],
        axis=2,
    )
    offs = offsets()
    geometry = None
    layers = radial_in.shape[0]
    for layer in range(layers):
        rin = jnp.concatenate(
            [radial_in[layer]]
            + [p[None, :] for p in pieces(radial_bias[layer])]
            + [jnp.zeros((5, hidden), bf16)],
            axis=0,
        )
        rin = (rin * jnp.asarray(0.5, bf16)).T
        weights = [
            rin,
            radial_out[layer].astype(f32),
            atom_in[layer],
            atom_bias[layer][None, :],
            atom_out[layer],
        ]
        last = layer == layers - 1
        if last:
            weights += [readout_in, readout_out[None, :]]
        cols = exchange(own)
        state, extra = layer_call(last, counts, offs, cols, geometry, weights)
        if not last:
            geometry = extra
            own = state.reshape(2, slots, 4 * chan)
    scalar_state = state[:, :chan].reshape(scalars.shape)
    vector_state = state[:, chan:].reshape(vectors.shape)
    every = lax.all_to_all(extra, ("gx", "gy", "gz"), 0, 0, tiled=True)
    energy = jnp.sum(every, axis=0)[:1]
    return scalar_state, vector_state, energy


def solution(mesh):
    in_specs = (
        P("gx", "gy", "gz", None, None),
        P("gx", "gy", "gz"),
        P("gx", "gy", "gz", None, None),
        P("gx", "gy", "gz", None, None, None),
        P(),
        P(),
        P(),
        P(),
        P(),
        P(),
        P(),
        P(),
    )
    out_specs = (P("gx", "gy", "gz", None, None), P("gx", "gy", "gz", None, None, None), P())
    return jax.shard_map(
        on_device, mesh=mesh, in_specs=in_specs, out_specs=out_specs, check_vma=False
    )
```

```python
import functools
import math

import jax
import jax.numpy as jnp
from jax import lax
from jax.experimental import pallas as pl
from jax.experimental.pallas import tpu as pltpu
from jax.sharding import PartitionSpec as P

cutoff = 5.0
message_scale = 0.5
slots = 32
chan = 128
hidden = 64
block = 4
blocks = slots // block
own_atoms, own_main, own_span = 576, 512, 640
side_atoms, side_main, side_span = 288, 256, 384
f32 = jnp.float32
bf16 = jnp.bfloat16
across = (((1,), (1,)), ((), ()))


def pieces(value):
    high = lax.reduce_precision(value, 8, 7)
    rest = value - high
    middle = lax.reduce_precision(rest, 8, 7)
    low = lax.reduce_precision(rest - middle, 8, 7)
    return high.astype(bf16), middle.astype(bf16), low.astype(bf16)


def dot(a, b):
    return jnp.dot(a, b, preferred_element_type=f32)


def half_silu(y):
    return y + y * jnp.tanh(y)


def iotas(shape):
    return lax.broadcasted_iota(jnp.int32, shape, 0), lax.broadcasted_iota(jnp.int32, shape, 1)


def flag(condition):
    return jnp.where(condition, 1.0, 0.0)


def rows_of(geo):
    row, lane = iotas((8, chan))
    pick = flag((lane == row) | (lane == row + 8) | (lane == row + 16)).astype(bf16)
    return lax.dot_general(pick, geo, across, preferred_element_type=f32)


def columns_of(geo):
    row, lane = iotas((chan, chan))
    pick = flag((lane == row) | (lane + 8 == row) | (lane + 16 == row)).astype(bf16)
    return dot(geo, pick)


def compaction(live, span):
    atoms = live.shape[1]
    row, lane = iotas((atoms, atoms))
    before = flag(row < lane).astype(bf16)
    rank = dot(jnp.broadcast_to(live, (8, atoms)).astype(bf16), before)[0:1]
    rank = jnp.where(live > 0.5, rank, -1.0)
    row = lax.broadcasted_iota(jnp.int32, (span, atoms), 0).astype(f32)
    return flag(row == rank).astype(bf16)


def geometry(q, row, mine, shift, basis_ref, wts_ref, at):
    dist2 = None
    disp = []
    for k in range(3):
        other = row[k : k + 1] + (row[4 + k : 5 + k] + (shift if k == 0 else 0.0))
        d = other - mine[:, k : k + 1]
        disp.append(d)
        dist2 = d * d if k == 0 else dist2 + d * d
    live = row[3:4]
    number = lax.broadcasted_iota(jnp.int32, dist2.shape, 0) + (q * slots + 1)
    itself = flag(row[7:8] == number.astype(f32))
    dist = jnp.sqrt(dist2 + itself + (1.0 - live))
    smooth = jnp.where(dist < cutoff, 0.5 * (jnp.cos(math.pi * dist / cutoff) + 1.0), 0.0)
    weight = smooth * live * (1.0 - itself)
    scaled = weight / dist
    wts_ref[at, 0, :] = weight
    for k in range(3):
        wts_ref[at, 1 + k, :] = scaled * disp[k]
    sharp = 0.5 * (7.0 / cutoff) ** 2
    for k in range(8):
        away = dist - k * (cutoff / 7.0)
        basis_ref[at, k, :] = jnp.exp(-sharp * (away * away))


def features(layer, x, part, weights, feats):
    _, _, ain_ref, abias_ref, aout_ref = weights
    s = x[:, :chan]
    bias = abias_ref[layer : layer + 1, :]
    hid = half_silu(0.5 * (dot(s, ain_ref[layer]) + bias)).astype(bf16)
    gates = dot(hid, aout_ref[layer]).astype(bf16)
    ga, gb = gates[:, :chan], gates[:, chan : 2 * chan]
    gc, gg = gates[:, 2 * chan : 3 * chan], gates[:, 3 * chan :]
    vec = [x[:, (k + 1) * chan : (k + 2) * chan] for k in range(3)]
    feats[0][part, :] = jnp.concatenate([ga] + [gb * v for v in vec], axis=1)
    for k in range(3):
        feats[1 + k][part, :] = jnp.concatenate([gc, gg * vec[k]], axis=1)


def messages(layer, q, count, window, weights, basis_ref, wts_ref, feats, edges, delta):
    rin_ref, rout_ref = weights[:2]
    width = window.stop - window.start

    def one_block(b, carry):
        for r in range(block):
            i = q * slots + b * block + r
            wide = jnp.concatenate(
                [basis_ref[i][:, window], jnp.ones((8, width), f32)], axis=0
            ).astype(bf16)
            s = half_silu(dot(rin_ref[layer], wide)).astype(bf16).reshape(4, 16, width)
            part = slice(r * hidden, (r + 1) * hidden)
            w = wts_ref[i][:, window]
            for g in range(4):
                line = jnp.broadcast_to(w[g : g + 1, :], (16, width)).astype(bf16)
                edges[g][part, :width] = (s * line[None]).reshape(hidden, width)
        plain = dot(edges[0][:, :width], feats[0][window, :])
        turned = [dot(edges[k + 1][:, :width], feats[k + 1][window, :]) for k in range(3)]
        radial = [rout_ref[layer, :, g * chan : (g + 1) * chan].astype(f32)[None] for g in range(4)]
        split = (block, hidden, chan)
        proj = turned[0][:, chan:] + turned[1][:, chan:] + turned[2][:, chan:]
        totals = [plain[:, :chan].reshape(split) * radial[0] + proj.reshape(split) * radial[3]]
        for k in range(3):
            totals.append(
                plain[:, (k + 1) * chan : (k + 2) * chan].reshape(split) * radial[1]
                + turned[k][:, :chan].reshape(split) * radial[2]
            )
        at = q * blocks + b
        for g in range(4):
            lanes = slice(g * chan, (g + 1) * chan)
            delta[at, 0:block, lanes] += jnp.sum(totals[g], axis=1)
        return carry

    lax.fori_loop(0, (count + block - 1) // block, one_block, 0)


def own_kernel(layer, *refs):
    counts_ref, low, middle, high = refs[:4]
    weights = refs[4:9]
    refs = refs[9:]
    if layer == 0:
        table_ref, delta, basis, wts, order, more = refs[:6]
        refs = refs[6:]
    else:
        basis, wts, order, more, delta = refs[:5]
        refs = refs[5:]
    feats, edges = refs[:4], refs[4:8]
    parts = [ref[...].reshape(own_atoms // 3, -1) for ref in (low, middle, high)]
    third = own_atoms // 3
    if layer == 0:
        geo = jnp.concatenate([p[:, 4 * chan :] for p in parts], axis=0) + table_ref[...]
        live = rows_of(geo)[3:4]
        order[...] = compaction(live, own_span)
        row = rows_of(dot(order[...], geo).astype(bf16))
        total = jnp.sum(live)
        more[0] = jnp.where(total > own_main + 0.5, 1, 0)
        for q in range(2):
            mine = columns_of(middle[q, 1][:, 4 * chan :])
            at = slice(q * slots, (q + 1) * slots)
            geometry(q, row, mine, -q * cutoff, basis, wts, at)

    def gathered(part):
        x = None
        for n in range(3):
            y = dot(order[part, n * third : (n + 1) * third], parts[n][:, : 4 * chan])
            x = y if n == 0 else x + y
        features(layer, x.astype(bf16), part, weights, feats)

    delta[...] = jnp.zeros_like(delta)
    main, rest = slice(0, own_main), slice(own_main, own_span)
    gathered(main)
    for q in range(2):
        messages(layer, q, counts_ref[q], main, weights, basis, wts, feats, edges, delta)

    @pl.when(more[0] > 0)
    def _():
        gathered(rest)
        for q in range(2):
            messages(layer, q, counts_ref[q], rest, weights, basis, wts, feats, edges, delta)


def side_kernel(layer, last, *refs):
    counts_ref, low, high, own_ref, before = refs[:5]
    weights = refs[5:10]
    refs = refs[10:]
    if last:
        read_in_ref, read_out_ref = refs[:2]
        refs = refs[2:]
    if layer == 0:
        table_ref, refs = refs[0], refs[1:]
    else:
        (basis, wts, order, more), refs = refs[:4], refs[4:]
    state_ref, refs = refs[0], refs[1:]
    if last:
        energy_ref, refs = refs[0], refs[1:]
    if layer == 0:
        (basis, wts, order, more), refs = refs[:4], refs[4:]
    feats, edges, delta = refs[:4], refs[4:8], refs[8]
    delta[...] = before[...]
    main, rest = slice(0, side_main), slice(side_main, side_span)
    for q in range(2):
        x_all = (low, high)[q][...].reshape(side_atoms, -1)
        if layer == 0:
            geo = x_all[:, 4 * chan :] + table_ref[...]
            live = rows_of(geo)[3:4]
            order[q] = compaction(live, side_span)
            row = rows_of(dot(order[q], geo).astype(bf16))
            total = jnp.sum(live)
            more[q] = jnp.where(total > side_main + 0.5, 1, 0)
            mine = columns_of(own_ref[q][:, 4 * chan :])
            at = slice(q * slots, (q + 1) * slots)
            geometry(q, row, mine, (-cutoff, cutoff)[q], basis, wts, at)

        def gathered(part, q=q, x_all=x_all):
            x = dot(order[q, part, :], x_all[:, : 4 * chan])
            features(layer, x.astype(bf16), part, weights, feats)

        gathered(main)
        messages(layer, q, counts_ref[q], main, weights, basis, wts, feats, edges, delta)

        @pl.when(more[q] > 0)
        def _(q=q, gathered=gathered):
            gathered(rest)
            messages(layer, q, counts_ref[q], rest, weights, basis, wts, feats, edges, delta)

    slot = lax.broadcasted_iota(jnp.int32, (2 * slots, 1), 0)
    limit = jnp.where(slot < slots, counts_ref[0], counts_ref[1] + slots)
    live = flag(slot < limit)
    mine = own_ref[...].reshape(2 * slots, -1)[:, : 4 * chan].astype(f32)
    change = jnp.concatenate([delta[b, 0:block, :] for b in range(2 * blocks)], axis=0)
    state = ((mine + message_scale * change) * live).astype(bf16)
    state_ref[...] = state
    if last:
        x = dot(state[:, :chan], read_in_ref[...])
        each = half_silu(0.5 * x) * read_out_ref[...] * live
        energy_ref[...] = jnp.broadcast_to(jnp.sum(each, keepdims=True), energy_ref.shape)


vmem = pl.BlockSpec(memory_space=pltpu.VMEM)
smem = pl.BlockSpec(memory_space=pltpu.SMEM)


def scratch(span, main):
    return [
        pltpu.VMEM((span, 4 * chan), bf16),
        *[pltpu.VMEM((span, 2 * chan), bf16)] * 3,
        *[pltpu.VMEM((block * hidden, main), bf16)] * 4,
    ]


def cost(atoms):
    return pl.CostEstimate(
        flops=2 * 2 * slots * atoms * 81920, bytes_accessed=4000000, transcendentals=4000000
    )


params = pltpu.CompilerParams(vmem_limit_bytes=40 * 1024 * 1024)
delta_shape = jax.ShapeDtypeStruct((2 * blocks, 8, 4 * chan), f32)


def kept_shapes(span, order):
    pairs = jax.ShapeDtypeStruct((2 * slots, 8, span), f32)
    return (
        pairs,
        pairs,
        jax.ShapeDtypeStruct(order, bf16),
        jax.ShapeDtypeStruct((2,), jnp.int32),
    )


kept_specs = (vmem, vmem, vmem, smem)


def own_call(layer, counts, ys, weights, table, kept):
    operands = [counts, *ys, *weights]
    specs = [smem] + [vmem] * (len(operands) - 1)
    shapes, outs = (delta_shape,), (vmem,)
    if layer == 0:
        operands.append(table)
        specs.append(vmem)
        shapes += kept_shapes(own_span, (own_span, own_atoms))
        outs += kept_specs
    else:
        operands += kept
        specs += kept_specs
    return pl.pallas_call(
        functools.partial(own_kernel, layer),
        out_shape=shapes,
        in_specs=specs,
        out_specs=outs,
        scratch_shapes=scratch(own_span, own_main),
        compiler_params=params,
        cost_estimate=cost(own_atoms),
        name=f"own_part_{layer}",
    )(*operands)


def side_call(layer, last, counts, low, high, own, delta, weights, readout, table, kept):
    operands = [counts, low, high, own, delta, *weights]
    specs = [smem] + [vmem] * (len(operands) - 1)
    shapes, outs = (jax.ShapeDtypeStruct((2 * slots, 4 * chan), bf16),), (vmem,)
    if last:
        operands += readout
        specs += [vmem] * 2
        shapes += (jax.ShapeDtypeStruct((chan, chan), f32),)
        outs += (vmem,)
    if layer == 0:
        operands.append(table)
        specs.append(vmem)
        shapes += kept_shapes(side_span, (2, side_span, side_atoms))
        outs += kept_specs
    else:
        operands += kept
        specs += kept_specs
    return pl.pallas_call(
        functools.partial(side_kernel, layer, last),
        out_shape=shapes,
        in_specs=specs,
        out_specs=outs,
        scratch_shapes=scratch(side_span, side_main) + [pltpu.VMEM(delta_shape.shape, f32)],
        compiler_params=params,
        cost_estimate=cost(side_atoms),
        name=f"side_part_{layer}",
    )(*operands)


def shifted(value, axis, step):
    count = lax.axis_size(axis)
    return lax.ppermute(value, axis, [((i + step) % count, i) for i in range(count)])


def tables():
    j = lax.broadcasted_iota(jnp.int32, (own_atoms, chan), 0)
    lane = lax.broadcasted_iota(jnp.int32, (own_atoms, chan), 1)
    slot, z, plane, y = j % slots, j // slots % 3, j // (3 * slots) % 2, j // (6 * slots)
    name = jnp.where((y == 1) & (z == 1), plane * slots + slot + 1, 0)
    values = jnp.where(lane == 4, plane * 5, 0) + jnp.where(lane == 7, name, 0)
    values += jnp.where(lane == 5, (y - 1) * 5, 0) + jnp.where(lane == 6, (z - 1) * 5, 0)
    own = values.astype(bf16)
    j, lane = j[:side_atoms], lane[:side_atoms]
    z, y = j // slots % 3, j // (3 * slots)
    values = jnp.where(lane == 5, (y - 1) * 5, 0) + jnp.where(lane == 6, (z - 1) * 5, 0)
    return own, values.astype(bf16)


def on_device(
    positions,
    counts,
    scalars,
    vectors,
    radial_in,
    radial_bias,
    radial_out,
    atom_in,
    atom_bias,
    atom_out,
    readout_in,
    readout_out,
):
    counts = counts.reshape(2)
    live = (lax.broadcasted_iota(jnp.int32, (2, slots), 1) < counts[:, None]).astype(f32)
    geo = jnp.concatenate([positions.reshape(2, 3, slots), live[:, None, :]], axis=1)
    geo = jnp.pad(geo.transpose(0, 2, 1), ((0, 0), (0, 0), (0, 4)))
    geo = jnp.concatenate(pieces(geo), axis=2)
    geo = jnp.pad(geo, ((0, 0), (0, 0), (0, chan - 24)))
    own = jnp.concatenate(
        [
            scalars.reshape(2, slots, chan),
            vectors.reshape(2, slots, 3 * chan),
            geo,
        ],
        axis=2,
    )
    layers = radial_in.shape[0]
    rin = jnp.concatenate(
        [radial_in]
        + [p[:, None, :] for p in pieces(radial_bias)]
        + [jnp.zeros((layers, 5, hidden), bf16)],
        axis=1,
    )
    rin = (rin * jnp.asarray(0.5, bf16)).transpose(0, 2, 1)
    weights = [rin, radial_out, atom_in, atom_bias, atom_out]
    own_table, side_table = tables()
    own_kept = side_kept = ()
    for layer in range(layers):
        last = layer == layers - 1
        y = jnp.stack([shifted(own, "gz", -1), own, shifted(own, "gz", 1)], axis=1)
        ys = [shifted(y, "gy", -1), y, shifted(y, "gy", 1)]
        low = shifted(jnp.stack([v[1] for v in ys]), "gx", -1)
        high = shifted(jnp.stack([v[0] for v in ys]), "gx", 1)
        delta, *kept = own_call(layer, counts, ys, weights, own_table, own_kept)
        own_kept = own_kept or kept
        readout = [readout_in, readout_out[None, :]]
        state, *kept = side_call(
            layer, last, counts, low, high, own, delta, weights, readout, side_table, side_kept
        )
        if last:
            energy = kept[0]
        else:
            side_kept = side_kept or kept
            own = state.reshape(2, slots, 4 * chan)
    scalar_state = state[:, :chan].reshape(scalars.shape)
    vector_state = state[:, chan:].reshape(vectors.shape)
    every = lax.all_to_all(energy, ("gx", "gy", "gz"), 0, 0, tiled=True)
    energy = jnp.sum(every, axis=0)[:1]
    return scalar_state, vector_state, energy


def solution(mesh):
    in_specs = (
        P("gx", "gy", "gz", None, None),
        P("gx", "gy", "gz"),
        P("gx", "gy", "gz", None, None),
        P("gx", "gy", "gz", None, None, None),
        P(),
        P(),
        P(),
        P(),
        P(),
        P(),
        P(),
        P(),
    )
    out_specs = (P("gx", "gy", "gz", None, None), P("gx", "gy", "gz", None, None, None), P())
    return jax.shard_map(
        on_device, mesh=mesh, in_specs=in_specs, out_specs=out_specs, check_vma=False
    )
```

```python
import functools
import math

import jax
import jax.numpy as jnp
import numpy as np
from jax import lax
from jax.experimental import pallas as pl
from jax.experimental.pallas import tpu as pltpu
from jax.sharding import PartitionSpec as P

cutoff = 5.0
message_scale = 0.5
slots = 32
chan = 128
hidden = 64
block = 8
room = 2 * slots + block
depth = 80
own_atoms, own_main, own_span = 576, 512, 640
side_atoms, side_main, side_span = 288, 256, 384
f32 = jnp.float32
bf16 = jnp.bfloat16
across = (((1,), (1,)), ((), ()))


def pieces(value):
    high = lax.reduce_precision(value, 8, 7)
    rest = value - high
    middle = lax.reduce_precision(rest, 8, 7)
    low = lax.reduce_precision(rest - middle, 8, 7)
    return high.astype(bf16), middle.astype(bf16), low.astype(bf16)


def dot(a, b):
    return jnp.dot(a, b, preferred_element_type=f32)


def half_silu(y):
    return y + y * jnp.tanh(y)


def iotas(shape):
    return lax.broadcasted_iota(jnp.int32, shape, 0), lax.broadcasted_iota(jnp.int32, shape, 1)


def flag(condition):
    return jnp.where(condition, 1.0, 0.0)


def rows_of(geo):
    row, lane = iotas((8, chan))
    pick = flag((lane == row) | (lane == row + 8) | (lane == row + 16)).astype(bf16)
    return lax.dot_general(pick, geo, across, preferred_element_type=f32)


def columns_of(geo):
    row, lane = iotas((chan, chan))
    pick = flag((lane == row) | (lane + 8 == row) | (lane + 16 == row)).astype(bf16)
    return dot(geo, pick)


def compaction(live, span):
    atoms = live.shape[1]
    row, lane = iotas((atoms, atoms))
    before = flag(row < lane).astype(bf16)
    rank = dot(jnp.broadcast_to(live, (8, atoms)).astype(bf16), before)[0:1]
    rank = jnp.where(live > 0.5, rank, -1.0)
    row = lax.broadcasted_iota(jnp.int32, (span, atoms), 0).astype(f32)
    return flag(row == rank).astype(bf16)


def geometry(row, mine, number, shift, basis_ref, wts_ref, at):
    dist2 = None
    disp = []
    for k in range(3):
        offset = row[4 + k : 5 + k] + shift if k == 0 else row[4 + k : 5 + k]
        d = (row[k : k + 1] + offset) - mine[:, k : k + 1]
        disp.append(d)
        dist2 = d * d if k == 0 else dist2 + d * d
    live = row[3:4]
    itself = flag(row[7:8] == number.astype(f32))
    dist = jnp.sqrt(dist2 + itself + (1.0 - live))
    smooth = jnp.where(dist < cutoff, 0.5 * (jnp.cos(math.pi * dist / cutoff) + 1.0), 0.0)
    weight = smooth * live * (1.0 - itself)
    scaled = weight / dist
    wts_ref[0, at, :] = weight
    for k in range(3):
        wts_ref[1 + k, at, :] = scaled * disp[k]
    sharp = 0.5 * (7.0 / cutoff) ** 2
    for k in range(8):
        away = dist - k * (cutoff / 7.0)
        basis_ref[k, at, :] = jnp.exp(-sharp * (away * away))


def features(layer, x, part, weights, feats):
    _, _, ain_ref, abias_ref, aout_ref = weights
    s = x[:, :chan]
    bias = abias_ref[layer : layer + 1, :]
    hid = half_silu(0.5 * (dot(s, ain_ref[layer]) + bias)).astype(bf16)
    gates = dot(hid, aout_ref[layer]).astype(bf16)
    ga, gb = gates[:, :chan], gates[:, chan : 2 * chan]
    gc, gg = gates[:, 2 * chan : 3 * chan], gates[:, 3 * chan :]
    vec = [x[:, (k + 1) * chan : (k + 2) * chan] for k in range(3)]
    feats[0][part, :] = jnp.concatenate([ga] + [gb * v for v in vec], axis=1)
    for k in range(3):
        feats[1 + k][part, :] = jnp.concatenate([gc, gg * vec[k]], axis=1)


def messages(layer, base, count, window, weights, basis_ref, wts_ref, feats, edges, delta):
    rin_ref, rout_ref = weights[:2]
    width = window.stop - window.start
    even, odd = edges[:4], edges[4:]

    def rows_at(b):
        return pl.ds(pl.multiple_of(base + b * block, block), block)

    def hidden_of(b):
        slab = basis_ref[:, rows_at(b), window].reshape(8 * block, width)
        slab = jnp.concatenate([slab, jnp.ones((depth - 8 * block, width), f32)], axis=0)
        return dot(rin_ref[layer], slab.astype(bf16)), wts_ref[:, rows_at(b), window]

    def edge(r, y, w, out):
        part = slice(r * hidden, (r + 1) * hidden)
        s = half_silu(y[part]).astype(bf16).reshape(4, 16, width)
        for g in range(4):
            line = jnp.broadcast_to(w[g][r : r + 1, :], (16, width)).astype(bf16)
            out[g][part, :width] = (s * line[None]).reshape(hidden, width)

    def product(n, used):
        if n < 2:
            return dot(used[0][:, :width], feats[0][window, 2 * n * chan : 2 * (n + 1) * chan])
        return dot(used[n - 1][:, :width], feats[n - 1][window, :])

    def gather(n, result, radial, sums):
        groups = ((0, 1), (1, 1), (2, 3), (2, 3), (2, 3))[n]
        targets = ((0, 1), (2, 3), (1, 0), (2, 0), (3, 0))[n]
        for half in range(2):
            value = result[:, half * chan : (half + 1) * chan].reshape(block, hidden, chan)
            value = jnp.sum(value * radial[groups[half]], axis=1)
            t = targets[half]
            sums[t] = value if sums[t] is None else sums[t] + value

    def step(b, used, following):
        radial = [rout_ref[layer, :, g * chan : (g + 1) * chan].astype(f32)[None] for g in range(4)]
        sums = [None] * 4
        if following is not None:
            y, w = hidden_of(b + 1)
        made, previous = 0, None
        for n in range(5):
            result = product(n, used)
            while following is not None and made < block and made * 5 < (n + 1) * block:
                edge(made, y, w, following)
                made += 1
            if n > 0:
                gather(n - 1, previous, radial, sums)
            previous = result
        gather(4, previous, radial, sums)
        for g in range(4):
            delta[rows_at(b), g * chan : (g + 1) * chan] += sums[g]

    count = (count + block - 1) // block
    y, w = hidden_of(0)
    for r in range(block):
        edge(r, y, w, even)

    def two_steps(t, carry):
        step(2 * t, even, odd)
        step(2 * t + 1, odd, even)
        return carry

    lax.fori_loop(0, count // 2, two_steps, 0)

    @pl.when(count % 2 == 1)
    def _():
        step(count - 1, even, None)


def own_kernel(layer, *refs):
    counts_ref, low, middle, high = refs[:4]
    weights = refs[4:9]
    refs = refs[9:]
    if layer == 0:
        table_ref, delta, basis, wts, order, more = refs[:6]
        refs = refs[6:]
    else:
        basis, wts, order, more, delta = refs[:5]
        refs = refs[5:]
    feats, edges = refs[:4], refs[4:12]
    parts = [ref[...].reshape(own_atoms // 3, -1) for ref in (low, middle, high)]
    third = own_atoms // 3
    if layer == 0:
        geo = jnp.concatenate([p[:, 4 * chan :] for p in parts], axis=0) + table_ref[...]
        live = rows_of(geo)[3:4]
        order[...] = compaction(live, own_span)
        row = rows_of(dot(order[...], geo).astype(bf16))
        total = jnp.sum(live)
        more[0] = jnp.where(total > own_main + 0.5, 1, 0)
        first = counts_ref[0]
        mine = columns_of(
            jnp.concatenate([middle[q, 1][:, 4 * chan :] for q in range(2)], axis=0)
        )
        place = lax.broadcasted_iota(jnp.int32, (2 * slots, 1), 0)
        moved = pltpu.roll(mine, lax.rem(first + slots, 2 * slots), 0)
        mine = jnp.where(place < first, mine, moved)
        number = jnp.where(place < first, place + 1, place - first + (slots + 1))
        shift = jnp.where(place < first, 0.0, -cutoff)
        geometry(row, mine, number, shift, basis, wts, slice(0, 2 * slots))

    def gathered(part):
        x = None
        for n in range(3):
            y = dot(order[part, n * third : (n + 1) * third], parts[n][:, : 4 * chan])
            x = y if n == 0 else x + y
        features(layer, x.astype(bf16), part, weights, feats)

    delta[...] = jnp.zeros_like(delta)
    main, rest = slice(0, own_main), slice(own_main, own_span)
    count = counts_ref[0] + counts_ref[1]
    gathered(main)
    messages(layer, 0, count, main, weights, basis, wts, feats, edges, delta)

    @pl.when(more[0] > 0)
    def _():
        gathered(rest)
        messages(layer, 0, count, rest, weights, basis, wts, feats, edges, delta)


def side_kernel(layer, last, *refs):
    counts_ref, low, high, own_ref, before = refs[:5]
    weights = refs[5:10]
    refs = refs[10:]
    if last:
        read_in_ref, read_out_ref = refs[:2]
        refs = refs[2:]
    if layer == 0:
        table_ref, refs = refs[0], refs[1:]
    else:
        (basis, wts, order, more), refs = refs[:4], refs[4:]
    state_ref, refs = refs[0], refs[1:]
    if last:
        energy_ref, refs = refs[0], refs[1:]
    if layer == 0:
        (basis, wts, order, more), refs = refs[:4], refs[4:]
    feats, edges, delta = refs[:4], refs[4:12], refs[12]
    delta[...] = jnp.zeros_like(delta)
    main, rest = slice(0, side_main), slice(side_main, side_span)
    for q in range(2):
        x_all = (low, high)[q][...].reshape(side_atoms, -1)
        if layer == 0:
            geo = x_all[:, 4 * chan :] + table_ref[...]
            live = rows_of(geo)[3:4]
            order[q] = compaction(live, side_span)
            row = rows_of(dot(order[q], geo).astype(bf16))
            total = jnp.sum(live)
            more[q] = jnp.where(total > side_main + 0.5, 1, 0)
            mine = columns_of(own_ref[q][:, 4 * chan :])
            at = slice(q * slots, (q + 1) * slots)
            number = lax.broadcasted_iota(jnp.int32, (slots, 1), 0) + (q * slots + 1)
            geometry(row, mine, number, (-cutoff, cutoff)[q], basis, wts, at)

        def gathered(part, q=q, x_all=x_all):
            x = dot(order[q, part, :], x_all[:, : 4 * chan])
            features(layer, x.astype(bf16), part, weights, feats)

        gathered(main)
        messages(layer, q * slots, counts_ref[q], main, weights, basis, wts, feats, edges, delta)

        @pl.when(more[q] > 0)
        def _(q=q, gathered=gathered):
            gathered(rest)
            messages(layer, q * slots, counts_ref[q], rest, weights, basis, wts, feats, edges, delta)

    slot = lax.broadcasted_iota(jnp.int32, (2 * slots, 1), 0)
    limit = jnp.where(slot < slots, counts_ref[0], counts_ref[1] + slots)
    live = flag(slot < limit)
    mine = own_ref[...].reshape(2 * slots, -1)[:, : 4 * chan].astype(f32)
    packed = before[0 : 2 * slots, :]
    moved = pltpu.roll(packed, slots - counts_ref[0], 0)
    change = delta[0 : 2 * slots, :] + jnp.where(slot < slots, packed, moved)
    state = ((mine + message_scale * change) * live).astype(bf16)
    state_ref[...] = state
    if last:
        x = dot(state[:, :chan], read_in_ref[...])
        each = half_silu(0.5 * x) * read_out_ref[...] * live
        energy_ref[...] = jnp.broadcast_to(jnp.sum(each, keepdims=True), energy_ref.shape)


vmem = pl.BlockSpec(memory_space=pltpu.VMEM)
smem = pl.BlockSpec(memory_space=pltpu.SMEM)


def scratch(span, main):
    return [
        pltpu.VMEM((span, 4 * chan), bf16),
        *[pltpu.VMEM((span, 2 * chan), bf16)] * 3,
        *[pltpu.VMEM((block * hidden, main), bf16)] * 8,
    ]


def cost(atoms):
    return pl.CostEstimate(
        flops=2 * 2 * slots * atoms * 81920, bytes_accessed=4000000, transcendentals=4000000
    )


params = pltpu.CompilerParams(vmem_limit_bytes=40 * 1024 * 1024)
delta_shape = jax.ShapeDtypeStruct((room, 4 * chan), f32)


def kept_shapes(span, order):
    return (
        jax.ShapeDtypeStruct((8, room, span), f32),
        jax.ShapeDtypeStruct((4, room, span), f32),
        jax.ShapeDtypeStruct(order, bf16),
        jax.ShapeDtypeStruct((2,), jnp.int32),
    )


kept_specs = (vmem, vmem, vmem, smem)


def own_call(layer, counts, ys, weights, table, kept):
    operands = [counts, *ys, *weights]
    specs = [smem] + [vmem] * (len(operands) - 1)
    shapes, outs = (delta_shape,), (vmem,)
    if layer == 0:
        operands.append(table)
        specs.append(vmem)
        shapes += kept_shapes(own_span, (own_span, own_atoms))
        outs += kept_specs
    else:
        operands += kept
        specs += kept_specs
    return pl.pallas_call(
        functools.partial(own_kernel, layer),
        out_shape=shapes,
        in_specs=specs,
        out_specs=outs,
        scratch_shapes=scratch(own_span, own_main),
        compiler_params=params,
        cost_estimate=cost(own_atoms),
        name=f"own_part_{layer}",
    )(*operands)


def side_call(layer, last, counts, low, high, own, delta, weights, readout, table, kept):
    operands = [counts, low, high, own, delta, *weights]
    specs = [smem] + [vmem] * (len(operands) - 1)
    shapes, outs = (jax.ShapeDtypeStruct((2 * slots, 4 * chan), bf16),), (vmem,)
    if last:
        operands += readout
        specs += [vmem] * 2
        shapes += (jax.ShapeDtypeStruct((chan, chan), f32),)
        outs += (vmem,)
    if layer == 0:
        operands.append(table)
        specs.append(vmem)
        shapes += kept_shapes(side_span, (2, side_span, side_atoms))
        outs += kept_specs
    else:
        operands += kept
        specs += kept_specs
    return pl.pallas_call(
        functools.partial(side_kernel, layer, last),
        out_shape=shapes,
        in_specs=specs,
        out_specs=outs,
        scratch_shapes=scratch(side_span, side_main) + [pltpu.VMEM(delta_shape.shape, f32)],
        compiler_params=params,
        cost_estimate=cost(side_atoms),
        name=f"side_part_{layer}",
    )(*operands)


def shifted(value, axis, step):
    count = lax.axis_size(axis)
    return lax.ppermute(value, axis, [((i + step) % count, i) for i in range(count)])


def tables():
    j = np.arange(own_atoms)
    slot, z, plane, y = j % slots, j // slots % 3, j // (3 * slots) % 2, j // (6 * slots)
    own = np.zeros((own_atoms, chan), np.float32)
    own[:, 4], own[:, 5], own[:, 6] = plane * 5, (y - 1) * 5, (z - 1) * 5
    own[:, 7] = np.where((y == 1) & (z == 1), plane * slots + slot + 1, 0)
    j = np.arange(side_atoms)
    side = np.zeros((side_atoms, chan), np.float32)
    side[:, 5], side[:, 6] = (j // (3 * slots) - 1) * 5, (j // slots % 3 - 1) * 5
    return jnp.asarray(own, bf16), jnp.asarray(side, bf16)


def radial_rows(radial_in, radial_bias):
    layers = radial_in.shape[0]
    eye = jnp.asarray(np.eye(block) * 0.5, bf16)
    spread = radial_in.transpose(0, 2, 1)[:, None, :, :, None] * eye[:, None, None, :]
    spread = spread.reshape(layers, block * hidden, 8 * block)
    bias = jnp.stack([p * jnp.asarray(0.5, bf16) for p in pieces(radial_bias)], axis=2)
    bias = jnp.broadcast_to(bias[:, None], (layers, block, hidden, 3))
    bias = bias.reshape(layers, block * hidden, 3)
    return jnp.pad(
        jnp.concatenate([spread, bias], axis=2), ((0, 0), (0, 0), (0, depth - 8 * block - 3))
    )


def on_device(
    positions,
    counts,
    scalars,
    vectors,
    radial_in,
    radial_bias,
    radial_out,
    atom_in,
    atom_bias,
    atom_out,
    readout_in,
    readout_out,
):
    counts = counts.reshape(2)
    live = (lax.broadcasted_iota(jnp.int32, (2, slots), 1) < counts[:, None]).astype(f32)
    geo = jnp.concatenate([positions.reshape(2, 3, slots), live[:, None, :]], axis=1)
    geo = jnp.pad(geo.transpose(0, 2, 1), ((0, 0), (0, 0), (0, 4)))
    geo = jnp.concatenate(pieces(geo), axis=2)
    geo = jnp.pad(geo, ((0, 0), (0, 0), (0, chan - 24)))
    own = jnp.concatenate(
        [
            scalars.reshape(2, slots, chan),
            vectors.reshape(2, slots, 3 * chan),
            geo,
        ],
        axis=2,
    )
    layers = radial_in.shape[0]
    own_table, side_table = tables()
    own_kept = side_kept = ()
    for layer in range(layers):
        last = layer == layers - 1
        y = jnp.stack([shifted(own, "gz", -1), own, shifted(own, "gz", 1)], axis=1)
        if layer == 0:
            y, radial_in, radial_bias = lax.optimization_barrier((y, radial_in, radial_bias))
            rin = radial_rows(radial_in, radial_bias)
            weights = [rin, radial_out, atom_in, atom_bias, atom_out]
        ys = [shifted(y, "gy", -1), y, shifted(y, "gy", 1)]
        low = shifted(jnp.stack([v[1] for v in ys]), "gx", -1)
        high = shifted(jnp.stack([v[0] for v in ys]), "gx", 1)
        delta, *kept = own_call(layer, counts, ys, weights, own_table, own_kept)
        own_kept = own_kept or kept
        readout = [readout_in, readout_out[None, :]]
        state, *kept = side_call(
            layer, last, counts, low, high, own, delta, weights, readout, side_table, side_kept
        )
        if last:
            energy = kept[0]
        else:
            side_kept = side_kept or kept
            own = state.reshape(2, slots, 4 * chan)
    scalar_state = state[:, :chan].reshape(scalars.shape)
    vector_state = state[:, chan:].reshape(vectors.shape)
    every = lax.all_to_all(energy, ("gx", "gy", "gz"), 0, 0, tiled=True)
    energy = jnp.sum(every, axis=0)[:1]
    return scalar_state, vector_state, energy


def solution(mesh):
    in_specs = (
        P("gx", "gy", "gz", None, None),
        P("gx", "gy", "gz"),
        P("gx", "gy", "gz", None, None),
        P("gx", "gy", "gz", None, None, None),
        P(),
        P(),
        P(),
        P(),
        P(),
        P(),
        P(),
        P(),
    )
    out_specs = (P("gx", "gy", "gz", None, None), P("gx", "gy", "gz", None, None, None), P())
    return jax.shard_map(
        on_device, mesh=mesh, in_specs=in_specs, out_specs=out_specs, check_vma=False
    )
```

```python
import functools
import math

import jax
import jax.numpy as jnp
import numpy as np
from jax import lax
from jax.experimental import pallas as pl
from jax.experimental.pallas import tpu as pltpu
from jax.sharding import PartitionSpec as P

cutoff = 5.0
message_scale = 0.5
slots = 32
chan = 128
hidden = 64
block = 8
room = 2 * slots + block
depth = 80
own_atoms, own_main, own_span = 576, 512, 640
side_atoms, side_main, side_span = 288, 256, 384
f32 = jnp.float32
bf16 = jnp.bfloat16
across = (((1,), (1,)), ((), ()))


def pieces(value):
    high = lax.reduce_precision(value, 8, 7)
    rest = value - high
    middle = lax.reduce_precision(rest, 8, 7)
    low = lax.reduce_precision(rest - middle, 8, 7)
    return high.astype(bf16), middle.astype(bf16), low.astype(bf16)


def dot(a, b):
    return jnp.dot(a, b, preferred_element_type=f32)


def half_silu(y):
    return y + y * jnp.tanh(y)


def iotas(shape):
    return lax.broadcasted_iota(jnp.int32, shape, 0), lax.broadcasted_iota(jnp.int32, shape, 1)


def flag(condition):
    return jnp.where(condition, 1.0, 0.0)


def rows_of(geo):
    row, lane = iotas((8, chan))
    pick = flag((lane == row) | (lane == row + 8) | (lane == row + 16)).astype(bf16)
    return lax.dot_general(pick, geo, across, preferred_element_type=f32)


def columns_of(geo):
    row, lane = iotas((chan, chan))
    pick = flag((lane == row) | (lane + 8 == row) | (lane + 16 == row)).astype(bf16)
    return dot(geo, pick)


def own_table(y):
    row, lane = iotas((own_atoms // 3, chan))
    plane = flag(row >= 3 * slots)
    row = jnp.where(row >= 3 * slots, row - 3 * slots, row)
    z = flag(row >= slots) + flag(row >= 2 * slots) - 1.0
    table = jnp.where(lane == 4, plane * cutoff, 0.0) + jnp.where(lane == 6, z * cutoff, 0.0)
    table += jnp.where(lane == 5, (y - 1) * cutoff, 0.0)
    if y == 1:
        name = (row - slots + 1).astype(f32) + plane * slots
        table += jnp.where((lane == 7) & (z == 0.0), name, 0.0)
    return table.astype(bf16)


def side_table():
    row, lane = iotas((side_atoms, chan))
    y = flag(row >= 3 * slots) + flag(row >= 6 * slots) - 1.0
    row = row.astype(f32) - (y + 1.0) * (3 * slots)
    z = flag(row >= slots) + flag(row >= 2 * slots) - 1.0
    table = jnp.where(lane == 5, y * cutoff, 0.0) + jnp.where(lane == 6, z * cutoff, 0.0)
    return table.astype(bf16)


def compaction(live, span):
    atoms = live.shape[1]
    row, lane = iotas((atoms, atoms))
    before = flag(row < lane).astype(bf16)
    rank = dot(jnp.broadcast_to(live, (8, atoms)).astype(bf16), before)[0:1]
    rank = jnp.where(live > 0.5, rank, -1.0)
    row = lax.broadcasted_iota(jnp.int32, (span, atoms), 0).astype(f32)
    return flag(row == rank).astype(bf16)


def geometry(row, mine, number, shift, pairs_ref, at):
    dist2 = None
    disp = []
    for k in range(3):
        offset = row[4 + k : 5 + k] + shift if k == 0 else row[4 + k : 5 + k]
        d = (row[k : k + 1] + offset) - mine[:, k : k + 1]
        disp.append(d)
        dist2 = d * d if k == 0 else dist2 + d * d
    live = row[3:4]
    itself = flag(row[7:8] == number.astype(f32))
    dist = jnp.sqrt(dist2 + itself + (1.0 - live))
    smooth = jnp.where(dist < cutoff, 0.5 * (jnp.cos(math.pi * dist / cutoff) + 1.0), 0.0)
    weight = smooth * live * (1.0 - itself)
    scaled = weight / dist
    pairs_ref[8, at, :] = weight
    for k in range(3):
        pairs_ref[9 + k, at, :] = scaled * disp[k]
    sharp = 0.5 * (7.0 / cutoff) ** 2
    for k in range(8):
        away = dist - k * (cutoff / 7.0)
        pairs_ref[k, at, :] = jnp.exp(-sharp * (away * away))


def features(layer, x, part, weights, feats):
    _, _, ain_ref, abias_ref, aout_ref = weights
    s = x[:, :chan]
    bias = abias_ref[layer : layer + 1, :]
    hid = half_silu(0.5 * (dot(s, ain_ref[layer]) + bias)).astype(bf16)
    gates = dot(hid, aout_ref[layer]).astype(bf16)
    ga, gb = gates[:, :chan], gates[:, chan : 2 * chan]
    gc, gg = gates[:, 2 * chan : 3 * chan], gates[:, 3 * chan :]
    vec = [x[:, (k + 1) * chan : (k + 2) * chan] for k in range(3)]
    feats[0][part, :] = jnp.concatenate([ga] + [gb * v for v in vec], axis=1)
    for k in range(3):
        feats[1 + k][part, :] = jnp.concatenate([gc, gg * vec[k]], axis=1)


def messages(layer, count, place, window, weights, pairs_ref, feats, edges, delta):
    rin_ref, rout_ref = weights[:2]
    width = window.stop - window.start
    even, odd = edges[:4], edges[4:]

    def rows_at(b):
        return pl.ds(pl.multiple_of(place(b)[0], block), block)

    def hidden_of(b):
        slab = pairs_ref[0:8, rows_at(b), window].reshape(8 * block, width)
        slab = jnp.concatenate([slab, jnp.ones((depth - 8 * block, width), f32)], axis=0)
        return dot(rin_ref[layer], slab.astype(bf16)), pairs_ref[8:12, rows_at(b), window]

    def edge(r, y, w, out):
        part = slice(r * hidden, (r + 1) * hidden)
        s = half_silu(y[part]).astype(bf16).reshape(4, 16, width)
        for g in range(4):
            line = jnp.broadcast_to(w[g][r : r + 1, :], (16, width)).astype(bf16)
            out[g][part, :width] = (s * line[None]).reshape(hidden, width)

    def product(n, used, atoms):
        if n < 2:
            return dot(used[0][:, :width], feats[0][atoms, 2 * n * chan : 2 * (n + 1) * chan])
        return dot(used[n - 1][:, :width], feats[n - 1][atoms, :])

    def gather(n, result, radial, sums):
        groups = ((0, 1), (1, 1), (2, 3), (2, 3), (2, 3))[n]
        targets = ((0, 1), (2, 3), (1, 0), (2, 0), (3, 0))[n]
        for half in range(2):
            value = result[:, half * chan : (half + 1) * chan].reshape(block, hidden, chan)
            value = jnp.sum(value * radial[groups[half]], axis=1)
            t = targets[half]
            sums[t] = value if sums[t] is None else sums[t] + value

    def step(b, used, following):
        radial = [rout_ref[layer, :, g * chan : (g + 1) * chan].astype(f32)[None] for g in range(4)]
        sums = [None] * 4
        atoms = pl.ds(pl.multiple_of(place(b)[1], chan), width)
        if following is not None:
            y, w = hidden_of(b + 1)
        made, previous = 0, None
        for n in range(5):
            result = product(n, used, atoms)
            while following is not None and made < block and made * 5 < (n + 1) * block:
                edge(made, y, w, following)
                made += 1
            if n > 0:
                gather(n - 1, previous, radial, sums)
            previous = result
        gather(4, previous, radial, sums)
        for g in range(4):
            delta[rows_at(b), g * chan : (g + 1) * chan] += sums[g]

    y, w = hidden_of(0)
    for r in range(block):
        edge(r, y, w, even)

    def two_steps(t, carry):
        step(2 * t, even, odd)
        step(2 * t + 1, odd, even)
        return carry

    lax.fori_loop(0, count // 2, two_steps, 0)

    @pl.when(count % 2 == 1)
    def _():
        step(count - 1, even, None)


def own_kernel(layer, *refs):
    counts_ref, low, middle, high = refs[:4]
    weights = refs[4:9]
    refs = refs[9:]
    if layer == 0:
        delta, pairs_out, order_out, more = refs[:4]
        refs = refs[4:]
        pairs, order, done = refs[12:]
    else:
        pairs, order, more, delta = refs[:4]
        refs = refs[4:]
    feats, edges = refs[:4], refs[4:12]
    parts = [ref[...].reshape(own_atoms // 3, -1) for ref in (low, middle, high)]
    third = own_atoms // 3
    if layer == 0:
        geo = [p[:, 4 * chan :] + own_table(n) for n, p in enumerate(parts)]
        geo = jnp.concatenate(geo, axis=0)
        live = rows_of(geo)[3:4]
        order[...] = compaction(live, own_span)
        row = rows_of(dot(order[...], geo).astype(bf16))
        total = jnp.sum(live)
        more[0] = jnp.where(total > own_main + 0.5, 1, 0)
        first = counts_ref[0]
        mine = columns_of(
            jnp.concatenate([middle[q, 1][:, 4 * chan :] for q in range(2)], axis=0)
        )
        place = lax.broadcasted_iota(jnp.int32, (2 * slots, 1), 0)
        moved = pltpu.roll(mine, lax.rem(first + slots, 2 * slots), 0)
        mine = jnp.where(place < first, mine, moved)
        number = jnp.where(place < first, place + 1, place - first + (slots + 1))
        shift = jnp.where(place < first, 0.0, -cutoff)
        geometry(row, mine, number, shift, pairs, slice(0, 2 * slots))
        keep = [
            pltpu.make_async_copy(pairs, pairs_out, done.at[0]),
            pltpu.make_async_copy(order, order_out, done.at[1]),
        ]
        for copy in keep:
            copy.start()

    def gathered(part):
        x = None
        for n in range(3):
            y = dot(order[part, n * third : (n + 1) * third], parts[n][:, : 4 * chan])
            x = y if n == 0 else x + y
        features(layer, x.astype(bf16), part, weights, feats)

    delta[...] = jnp.zeros_like(delta)
    main, rest = slice(0, own_main), slice(own_main, own_span)
    count = (counts_ref[0] + counts_ref[1] + block - 1) // block

    def add(part):
        gathered(part)
        messages(
            layer,
            count,
            lambda b: (b * block, part.start),
            part,
            weights,
            pairs,
            feats,
            edges,
            delta,
        )

    add(main)

    @pl.when(more[0] > 0)
    def _():
        add(rest)

    if layer == 0:
        for copy in keep:
            copy.wait()


def side_kernel(layer, last, *refs):
    counts_ref, low, high, own_ref, before = refs[:5]
    weights = refs[5:10]
    refs = refs[10:]
    if last:
        read_in_ref, read_out_ref = refs[:2]
        refs = refs[2:]
    if layer > 0:
        (pairs, order, more), refs = refs[:3], refs[3:]
    state_ref, refs = refs[0], refs[1:]
    if last:
        energy_ref, refs = refs[0], refs[1:]
    if layer == 0:
        (pairs, order, more), refs = refs[:3], refs[3:]
    feats, edges, delta = refs[:4], refs[4:12], refs[12]
    delta[...] = jnp.zeros_like(delta)
    main, rest = slice(0, side_main), slice(side_main, side_span)
    atoms = [ref[...].reshape(side_atoms, -1) for ref in (low, high)]
    if layer == 0:
        total = []
        for q in range(2):
            geo = atoms[q][:, 4 * chan :] + side_table()
            live = rows_of(geo)[3:4]
            order[q] = compaction(live, side_span)
            row = rows_of(dot(order[q], geo).astype(bf16))
            total.append(jnp.sum(live))
            mine = columns_of(own_ref[q][:, 4 * chan :])
            at = slice(q * slots, (q + 1) * slots)
            number = lax.broadcasted_iota(jnp.int32, (slots, 1), 0) + (q * slots + 1)
            geometry(row, mine, number, (-cutoff, cutoff)[q], pairs, at)
        more[0] = jnp.where(jnp.maximum(total[0], total[1]) > side_main + 0.5, 1, 0)
    below = (counts_ref[0] + block - 1) // block
    above = (counts_ref[1] + block - 1) // block

    def add(part):
        for q in range(2):
            x = dot(order[q, part, :], atoms[q][:, : 4 * chan])
            rows = slice(q * side_span + part.start, q * side_span + part.stop)
            features(layer, x.astype(bf16), rows, weights, feats)

        def place(b):
            q = jnp.where(b >= below, 1, 0)
            return b * block + q * (slots - below * block), q * side_span + part.start

        messages(layer, below + above, place, part, weights, pairs, feats, edges, delta)

    add(main)

    @pl.when(more[0] > 0)
    def _():
        add(rest)

    slot = lax.broadcasted_iota(jnp.int32, (2 * slots, 1), 0)
    limit = jnp.where(slot < slots, counts_ref[0], counts_ref[1] + slots)
    live = flag(slot < limit)
    mine = own_ref[...].reshape(2 * slots, -1)[:, : 4 * chan].astype(f32)
    packed = before[0 : 2 * slots, :]
    moved = pltpu.roll(packed, slots - counts_ref[0], 0)
    change = delta[0 : 2 * slots, :] + jnp.where(slot < slots, packed, moved)
    state = ((mine + message_scale * change) * live).astype(bf16)
    state_ref[...] = state
    if last:
        x = dot(state[:, :chan], read_in_ref[...])
        each = half_silu(0.5 * x) * read_out_ref[...] * live
        energy_ref[...] = jnp.broadcast_to(jnp.sum(each, keepdims=True), energy_ref.shape)


vmem = pl.BlockSpec(memory_space=pltpu.VMEM)
smem = pl.BlockSpec(memory_space=pltpu.SMEM)
hbm = pl.BlockSpec(memory_space=pltpu.HBM)


def scratch(rows, main):
    return [
        pltpu.VMEM((rows, 4 * chan), bf16),
        *[pltpu.VMEM((rows, 2 * chan), bf16)] * 3,
        *[pltpu.VMEM((block * hidden, main), bf16)] * 8,
    ]


def cost(atoms):
    return pl.CostEstimate(
        flops=2 * 2 * slots * atoms * 81920, bytes_accessed=4000000, transcendentals=4000000
    )


params = pltpu.CompilerParams(vmem_limit_bytes=24 * 1024 * 1024)
delta_shape = jax.ShapeDtypeStruct((room, 4 * chan), f32)


def kept_shapes(span, order):
    return (
        jax.ShapeDtypeStruct((12, room, span), f32),
        jax.ShapeDtypeStruct(order, bf16),
        jax.ShapeDtypeStruct((2,), jnp.int32),
    )


kept_specs = (vmem, vmem, smem)


def own_call(layer, counts, ys, weights, kept):
    operands = [counts, *ys, *weights]
    specs = [smem] + [vmem] * (len(operands) - 1)
    shapes, outs = (delta_shape,), (vmem,)
    held = scratch(own_span, own_main)
    if layer == 0:
        kept_out = kept_shapes(own_span, (own_span, own_atoms))
        shapes += tuple(pltpu.HBM(k.shape, k.dtype) for k in kept_out[:2]) + kept_out[2:]
        outs += (hbm, hbm, smem)
        held += [pltpu.VMEM(k.shape, k.dtype) for k in kept_out[:2]]
        held += [pltpu.SemaphoreType.DMA((2,))]
    else:
        operands += kept
        specs += kept_specs
    return pl.pallas_call(
        functools.partial(own_kernel, layer),
        out_shape=shapes,
        in_specs=specs,
        out_specs=outs,
        scratch_shapes=held,
        compiler_params=params,
        cost_estimate=cost(own_atoms),
        name=f"own_part_{layer}",
    )(*operands)


def side_call(layer, last, counts, low, high, own, delta, weights, readout, kept):
    operands = [counts, low, high, own, delta, *weights]
    specs = [smem] + [vmem] * (len(operands) - 1)
    shapes, outs = (jax.ShapeDtypeStruct((2 * slots, 4 * chan), bf16),), (vmem,)
    if last:
        operands += readout
        specs += [vmem] * 2
        shapes += (jax.ShapeDtypeStruct((chan, chan), f32),)
        outs += (vmem,)
    if layer == 0:
        shapes += kept_shapes(side_span, (2, side_span, side_atoms))
        outs += kept_specs
    else:
        operands += kept
        specs += kept_specs
    return pl.pallas_call(
        functools.partial(side_kernel, layer, last),
        out_shape=shapes,
        in_specs=specs,
        out_specs=outs,
        scratch_shapes=scratch(2 * side_span, side_main) + [pltpu.VMEM(delta_shape.shape, f32)],
        compiler_params=params,
        cost_estimate=cost(side_atoms),
        name=f"side_part_{layer}",
    )(*operands)


def shifted(value, axis, step):
    count = lax.axis_size(axis)
    return lax.ppermute(value, axis, [((i + step) % count, i) for i in range(count)])


def radial_rows(radial_in, radial_bias):
    layers = radial_in.shape[0]
    eye = jnp.asarray(np.eye(block) * 0.5, bf16)
    spread = radial_in.transpose(0, 2, 1)[:, None, :, :, None] * eye[:, None, None, :]
    spread = spread.reshape(layers, block * hidden, 8 * block)
    bias = jnp.stack([p * jnp.asarray(0.5, bf16) for p in pieces(radial_bias)], axis=2)
    bias = jnp.broadcast_to(bias[:, None], (layers, block, hidden, 3))
    bias = bias.reshape(layers, block * hidden, 3)
    return jnp.pad(
        jnp.concatenate([spread, bias], axis=2), ((0, 0), (0, 0), (0, depth - 8 * block - 3))
    )


def on_device(
    positions,
    counts,
    scalars,
    vectors,
    radial_in,
    radial_bias,
    radial_out,
    atom_in,
    atom_bias,
    atom_out,
    readout_in,
    readout_out,
):
    counts = counts.reshape(2)
    live = (lax.broadcasted_iota(jnp.int32, (2, slots), 1) < counts[:, None]).astype(f32)
    geo = jnp.concatenate([positions.reshape(2, 3, slots), live[:, None, :]], axis=1)
    geo = jnp.pad(geo.transpose(0, 2, 1), ((0, 0), (0, 0), (0, 4)))
    geo = jnp.concatenate(pieces(geo), axis=2)
    geo = jnp.pad(geo, ((0, 0), (0, 0), (0, chan - 24)))
    own = jnp.concatenate(
        [
            scalars.reshape(2, slots, chan),
            vectors.reshape(2, slots, 3 * chan),
            geo,
        ],
        axis=2,
    )
    layers = radial_in.shape[0]
    own_kept = side_kept = ()
    for layer in range(layers):
        last = layer == layers - 1
        y = jnp.stack([shifted(own, "gz", -1), own, shifted(own, "gz", 1)], axis=1)
        if layer == 0:
            y, radial_in, radial_bias = lax.optimization_barrier((y, radial_in, radial_bias))
            rin = radial_rows(radial_in, radial_bias)
            weights = [rin, radial_out, atom_in, atom_bias, atom_out]
        ys = [shifted(y, "gy", -1), y, shifted(y, "gy", 1)]
        low = shifted(jnp.stack([v[1] for v in ys]), "gx", -1)
        high = shifted(jnp.stack([v[0] for v in ys]), "gx", 1)
        delta, *kept = own_call(layer, counts, ys, weights, own_kept)
        own_kept = own_kept or kept
        readout = [readout_in, readout_out[None, :]]
        state, *kept = side_call(
            layer, last, counts, low, high, own, delta, weights, readout, side_kept
        )
        if last:
            energy = kept[0]
        else:
            side_kept = side_kept or kept
            own = state.reshape(2, slots, 4 * chan)
    scalar_state = state[:, :chan].reshape(scalars.shape)
    vector_state = state[:, chan:].reshape(vectors.shape)
    every = lax.all_to_all(energy, ("gx", "gy", "gz"), 0, 0, tiled=True)
    energy = jnp.sum(every, axis=0)[:1]
    return scalar_state, vector_state, energy


def solution(mesh):
    in_specs = (
        P("gx", "gy", "gz", None, None),
        P("gx", "gy", "gz"),
        P("gx", "gy", "gz", None, None),
        P("gx", "gy", "gz", None, None, None),
        P(),
        P(),
        P(),
        P(),
        P(),
        P(),
        P(),
        P(),
    )
    out_specs = (P("gx", "gy", "gz", None, None), P("gx", "gy", "gz", None, None, None), P())
    return jax.shard_map(
        on_device, mesh=mesh, in_specs=in_specs, out_specs=out_specs, check_vma=False
    )
```

```python
import functools
import math

import jax
import jax.numpy as jnp
import numpy as np
from jax import lax
from jax.experimental import pallas as pl
from jax.experimental.pallas import tpu as pltpu
from jax.sharding import PartitionSpec as P

cutoff = 5.0
message_scale = 0.5
slots = 32
chan = 128
hidden = 64
block = 8
room = 2 * slots + block
depth = 80
own_atoms, own_main, own_span = 576, 512, 640
side_atoms, side_main, side_span = 288, 256, 384
f32 = jnp.float32
bf16 = jnp.bfloat16
across = (((1,), (1,)), ((), ()))


def pieces(value):
    high = lax.reduce_precision(value, 8, 7)
    rest = value - high
    middle = lax.reduce_precision(rest, 8, 7)
    low = lax.reduce_precision(rest - middle, 8, 7)
    return high.astype(bf16), middle.astype(bf16), low.astype(bf16)


def dot(a, b):
    return jnp.dot(a, b, preferred_element_type=f32)


def half_silu(y):
    return y + y * jnp.tanh(y)


def iotas(shape):
    return lax.broadcasted_iota(jnp.int32, shape, 0), lax.broadcasted_iota(jnp.int32, shape, 1)


def flag(condition):
    return jnp.where(condition, 1.0, 0.0)


def rows_of(geo):
    row, lane = iotas((8, chan))
    pick = flag((lane == row) | (lane == row + 8) | (lane == row + 16)).astype(bf16)
    return lax.dot_general(pick, geo, across, preferred_element_type=f32)


def columns_of(geo):
    row, lane = iotas((chan, chan))
    pick = flag((lane == row) | (lane + 8 == row) | (lane + 16 == row)).astype(bf16)
    return dot(geo, pick)


def own_table(y):
    row, lane = iotas((own_atoms // 3, chan))
    plane = flag(row >= 3 * slots)
    row = jnp.where(row >= 3 * slots, row - 3 * slots, row)
    z = flag(row >= slots) + flag(row >= 2 * slots) - 1.0
    table = jnp.where(lane == 4, plane * cutoff, 0.0) + jnp.where(lane == 6, z * cutoff, 0.0)
    table += jnp.where(lane == 5, (y - 1) * cutoff, 0.0)
    if y == 1:
        name = (row - slots + 1).astype(f32) + plane * slots
        table += jnp.where((lane == 7) & (z == 0.0), name, 0.0)
    return table.astype(bf16)


def side_table():
    row, lane = iotas((side_atoms, chan))
    y = flag(row >= 3 * slots) + flag(row >= 6 * slots) - 1.0
    row = row.astype(f32) - (y + 1.0) * (3 * slots)
    z = flag(row >= slots) + flag(row >= 2 * slots) - 1.0
    table = jnp.where(lane == 5, y * cutoff, 0.0) + jnp.where(lane == 6, z * cutoff, 0.0)
    return table.astype(bf16)


def compaction(live, span):
    atoms = live.shape[0]
    ranks = []
    total = jnp.zeros((1, 1), f32)
    for at in range(0, atoms, chan):
        part = live[at : at + chan]
        row, lane = iotas((part.shape[0], part.shape[0]))
        before = jnp.sum(jnp.where(row < lane, part, 0.0), axis=0, keepdims=True)
        own = jnp.sum(jnp.where(row == lane, part, 0.0), axis=0, keepdims=True)
        ranks.append(jnp.where(own > 0.5, before + total, -1.0))
        total = total + jnp.sum(part, axis=0, keepdims=True)
    rank = jnp.concatenate(ranks, axis=1)
    row = lax.broadcasted_iota(jnp.int32, (span, atoms), 0).astype(f32)
    return flag(row == rank).astype(bf16), total


def geometry(row, mine, number, shift, pairs_ref, at):
    dist2 = None
    disp = []
    for k in range(3):
        offset = row[4 + k : 5 + k] + shift if k == 0 else row[4 + k : 5 + k]
        d = (row[k : k + 1] + offset) - mine[:, k : k + 1]
        disp.append(d)
        dist2 = d * d if k == 0 else dist2 + d * d
    live = row[3:4]
    itself = flag(row[7:8] == number.astype(f32))
    dist = jnp.sqrt(dist2 + itself + (1.0 - live))
    smooth = jnp.where(dist < cutoff, 0.5 * (jnp.cos(math.pi * dist / cutoff) + 1.0), 0.0)
    weight = smooth * live * (1.0 - itself)
    scaled = weight / dist
    pairs_ref[8, at, :] = weight
    for k in range(3):
        pairs_ref[9 + k, at, :] = scaled * disp[k]
    sharp = 0.5 * (7.0 / cutoff) ** 2
    for k in range(8):
        away = dist - k * (cutoff / 7.0)
        pairs_ref[k, at, :] = jnp.exp(-sharp * (away * away))


def features(layer, x, part, weights, feats):
    _, _, ain_ref, abias_ref, aout_ref = weights
    s = x[:, :chan]
    bias = abias_ref[layer : layer + 1, :]
    hid = half_silu(0.5 * (dot(s, ain_ref[layer]) + bias)).astype(bf16)
    gates = dot(hid, aout_ref[layer]).astype(bf16)
    ga, gb = gates[:, :chan], gates[:, chan : 2 * chan]
    gc, gg = gates[:, 2 * chan : 3 * chan], gates[:, 3 * chan :]
    vec = [x[:, (k + 1) * chan : (k + 2) * chan] for k in range(3)]
    feats[0][part, :] = jnp.concatenate([ga] + [gb * v for v in vec], axis=1)
    for k in range(3):
        feats[1 + k][part, :] = jnp.concatenate([gc, gg * vec[k]], axis=1)


def messages(layer, count, place, window, weights, pairs_ref, feats, edges, delta):
    rin_ref, rout_ref = weights[:2]
    width = window.stop - window.start
    even, odd = edges[:4], edges[4:]

    def rows_at(b):
        return pl.ds(pl.multiple_of(place(b)[0], block), block)

    def hidden_of(b):
        slab = pairs_ref[0:8, rows_at(b), window].reshape(8 * block, width)
        slab = jnp.concatenate([slab, jnp.ones((depth - 8 * block, width), f32)], axis=0)
        return dot(rin_ref[layer], slab.astype(bf16)), pairs_ref[8:12, rows_at(b), window]

    def edge(r, y, w, out):
        part = slice(r * hidden, (r + 1) * hidden)
        s = half_silu(y[part]).astype(bf16).reshape(4, 16, width)
        for g in range(4):
            line = jnp.broadcast_to(w[g][r : r + 1, :], (16, width)).astype(bf16)
            out[g][part, :width] = (s * line[None]).reshape(hidden, width)

    def product(n, used, atoms):
        if n < 2:
            return dot(used[0][:, :width], feats[0][atoms, 2 * n * chan : 2 * (n + 1) * chan])
        return dot(used[n - 1][:, :width], feats[n - 1][atoms, :])

    def gather(n, result, radial, sums):
        groups = ((0, 1), (1, 1), (2, 3), (2, 3), (2, 3))[n]
        targets = ((0, 1), (2, 3), (1, 0), (2, 0), (3, 0))[n]
        for half in range(2):
            value = result[:, half * chan : (half + 1) * chan].reshape(block, hidden, chan)
            value = jnp.sum(value * radial[groups[half]], axis=1)
            t = targets[half]
            sums[t] = value if sums[t] is None else sums[t] + value

    def step(b, used, following):
        radial = [rout_ref[layer, :, g * chan : (g + 1) * chan].astype(f32)[None] for g in range(4)]
        sums = [None] * 4
        atoms = pl.ds(pl.multiple_of(place(b)[1], chan), width)
        if following is not None:
            y, w = hidden_of(b + 1)
        made, previous = 0, None
        for n in range(5):
            result = product(n, used, atoms)
            while following is not None and made < block and made * 5 < (n + 1) * block:
                edge(made, y, w, following)
                made += 1
            if n > 0:
                gather(n - 1, previous, radial, sums)
            previous = result
        gather(4, previous, radial, sums)
        for g in range(4):
            delta[rows_at(b), g * chan : (g + 1) * chan] += sums[g]

    y, w = hidden_of(0)
    for r in range(block):
        edge(r, y, w, even)

    def two_steps(t, carry):
        step(2 * t, even, odd)
        step(2 * t + 1, odd, even)
        return carry

    lax.fori_loop(0, count // 2, two_steps, 0)

    @pl.when(count % 2 == 1)
    def _():
        step(count - 1, even, None)


def own_kernel(layer, *refs):
    counts_ref, low, middle, high = refs[:4]
    weights = refs[4:9]
    refs = refs[9:]
    if layer == 0:
        delta, pairs_out, order_out, more = refs[:4]
        refs = refs[4:]
        pairs, order, done = refs[12:]
    else:
        pairs, order, more, delta = refs[:4]
        refs = refs[4:]
    feats, edges = refs[:4], refs[4:12]
    parts = [ref[...].reshape(own_atoms // 3, -1) for ref in (low, middle, high)]
    third = own_atoms // 3
    if layer == 0:
        geo = [p[:, 4 * chan :] + own_table(n) for n, p in enumerate(parts)]
        geo = jnp.concatenate(geo, axis=0)
        order[...], total = compaction(geo[:, 3:4].astype(f32), own_span)
        row = rows_of(dot(order[...], geo).astype(bf16))
        more[0] = jnp.where(jnp.sum(total) > own_main + 0.5, 1, 0)
        first = counts_ref[0]
        mine = columns_of(
            jnp.concatenate([middle[q, 1][:, 4 * chan :] for q in range(2)], axis=0)
        )
        place = lax.broadcasted_iota(jnp.int32, (2 * slots, 1), 0)
        moved = pltpu.roll(mine, lax.rem(first + slots, 2 * slots), 0)
        mine = jnp.where(place < first, mine, moved)
        number = jnp.where(place < first, place + 1, place - first + (slots + 1))
        shift = jnp.where(place < first, 0.0, -cutoff)
        geometry(row, mine, number, shift, pairs, slice(0, 2 * slots))
        keep = [
            pltpu.make_async_copy(pairs, pairs_out, done.at[0]),
            pltpu.make_async_copy(order, order_out, done.at[1]),
        ]
        for copy in keep:
            copy.start()

    def gathered(part):
        x = None
        for n in range(3):
            y = dot(order[part, n * third : (n + 1) * third], parts[n][:, : 4 * chan])
            x = y if n == 0 else x + y
        features(layer, x.astype(bf16), part, weights, feats)

    delta[...] = jnp.zeros_like(delta)
    main, rest = slice(0, own_main), slice(own_main, own_span)
    count = (counts_ref[0] + counts_ref[1] + block - 1) // block

    def add(part):
        gathered(part)
        messages(
            layer,
            count,
            lambda b: (b * block, part.start),
            part,
            weights,
            pairs,
            feats,
            edges,
            delta,
        )

    add(main)

    @pl.when(more[0] > 0)
    def _():
        add(rest)

    if layer == 0:
        for copy in keep:
            copy.wait()


def side_kernel(layer, last, *refs):
    counts_ref, low, high, own_ref, before = refs[:5]
    weights = refs[5:10]
    refs = refs[10:]
    if last:
        read_in_ref, read_out_ref = refs[:2]
        refs = refs[2:]
    if layer > 0:
        (pairs, order, more), refs = refs[:3], refs[3:]
    if last:
        (scalar_ref, vector_ref, energy_ref), refs = refs[:3], refs[3:]
    else:
        state_ref, refs = refs[0], refs[1:]
    if layer == 0:
        (pairs, order, more), refs = refs[:3], refs[3:]
    feats, edges, delta = refs[:4], refs[4:12], refs[12]
    delta[...] = jnp.zeros_like(delta)
    main, rest = slice(0, side_main), slice(side_main, side_span)
    atoms = [ref[...].reshape(side_atoms, -1) for ref in (low, high)]
    if layer == 0:
        total = []
        for q in range(2):
            geo = atoms[q][:, 4 * chan :] + side_table()
            order[q], number = compaction(geo[:, 3:4].astype(f32), side_span)
            total.append(jnp.sum(number))
            row = rows_of(dot(order[q], geo).astype(bf16))
            mine = columns_of(own_ref[q][:, 4 * chan :])
            at = slice(q * slots, (q + 1) * slots)
            number = lax.broadcasted_iota(jnp.int32, (slots, 1), 0) + (q * slots + 1)
            geometry(row, mine, number, (-cutoff, cutoff)[q], pairs, at)
        more[0] = jnp.where(jnp.maximum(total[0], total[1]) > side_main + 0.5, 1, 0)
    below = (counts_ref[0] + block - 1) // block
    above = (counts_ref[1] + block - 1) // block

    def add(part):
        for q in range(2):
            x = dot(order[q, part, :], atoms[q][:, : 4 * chan])
            rows = slice(q * side_span + part.start, q * side_span + part.stop)
            features(layer, x.astype(bf16), rows, weights, feats)

        def place(b):
            q = jnp.where(b >= below, 1, 0)
            return b * block + q * (slots - below * block), q * side_span + part.start

        messages(layer, below + above, place, part, weights, pairs, feats, edges, delta)

    add(main)

    @pl.when(more[0] > 0)
    def _():
        add(rest)

    slot = lax.broadcasted_iota(jnp.int32, (2 * slots, 1), 0)
    limit = jnp.where(slot < slots, counts_ref[0], counts_ref[1] + slots)
    live = flag(slot < limit)
    mine = own_ref[...].reshape(2 * slots, -1)[:, : 4 * chan].astype(f32)
    packed = before[0 : 2 * slots, :]
    moved = pltpu.roll(packed, slots - counts_ref[0], 0)
    change = delta[0 : 2 * slots, :] + jnp.where(slot < slots, packed, moved)
    state = ((mine + message_scale * change) * live).astype(bf16)
    if not last:
        state_ref[...] = state
    else:
        for q in range(2):
            at = slice(q * slots, (q + 1) * slots)
            scalar_ref[q] = state[at, :chan]
            for k in range(3):
                vector_ref[q, k] = state[at, (k + 1) * chan : (k + 2) * chan]
        x = dot(state[:, :chan], read_in_ref[...])
        each = half_silu(0.5 * x) * read_out_ref[...] * live
        energy_ref[...] = jnp.broadcast_to(jnp.sum(each, keepdims=True), energy_ref.shape)


vmem = pl.BlockSpec(memory_space=pltpu.VMEM)
smem = pl.BlockSpec(memory_space=pltpu.SMEM)
hbm = pl.BlockSpec(memory_space=pltpu.HBM)


def scratch(rows, main):
    return [
        pltpu.VMEM((rows, 4 * chan), bf16),
        *[pltpu.VMEM((rows, 2 * chan), bf16)] * 3,
        *[pltpu.VMEM((block * hidden, main), bf16)] * 8,
    ]


def cost(atoms):
    return pl.CostEstimate(
        flops=2 * 2 * slots * atoms * 81920, bytes_accessed=4000000, transcendentals=4000000
    )


params = pltpu.CompilerParams(vmem_limit_bytes=24 * 1024 * 1024)
delta_shape = jax.ShapeDtypeStruct((room, 4 * chan), f32)


def kept_shapes(span, order):
    return (
        jax.ShapeDtypeStruct((12, room, span), f32),
        jax.ShapeDtypeStruct(order, bf16),
        jax.ShapeDtypeStruct((2,), jnp.int32),
    )


kept_specs = (vmem, vmem, smem)


def own_call(layer, counts, ys, weights, kept):
    operands = [counts, *ys, *weights]
    specs = [smem] + [vmem] * (len(operands) - 1)
    shapes, outs = (delta_shape,), (vmem,)
    held = scratch(own_span, own_main)
    if layer == 0:
        kept_out = kept_shapes(own_span, (own_span, own_atoms))
        shapes += tuple(pltpu.HBM(k.shape, k.dtype) for k in kept_out[:2]) + kept_out[2:]
        outs += (hbm, hbm, smem)
        held += [pltpu.VMEM(k.shape, k.dtype) for k in kept_out[:2]]
        held += [pltpu.SemaphoreType.DMA((2,))]
    else:
        operands += kept
        specs += kept_specs
    return pl.pallas_call(
        functools.partial(own_kernel, layer),
        out_shape=shapes,
        in_specs=specs,
        out_specs=outs,
        scratch_shapes=held,
        compiler_params=params,
        cost_estimate=cost(own_atoms),
        name=f"own_part_{layer}",
    )(*operands)


def side_call(layer, last, counts, low, high, own, delta, weights, readout, kept):
    operands = [counts, low, high, own, delta, *weights]
    specs = [smem] + [vmem] * (len(operands) - 1)
    shapes, outs = (jax.ShapeDtypeStruct((2 * slots, 4 * chan), bf16),), (vmem,)
    if last:
        operands += readout
        specs += [vmem] * 2
        shapes = (
            jax.ShapeDtypeStruct((2, slots, chan), bf16),
            jax.ShapeDtypeStruct((2, 3, slots, chan), bf16),
            jax.ShapeDtypeStruct((chan, chan), f32),
        )
        outs = (vmem,) * 3
    if layer == 0:
        shapes += kept_shapes(side_span, (2, side_span, side_atoms))
        outs += kept_specs
    else:
        operands += kept
        specs += kept_specs
    return pl.pallas_call(
        functools.partial(side_kernel, layer, last),
        out_shape=shapes,
        in_specs=specs,
        out_specs=outs,
        scratch_shapes=scratch(2 * side_span, side_main) + [pltpu.VMEM(delta_shape.shape, f32)],
        compiler_params=params,
        cost_estimate=cost(side_atoms),
        name=f"side_part_{layer}",
    )(*operands)


def pack_kernel(counts_in, position_in, scalar_in, vector_in, out_ref, counts_ref, place, done):
    copies = [(counts_in, counts_ref), (position_in, place)]
    for q in range(2):
        copies.append((scalar_in.at[q], out_ref.at[q, :, pl.ds(0, chan)]))
        for k in range(3):
            at = pl.ds((k + 1) * chan, chan)
            copies.append((vector_in.at[q, k], out_ref.at[q, :, at]))
    copies = [pltpu.make_async_copy(*c, done.at[n]) for n, c in enumerate(copies)]
    for copy in copies:
        copy.start()
    for copy in copies:
        copy.wait()
    row, lane = iotas((2, slots))
    live = flag(lane < jnp.where(row == 0, counts_ref[0], counts_ref[1]))
    rest = jnp.concatenate([place[q, k] for k in range(3) for q in range(2)] + [live], axis=0)
    addends = []
    for _ in range(3):
        addends.append(rest.astype(bf16).astype(f32))
        rest = rest - addends[-1]
    addends = jnp.concatenate(addends, axis=0).astype(bf16)
    row, lane = iotas((24, chan))
    target = (row // 8) * 8 + (row % 8) // 2
    for q in range(2):
        spread = flag((lane == target) & (row % 2 == q)).astype(bf16)
        geo = lax.dot_general(
            addends, spread, (((0,), (0,)), ((), ())), preferred_element_type=f32
        )
        out_ref[q, :, 4 * chan :] = geo.astype(bf16)


def pack_call(*operands):
    operands = [pltpu.with_memory_space_constraint(x, pltpu.HBM) for x in operands]
    return pl.pallas_call(
        pack_kernel,
        out_shape=jax.ShapeDtypeStruct((2, slots, 5 * chan), bf16),
        in_specs=[hbm] * 4,
        out_specs=vmem,
        scratch_shapes=[
            pltpu.SMEM((2,), jnp.int32),
            pltpu.VMEM((2, 3, 1, slots), f32),
            pltpu.SemaphoreType.DMA((10,)),
        ],
        compiler_params=pltpu.CompilerParams(vmem_limit_bytes=4 * 1024 * 1024),
        name="pack",
    )(*operands)


def shifted(value, axis, step):
    count = lax.axis_size(axis)
    return lax.ppermute(value, axis, [((i + step) % count, i) for i in range(count)])


def radial_rows(radial_in, radial_bias):
    layers = radial_in.shape[0]
    eye = jnp.asarray(np.eye(block) * 0.5, bf16)
    spread = radial_in.transpose(0, 2, 1)[:, None, :, :, None] * eye[:, None, None, :]
    spread = spread.reshape(layers, block * hidden, 8 * block)
    bias = jnp.stack([p * jnp.asarray(0.5, bf16) for p in pieces(radial_bias)], axis=2)
    bias = jnp.broadcast_to(bias[:, None], (layers, block, hidden, 3))
    bias = bias.reshape(layers, block * hidden, 3)
    return jnp.pad(
        jnp.concatenate([spread, bias], axis=2), ((0, 0), (0, 0), (0, depth - 8 * block - 3))
    )


def on_device(
    positions,
    counts,
    scalars,
    vectors,
    radial_in,
    radial_bias,
    radial_out,
    atom_in,
    atom_bias,
    atom_out,
    readout_in,
    readout_out,
):
    counts = counts.reshape(2)
    own = pack_call(
        counts,
        positions.reshape(2, 3, 1, slots),
        scalars.reshape(2, slots, chan),
        vectors.reshape(2, slots, 3, chan).transpose(0, 2, 1, 3),
    )
    layers = radial_in.shape[0]
    own_kept = side_kept = ()
    for layer in range(layers):
        last = layer == layers - 1
        y = jnp.stack([shifted(own, "gz", -1), own, shifted(own, "gz", 1)], axis=1)
        if layer == 0:
            y, radial_in, radial_bias = lax.optimization_barrier((y, radial_in, radial_bias))
            rin = radial_rows(radial_in, radial_bias)
            weights = [rin, radial_out, atom_in, atom_bias, atom_out]
        ys = [shifted(y, "gy", -1), y, shifted(y, "gy", 1)]
        low = shifted(jnp.stack([v[1] for v in ys]), "gx", -1)
        high = shifted(jnp.stack([v[0] for v in ys]), "gx", 1)
        delta, *kept = own_call(layer, counts, ys, weights, own_kept)
        own_kept = own_kept or kept
        readout = [readout_in, readout_out[None, :]]
        state, *kept = side_call(
            layer, last, counts, low, high, own, delta, weights, readout, side_kept
        )
        if last:
            vector_state, energy = kept
        else:
            side_kept = side_kept or kept
            own = state.reshape(2, slots, 4 * chan)
    scalar_state = state.reshape(scalars.shape)
    vector_state = vector_state.transpose(0, 2, 1, 3).reshape(vectors.shape)
    every = lax.all_to_all(energy, ("gx", "gy", "gz"), 0, 0, tiled=True)
    energy = jnp.sum(every, axis=0)[:1]
    return scalar_state, vector_state, energy


def solution(mesh):
    in_specs = (
        P("gx", "gy", "gz", None, None),
        P("gx", "gy", "gz"),
        P("gx", "gy", "gz", None, None),
        P("gx", "gy", "gz", None, None, None),
        P(),
        P(),
        P(),
        P(),
        P(),
        P(),
        P(),
        P(),
    )
    out_specs = (P("gx", "gy", "gz", None, None), P("gx", "gy", "gz", None, None, None), P())
    return jax.shard_map(
        on_device, mesh=mesh, in_specs=in_specs, out_specs=out_specs, check_vma=False
    )
```

```python
import functools
import math

import jax
import jax.numpy as jnp
import numpy as np
from jax import lax
from jax.experimental import pallas as pl
from jax.experimental.pallas import tpu as pltpu
from jax.sharding import PartitionSpec as P

cutoff = 5.0
message_scale = 0.5
slots = 32
chan = 128
hidden = 64
block = 8
room = 2 * slots + block
depth = 80
own_atoms, own_main, own_span = 576, 512, 640
side_atoms, side_main, side_span = 288, 256, 384
f32 = jnp.float32
bf16 = jnp.bfloat16
across = (((1,), (1,)), ((), ()))


def pieces(value):
    high = lax.reduce_precision(value, 8, 7)
    rest = value - high
    middle = lax.reduce_precision(rest, 8, 7)
    low = lax.reduce_precision(rest - middle, 8, 7)
    return high.astype(bf16), middle.astype(bf16), low.astype(bf16)


def dot(a, b):
    return jnp.dot(a, b, preferred_element_type=f32)


def half_silu(y):
    return y + y * jnp.tanh(y)


def iotas(shape):
    return lax.broadcasted_iota(jnp.int32, shape, 0), lax.broadcasted_iota(jnp.int32, shape, 1)


def flag(condition):
    return jnp.where(condition, 1.0, 0.0)


def rows_of(geo):
    row, lane = iotas((8, chan))
    pick = flag((lane == row) | (lane == row + 8) | (lane == row + 16)).astype(bf16)
    return lax.dot_general(pick, geo, across, preferred_element_type=f32)


def columns_of(geo):
    row, lane = iotas((chan, chan))
    pick = flag((lane == row) | (lane + 8 == row) | (lane + 16 == row)).astype(bf16)
    return dot(geo, pick)


def own_table(y):
    row, lane = iotas((own_atoms // 3, chan))
    plane = flag(row >= 3 * slots)
    row = jnp.where(row >= 3 * slots, row - 3 * slots, row)
    z = flag(row >= slots) + flag(row >= 2 * slots) - 1.0
    table = jnp.where(lane == 4, plane * cutoff, 0.0) + jnp.where(lane == 6, z * cutoff, 0.0)
    table += jnp.where(lane == 5, (y - 1) * cutoff, 0.0)
    if y == 1:
        name = (row - slots + 1).astype(f32) + plane * slots
        table += jnp.where((lane == 7) & (z == 0.0), name, 0.0)
    return table.astype(bf16)


def side_table():
    row, lane = iotas((side_atoms, chan))
    y = flag(row >= 3 * slots) + flag(row >= 6 * slots) - 1.0
    row = row.astype(f32) - (y + 1.0) * (3 * slots)
    z = flag(row >= slots) + flag(row >= 2 * slots) - 1.0
    table = jnp.where(lane == 5, y * cutoff, 0.0) + jnp.where(lane == 6, z * cutoff, 0.0)
    return table.astype(bf16)


def compaction(live, span):
    atoms = live.shape[0]
    ranks = []
    total = jnp.zeros((1, 1), f32)
    for at in range(0, atoms, chan):
        part = live[at : at + chan]
        row, lane = iotas((part.shape[0], part.shape[0]))
        before = jnp.sum(jnp.where(row < lane, part, 0.0), axis=0, keepdims=True)
        own = jnp.sum(jnp.where(row == lane, part, 0.0), axis=0, keepdims=True)
        ranks.append(jnp.where(own > 0.5, before + total, -1.0))
        total = total + jnp.sum(part, axis=0, keepdims=True)
    rank = jnp.concatenate(ranks, axis=1)
    row = lax.broadcasted_iota(jnp.int32, (span, atoms), 0).astype(f32)
    return flag(row == rank).astype(bf16), total


def geometry(row, mine, number, shift, pairs_ref, at):
    dist2 = None
    disp = []
    for k in range(3):
        offset = row[4 + k : 5 + k] + shift if k == 0 else row[4 + k : 5 + k]
        d = (row[k : k + 1] + offset) - mine[:, k : k + 1]
        disp.append(d)
        dist2 = d * d if k == 0 else dist2 + d * d
    live = row[3:4]
    itself = flag(row[7:8] == number.astype(f32))
    dist = jnp.sqrt(dist2 + itself + (1.0 - live))
    smooth = jnp.where(dist < cutoff, 0.5 * (jnp.cos(math.pi * dist / cutoff) + 1.0), 0.0)
    weight = smooth * live * (1.0 - itself)
    scaled = weight / dist
    pairs_ref[8, at, :] = weight
    for k in range(3):
        pairs_ref[9 + k, at, :] = scaled * disp[k]
    sharp = 0.5 * (7.0 / cutoff) ** 2
    for k in range(8):
        away = dist - k * (cutoff / 7.0)
        pairs_ref[k, at, :] = jnp.exp(-sharp * (away * away))


def features(layer, x, part, weights, feats):
    _, _, ain_ref, abias_ref, aout_ref = weights
    s = x[:, :chan]
    bias = abias_ref[layer : layer + 1, :]
    hid = half_silu(0.5 * (dot(s, ain_ref[layer]) + bias)).astype(bf16)
    gates = dot(hid, aout_ref[layer]).astype(bf16)
    ga, gb = gates[:, :chan], gates[:, chan : 2 * chan]
    gc, gg = gates[:, 2 * chan : 3 * chan], gates[:, 3 * chan :]
    vec = [x[:, (k + 1) * chan : (k + 2) * chan] for k in range(3)]
    feats[0][part, :] = jnp.concatenate([ga] + [gb * v for v in vec], axis=1)
    for k in range(3):
        feats[1 + k][part, :] = jnp.concatenate([gc, gg * vec[k]], axis=1)


def rows_from(start):
    return pl.ds(pl.multiple_of(start, block), block)


def hidden_of(rin, pairs_ref, rows, window):
    width = window.stop - window.start
    slab = pairs_ref[0:8, rows, window].reshape(8 * block, width)
    slab = jnp.concatenate([slab, jnp.ones((depth - 8 * block, width), f32)], axis=0)
    return dot(rin, slab.astype(bf16)), pairs_ref[8:12, rows, window]


def edge(r, y, w, out):
    part = slice(r * hidden, (r + 1) * hidden)
    width = y.shape[1]
    s = half_silu(y[part]).astype(bf16).reshape(4, 16, width)
    for g in range(4):
        line = jnp.broadcast_to(w[g][r : r + 1, :], (16, width)).astype(bf16)
        out[g][part, :width] = (s * line[None]).reshape(hidden, width)


def messages(layer, count, place, window, weights, pairs_ref, feats, edges, delta, ready=None):
    rin_ref, rout_ref = weights[:2]
    width = window.stop - window.start
    even, odd = edges[:4], edges[4:]

    def product(n, used, atoms):
        if n < 2:
            return dot(used[0][:, :width], feats[0][atoms, 2 * n * chan : 2 * (n + 1) * chan])
        return dot(used[n - 1][:, :width], feats[n - 1][atoms, :])

    def gather(n, result, radial, sums):
        groups = ((0, 1), (1, 1), (2, 3), (2, 3), (2, 3))[n]
        targets = ((0, 1), (2, 3), (1, 0), (2, 0), (3, 0))[n]
        for half in range(2):
            value = result[:, half * chan : (half + 1) * chan].reshape(block, hidden, chan)
            value = jnp.sum(value * radial[groups[half]], axis=1)
            t = targets[half]
            sums[t] = value if sums[t] is None else sums[t] + value

    def step(b, used, following):
        radial = [rout_ref[layer, :, g * chan : (g + 1) * chan].astype(f32)[None] for g in range(4)]
        sums = [None] * 4
        row, start = place(b)
        atoms = pl.ds(pl.multiple_of(start, chan), width)
        if ready is not None:
            used = [ready.at[b, g] for g in range(4)]
        if following is not None:
            y, w = hidden_of(rin_ref[layer], pairs_ref, rows_from(place(b + 1)[0]), window)
        made, previous = 0, None
        for n in range(5):
            result = product(n, used, atoms)
            while following is not None and made < block and made * 5 < (n + 1) * block:
                edge(made, y, w, following)
                made += 1
            if n > 0:
                gather(n - 1, previous, radial, sums)
            previous = result
        gather(4, previous, radial, sums)
        for g in range(4):
            delta[rows_from(row), g * chan : (g + 1) * chan] += sums[g]

    if ready is None:
        y, w = hidden_of(rin_ref[layer], pairs_ref, rows_from(place(0)[0]), window)
        for r in range(block):
            edge(r, y, w, even)
    else:
        even = odd = None

    def two_steps(t, carry):
        step(2 * t, even, odd)
        step(2 * t + 1, odd, even)
        return carry

    lax.fori_loop(0, count // 2, two_steps, 0)

    @pl.when(count % 2 == 1)
    def _():
        step(count - 1, even, None)


def blocks_of(count):
    return (count + block - 1) // block


def side_place(counts_ref, start):
    below = blocks_of(counts_ref[0])

    def place(b):
        q = jnp.where(b >= below, 1, 0)
        return b * block + q * (slots - below * block), q * side_span + start

    return below + blocks_of(counts_ref[1]), place


def edge_kernel(layer, counts_ref, rin_ref, own_pairs, side_pairs, own_out, side_out):
    def make(count, place, pairs, window, out):
        def one(b, carry):
            y, w = hidden_of(rin_ref[layer], pairs, rows_from(place(b)[0]), window)
            for r in range(block):
                edge(r, y, w, [out.at[b, g] for g in range(4)])
            return carry

        lax.fori_loop(0, count, one, 0)

    count = blocks_of(counts_ref[0] + counts_ref[1])
    make(count, lambda b: (b * block, 0), own_pairs, slice(0, own_main), own_out)
    make(*side_place(counts_ref, 0), side_pairs, slice(0, side_main), side_out)


def own_kernel(layer, *refs):
    counts_ref, low, middle, high = refs[:4]
    weights = refs[4:9]
    refs = refs[9:]
    if layer == 0:
        delta, pairs_out, order_out, more = refs[:4]
        refs = refs[4:]
        pairs, order, done = refs[12:]
    else:
        pairs, order, more, ready, delta = refs[:5]
        refs = refs[5:]
    feats, edges = refs[:4], refs[4:12]
    parts = [ref[...].reshape(own_atoms // 3, -1) for ref in (low, middle, high)]
    third = own_atoms // 3
    if layer == 0:
        geo = [p[:, 4 * chan :] + own_table(n) for n, p in enumerate(parts)]
        geo = jnp.concatenate(geo, axis=0)
        order[...], total = compaction(geo[:, 3:4].astype(f32), own_span)
        row = rows_of(dot(order[...], geo).astype(bf16))
        more[0] = jnp.where(jnp.sum(total) > own_main + 0.5, 1, 0)
        first = counts_ref[0]
        mine = columns_of(
            jnp.concatenate([middle[q, 1][:, 4 * chan :] for q in range(2)], axis=0)
        )
        place = lax.broadcasted_iota(jnp.int32, (2 * slots, 1), 0)
        moved = pltpu.roll(mine, lax.rem(first + slots, 2 * slots), 0)
        mine = jnp.where(place < first, mine, moved)
        number = jnp.where(place < first, place + 1, place - first + (slots + 1))
        shift = jnp.where(place < first, 0.0, -cutoff)
        geometry(row, mine, number, shift, pairs, slice(0, 2 * slots))
        keep = [
            pltpu.make_async_copy(pairs, pairs_out, done.at[0]),
            pltpu.make_async_copy(order, order_out, done.at[1]),
        ]
        for copy in keep:
            copy.start()

    def gathered(part):
        x = None
        for n in range(3):
            y = dot(order[part, n * third : (n + 1) * third], parts[n][:, : 4 * chan])
            x = y if n == 0 else x + y
        features(layer, x.astype(bf16), part, weights, feats)

    delta[...] = jnp.zeros_like(delta)
    main, rest = slice(0, own_main), slice(own_main, own_span)
    count = blocks_of(counts_ref[0] + counts_ref[1])

    def add(part, ready=None):
        gathered(part)
        messages(
            layer,
            count,
            lambda b: (b * block, part.start),
            part,
            weights,
            pairs,
            feats,
            edges,
            delta,
            ready,
        )

    add(main, None if layer == 0 else ready)

    @pl.when(more[0] > 0)
    def _():
        add(rest)

    if layer == 0:
        for copy in keep:
            copy.wait()


def side_kernel(layer, last, *refs):
    counts_ref, low, high, own_ref, before = refs[:5]
    weights = refs[5:10]
    refs = refs[10:]
    if last:
        read_in_ref, read_out_ref = refs[:2]
        refs = refs[2:]
    if layer > 0:
        (pairs, order, more, ready), refs = refs[:4], refs[4:]
    if last:
        (scalar_ref, vector_ref, energy_ref), refs = refs[:3], refs[3:]
    else:
        state_ref, refs = refs[0], refs[1:]
    if layer == 0:
        (pairs, order, more), refs = refs[:3], refs[3:]
    feats, edges, delta = refs[:4], refs[4:12], refs[12]
    delta[...] = jnp.zeros_like(delta)
    main, rest = slice(0, side_main), slice(side_main, side_span)
    atoms = [ref[...].reshape(side_atoms, -1) for ref in (low, high)]
    if layer == 0:
        total = []
        for q in range(2):
            geo = atoms[q][:, 4 * chan :] + side_table()
            order[q], number = compaction(geo[:, 3:4].astype(f32), side_span)
            total.append(jnp.sum(number))
            row = rows_of(dot(order[q], geo).astype(bf16))
            mine = columns_of(own_ref[q][:, 4 * chan :])
            at = slice(q * slots, (q + 1) * slots)
            number = lax.broadcasted_iota(jnp.int32, (slots, 1), 0) + (q * slots + 1)
            geometry(row, mine, number, (-cutoff, cutoff)[q], pairs, at)
        more[0] = jnp.where(jnp.maximum(total[0], total[1]) > side_main + 0.5, 1, 0)

    def add(part, ready=None):
        for q in range(2):
            x = dot(order[q, part, :], atoms[q][:, : 4 * chan])
            rows = slice(q * side_span + part.start, q * side_span + part.stop)
            features(layer, x.astype(bf16), rows, weights, feats)

        count, place = side_place(counts_ref, part.start)
        messages(layer, count, place, part, weights, pairs, feats, edges, delta, ready)

    add(main, None if layer == 0 else ready)

    @pl.when(more[0] > 0)
    def _():
        add(rest)

    slot = lax.broadcasted_iota(jnp.int32, (2 * slots, 1), 0)
    limit = jnp.where(slot < slots, counts_ref[0], counts_ref[1] + slots)
    live = flag(slot < limit)
    mine = own_ref[...].reshape(2 * slots, -1)[:, : 4 * chan].astype(f32)
    packed = before[0 : 2 * slots, :]
    moved = pltpu.roll(packed, slots - counts_ref[0], 0)
    change = delta[0 : 2 * slots, :] + jnp.where(slot < slots, packed, moved)
    state = ((mine + message_scale * change) * live).astype(bf16)
    if not last:
        state_ref[...] = state
    else:
        for q in range(2):
            at = slice(q * slots, (q + 1) * slots)
            scalar_ref[q] = state[at, :chan]
            for k in range(3):
                vector_ref[q, k] = state[at, (k + 1) * chan : (k + 2) * chan]
        x = dot(state[:, :chan], read_in_ref[...])
        each = half_silu(0.5 * x) * read_out_ref[...] * live
        energy_ref[...] = jnp.broadcast_to(jnp.sum(each, keepdims=True), energy_ref.shape)


vmem = pl.BlockSpec(memory_space=pltpu.VMEM)
smem = pl.BlockSpec(memory_space=pltpu.SMEM)
hbm = pl.BlockSpec(memory_space=pltpu.HBM)


def scratch(rows, main):
    return [
        pltpu.VMEM((rows, 4 * chan), bf16),
        *[pltpu.VMEM((rows, 2 * chan), bf16)] * 3,
        *[pltpu.VMEM((block * hidden, main), bf16)] * 8,
    ]


def cost(atoms):
    return pl.CostEstimate(
        flops=2 * 2 * slots * atoms * 81920, bytes_accessed=4000000, transcendentals=4000000
    )


params = [
    pltpu.CompilerParams(vmem_limit_bytes=24 * 1024 * 1024),
    pltpu.CompilerParams(vmem_limit_bytes=12 * 1024 * 1024),
]
delta_shape = jax.ShapeDtypeStruct((room, 4 * chan), f32)


def kept_shapes(span, order):
    return (
        jax.ShapeDtypeStruct((12, room, span), f32),
        jax.ShapeDtypeStruct(order, bf16),
        jax.ShapeDtypeStruct((2,), jnp.int32),
    )


kept_specs = (vmem, vmem, smem)


def own_call(layer, counts, ys, weights, kept):
    operands = [counts, *ys, *weights]
    specs = [smem] + [vmem] * (len(operands) - 1)
    shapes, outs = (delta_shape,), (vmem,)
    held = scratch(own_span, own_main if layer == 0 else own_span - own_main)
    if layer == 0:
        kept_out = kept_shapes(own_span, (own_span, own_atoms))
        shapes += tuple(pltpu.HBM(k.shape, k.dtype) for k in kept_out[:2]) + kept_out[2:]
        outs += (hbm, hbm, smem)
        held += [pltpu.VMEM(k.shape, k.dtype) for k in kept_out[:2]]
        held += [pltpu.SemaphoreType.DMA((2,))]
    else:
        operands += kept
        specs += kept_specs + (vmem,)
    return pl.pallas_call(
        functools.partial(own_kernel, layer),
        out_shape=shapes,
        in_specs=specs,
        out_specs=outs,
        scratch_shapes=held,
        compiler_params=params[min(layer, 1)],
        cost_estimate=cost(own_atoms),
        name=f"own_part_{layer}",
    )(*operands)


def edge_call(layer, counts, rin, own_pairs, side_pairs):
    count = 2 * slots // block
    return pl.pallas_call(
        functools.partial(edge_kernel, layer),
        out_shape=(
            pltpu.VMEM((count, 4, block * hidden, own_main), bf16),
            pltpu.VMEM((count, 4, block * hidden, side_main), bf16),
        ),
        in_specs=[smem, vmem, vmem, vmem],
        out_specs=(vmem, vmem),
        compiler_params=params[1],
        cost_estimate=pl.CostEstimate(
            flops=1000000000, bytes_accessed=4000000, transcendentals=4000000
        ),
        name=f"edges_{layer}",
    )(counts, rin, own_pairs, side_pairs)


def side_call(layer, last, counts, low, high, own, delta, weights, readout, kept):
    operands = [counts, low, high, own, delta, *weights]
    specs = [smem] + [vmem] * (len(operands) - 1)
    shapes, outs = (jax.ShapeDtypeStruct((2 * slots, 4 * chan), bf16),), (vmem,)
    if last:
        operands += readout
        specs += [vmem] * 2
        shapes = (
            jax.ShapeDtypeStruct((2, slots, chan), bf16),
            jax.ShapeDtypeStruct((2, 3, slots, chan), bf16),
            jax.ShapeDtypeStruct((chan, chan), f32),
        )
        outs = (vmem,) * 3
    if layer == 0:
        shapes += kept_shapes(side_span, (2, side_span, side_atoms))
        outs += kept_specs
    else:
        operands += kept
        specs += kept_specs + (vmem,)
    return pl.pallas_call(
        functools.partial(side_kernel, layer, last),
        out_shape=shapes,
        in_specs=specs,
        out_specs=outs,
        scratch_shapes=scratch(2 * side_span, side_main if layer == 0 else side_span - side_main) + [pltpu.VMEM(delta_shape.shape, f32)],
        compiler_params=params[min(layer, 1)],
        cost_estimate=cost(side_atoms),
        name=f"side_part_{layer}",
    )(*operands)


def pack_kernel(counts_in, position_in, scalar_in, vector_in, out_ref, counts_ref, place, done):
    copies = [(counts_in, counts_ref), (position_in, place)]
    for q in range(2):
        copies.append((scalar_in.at[q], out_ref.at[q, :, pl.ds(0, chan)]))
        for k in range(3):
            at = pl.ds((k + 1) * chan, chan)
            copies.append((vector_in.at[q, k], out_ref.at[q, :, at]))
    copies = [pltpu.make_async_copy(*c, done.at[n]) for n, c in enumerate(copies)]
    for copy in copies:
        copy.start()
    for copy in copies:
        copy.wait()
    row, lane = iotas((2, slots))
    live = flag(lane < jnp.where(row == 0, counts_ref[0], counts_ref[1]))
    rest = jnp.concatenate([place[q, k] for k in range(3) for q in range(2)] + [live], axis=0)
    addends = []
    for _ in range(3):
        addends.append(rest.astype(bf16).astype(f32))
        rest = rest - addends[-1]
    addends = jnp.concatenate(addends, axis=0).astype(bf16)
    row, lane = iotas((24, chan))
    target = (row // 8) * 8 + (row % 8) // 2
    for q in range(2):
        spread = flag((lane == target) & (row % 2 == q)).astype(bf16)
        geo = lax.dot_general(
            addends, spread, (((0,), (0,)), ((), ())), preferred_element_type=f32
        )
        out_ref[q, :, 4 * chan :] = geo.astype(bf16)


def pack_call(*operands):
    operands = [pltpu.with_memory_space_constraint(x, pltpu.HBM) for x in operands]
    return pl.pallas_call(
        pack_kernel,
        out_shape=jax.ShapeDtypeStruct((2, slots, 5 * chan), bf16),
        in_specs=[hbm] * 4,
        out_specs=vmem,
        scratch_shapes=[
            pltpu.SMEM((2,), jnp.int32),
            pltpu.VMEM((2, 3, 1, slots), f32),
            pltpu.SemaphoreType.DMA((10,)),
        ],
        compiler_params=pltpu.CompilerParams(vmem_limit_bytes=4 * 1024 * 1024),
        name="pack",
    )(*operands)


def shifted(value, axis, step):
    count = lax.axis_size(axis)
    return lax.ppermute(value, axis, [((i + step) % count, i) for i in range(count)])


def radial_rows(radial_in, radial_bias):
    layers = radial_in.shape[0]
    eye = jnp.asarray(np.eye(block) * 0.5, bf16)
    spread = radial_in.transpose(0, 2, 1)[:, None, :, :, None] * eye[:, None, None, :]
    spread = spread.reshape(layers, block * hidden, 8 * block)
    bias = jnp.stack([p * jnp.asarray(0.5, bf16) for p in pieces(radial_bias)], axis=2)
    bias = jnp.broadcast_to(bias[:, None], (layers, block, hidden, 3))
    bias = bias.reshape(layers, block * hidden, 3)
    return jnp.pad(
        jnp.concatenate([spread, bias], axis=2), ((0, 0), (0, 0), (0, depth - 8 * block - 3))
    )


def on_device(
    positions,
    counts,
    scalars,
    vectors,
    radial_in,
    radial_bias,
    radial_out,
    atom_in,
    atom_bias,
    atom_out,
    readout_in,
    readout_out,
):
    counts = counts.reshape(2)
    own = pack_call(
        counts,
        positions.reshape(2, 3, 1, slots),
        scalars.reshape(2, slots, chan),
        vectors.reshape(2, slots, 3, chan).transpose(0, 2, 1, 3),
    )
    layers = radial_in.shape[0]
    own_kept = side_kept = ()
    for layer in range(layers):
        last = layer == layers - 1
        y = jnp.stack([shifted(own, "gz", -1), own, shifted(own, "gz", 1)], axis=1)
        if layer == 0:
            y, radial_in, radial_bias = lax.optimization_barrier((y, radial_in, radial_bias))
            rin = radial_rows(radial_in, radial_bias)
            weights = [rin, radial_out, atom_in, atom_bias, atom_out]
            own_ready = side_ready = []
        else:
            y, own_kept, side_kept = lax.optimization_barrier((y, own_kept, side_kept))
            own_ready, side_ready = (
                [e] for e in edge_call(layer, counts, rin, own_kept[0], side_kept[0])
            )
        ys = [shifted(y, "gy", -1), y, shifted(y, "gy", 1)]
        low = shifted(jnp.stack([v[1] for v in ys]), "gx", -1)
        high = shifted(jnp.stack([v[0] for v in ys]), "gx", 1)
        delta, *kept = own_call(layer, counts, ys, weights, [*own_kept, *own_ready])
        own_kept = own_kept or kept
        readout = [readout_in, readout_out[None, :]]
        state, *kept = side_call(
            layer, last, counts, low, high, own, delta, weights, readout, [*side_kept, *side_ready]
        )
        if last:
            vector_state, energy = kept
        else:
            side_kept = side_kept or kept
            own = state.reshape(2, slots, 4 * chan)
    scalar_state = state.reshape(scalars.shape)
    vector_state = vector_state.transpose(0, 2, 1, 3).reshape(vectors.shape)
    every = lax.all_to_all(energy, ("gx", "gy", "gz"), 0, 0, tiled=True)
    energy = jnp.sum(every, axis=0)[:1]
    return scalar_state, vector_state, energy


def solution(mesh):
    in_specs = (
        P("gx", "gy", "gz", None, None),
        P("gx", "gy", "gz"),
        P("gx", "gy", "gz", None, None),
        P("gx", "gy", "gz", None, None, None),
        P(),
        P(),
        P(),
        P(),
        P(),
        P(),
        P(),
        P(),
    )
    out_specs = (P("gx", "gy", "gz", None, None), P("gx", "gy", "gz", None, None, None), P())
    return jax.shard_map(
        on_device, mesh=mesh, in_specs=in_specs, out_specs=out_specs, check_vma=False
    )
```

```python
import functools
import math

import jax
import jax.numpy as jnp
import numpy as np
from jax import lax
from jax.experimental import pallas as pl
from jax.experimental.pallas import tpu as pltpu
from jax.sharding import PartitionSpec as P

cutoff = 5.0
message_scale = 0.5
slots = 32
chan = 128
hidden = 64
block = 8
room = 2 * slots + block
depth = 80
own_atoms, own_main, own_span = 576, 512, 640
side_atoms, side_main, side_span = 288, 256, 384
f32 = jnp.float32
bf16 = jnp.bfloat16
across = (((1,), (1,)), ((), ()))


def pieces(value):
    high = lax.reduce_precision(value, 8, 7)
    rest = value - high
    middle = lax.reduce_precision(rest, 8, 7)
    low = lax.reduce_precision(rest - middle, 8, 7)
    return high.astype(bf16), middle.astype(bf16), low.astype(bf16)


def dot(a, b):
    return jnp.dot(a, b, preferred_element_type=f32)


def half_silu(y):
    return y + y * jnp.tanh(y)


def iotas(shape):
    return lax.broadcasted_iota(jnp.int32, shape, 0), lax.broadcasted_iota(jnp.int32, shape, 1)


def flag(condition):
    return jnp.where(condition, 1.0, 0.0)


def rows_of(geo):
    row, lane = iotas((8, chan))
    pick = flag((lane == row) | (lane == row + 8) | (lane == row + 16)).astype(bf16)
    return lax.dot_general(pick, geo, across, preferred_element_type=f32)


def columns_of(geo):
    row, lane = iotas((chan, chan))
    pick = flag((lane == row) | (lane + 8 == row) | (lane + 16 == row)).astype(bf16)
    return dot(geo, pick)


def own_table(y):
    row, lane = iotas((own_atoms // 3, chan))
    plane = flag(row >= 3 * slots)
    row = jnp.where(row >= 3 * slots, row - 3 * slots, row)
    z = flag(row >= slots) + flag(row >= 2 * slots) - 1.0
    table = jnp.where(lane == 4, plane * cutoff, 0.0) + jnp.where(lane == 6, z * cutoff, 0.0)
    table += jnp.where(lane == 5, (y - 1) * cutoff, 0.0)
    if y == 1:
        name = (row - slots + 1).astype(f32) + plane * slots
        table += jnp.where((lane == 7) & (z == 0.0), name, 0.0)
    return table.astype(bf16)


def side_table():
    row, lane = iotas((side_atoms, chan))
    y = flag(row >= 3 * slots) + flag(row >= 6 * slots) - 1.0
    row = row.astype(f32) - (y + 1.0) * (3 * slots)
    z = flag(row >= slots) + flag(row >= 2 * slots) - 1.0
    table = jnp.where(lane == 5, y * cutoff, 0.0) + jnp.where(lane == 6, z * cutoff, 0.0)
    return table.astype(bf16)


def compaction(live, span):
    atoms = live.shape[0]
    ranks = []
    total = jnp.zeros((1, 1), f32)
    for at in range(0, atoms, chan):
        part = live[at : at + chan]
        row, lane = iotas((part.shape[0], part.shape[0]))
        before = jnp.sum(jnp.where(row < lane, part, 0.0), axis=0, keepdims=True)
        own = jnp.sum(jnp.where(row == lane, part, 0.0), axis=0, keepdims=True)
        ranks.append(jnp.where(own > 0.5, before + total, -1.0))
        total = total + jnp.sum(part, axis=0, keepdims=True)
    rank = jnp.concatenate(ranks, axis=1)
    row = lax.broadcasted_iota(jnp.int32, (span, atoms), 0).astype(f32)
    return flag(row == rank).astype(bf16), total


def geometry(row, mine, number, shift, pairs_ref, at):
    dist2 = None
    disp = []
    for k in range(3):
        offset = row[4 + k : 5 + k] + shift if k == 0 else row[4 + k : 5 + k]
        d = (row[k : k + 1] + offset) - mine[:, k : k + 1]
        disp.append(d)
        dist2 = d * d if k == 0 else dist2 + d * d
    live = row[3:4]
    itself = flag(row[7:8] == number.astype(f32))
    dist = jnp.sqrt(dist2 + itself + (1.0 - live))
    smooth = jnp.where(dist < cutoff, 0.5 * (jnp.cos(math.pi * dist / cutoff) + 1.0), 0.0)
    weight = smooth * live * (1.0 - itself)
    scaled = weight / dist
    pairs_ref[8, at, :] = weight
    for k in range(3):
        pairs_ref[9 + k, at, :] = scaled * disp[k]
    sharp = 0.5 * (7.0 / cutoff) ** 2
    for k in range(8):
        away = dist - k * (cutoff / 7.0)
        pairs_ref[k, at, :] = jnp.exp(-sharp * (away * away))


def features(layer, x, part, weights, feats):
    _, _, ain_ref, abias_ref, aout_ref = weights
    s = x[:, :chan]
    bias = abias_ref[layer : layer + 1, :]
    hid = half_silu(0.5 * (dot(s, ain_ref[layer]) + bias)).astype(bf16)
    gates = dot(hid, aout_ref[layer]).astype(bf16)
    ga, gb = gates[:, :chan], gates[:, chan : 2 * chan]
    gc, gg = gates[:, 2 * chan : 3 * chan], gates[:, 3 * chan :]
    vec = [x[:, (k + 1) * chan : (k + 2) * chan] for k in range(3)]
    feats[0][part, :] = jnp.concatenate([ga] + [gb * v for v in vec], axis=1)
    for k in range(3):
        feats[1 + k][part, :] = jnp.concatenate([gc, gg * vec[k]], axis=1)


def messages(layer, count, place, window, weights, pairs_ref, feats, edges, delta):
    rin_ref, rout_ref = weights[:2]
    width = window.stop - window.start
    even, odd = edges[:4], edges[4:]

    def rows_at(b):
        return pl.ds(pl.multiple_of(place(b)[0], block), block)

    def hidden_of(b):
        slab = pairs_ref[0:8, rows_at(b), window].reshape(8 * block, width)
        slab = jnp.concatenate([slab, jnp.ones((depth - 8 * block, width), f32)], axis=0)
        return dot(rin_ref[layer], slab.astype(bf16)), pairs_ref[8:12, rows_at(b), window]

    def edge(r, y, w, out):
        part = slice(r * hidden, (r + 1) * hidden)
        s = half_silu(y[part]).astype(bf16).reshape(4, 16, width)
        for g in range(4):
            line = jnp.broadcast_to(w[g][r : r + 1, :], (16, width)).astype(bf16)
            out[g][part, :width] = (s * line[None]).reshape(hidden, width)

    def product(n, used, atoms):
        if n < 2:
            return dot(used[0][:, :width], feats[0][atoms, 2 * n * chan : 2 * (n + 1) * chan])
        return dot(used[n - 1][:, :width], feats[n - 1][atoms, :])

    def gather(n, result, radial, sums):
        groups = ((0, 1), (1, 1), (2, 3), (2, 3), (2, 3))[n]
        targets = ((0, 1), (2, 3), (1, 0), (2, 0), (3, 0))[n]
        for half in range(2):
            value = result[:, half * chan : (half + 1) * chan].reshape(block, hidden, chan)
            value = jnp.sum(value * radial[groups[half]], axis=1)
            t = targets[half]
            sums[t] = value if sums[t] is None else sums[t] + value

    def step(b, used, following):
        radial = [rout_ref[layer, :, g * chan : (g + 1) * chan].astype(f32)[None] for g in range(4)]
        sums = [None] * 4
        atoms = pl.ds(pl.multiple_of(place(b)[1], chan), width)
        if following is not None:
            y, w = hidden_of(b + 1)
        made, previous = 0, None
        for n in range(5):
            result = product(n, used, atoms)
            while following is not None and made < block and made * 5 < (n + 1) * block:
                edge(made, y, w, following)
                made += 1
            if n > 0:
                gather(n - 1, previous, radial, sums)
            previous = result
        gather(4, previous, radial, sums)
        for g in range(4):
            delta[rows_at(b), g * chan : (g + 1) * chan] += sums[g]

    y, w = hidden_of(0)
    for r in range(block):
        edge(r, y, w, even)

    def two_steps(t, carry):
        step(2 * t, even, odd)
        step(2 * t + 1, odd, even)
        return carry

    lax.fori_loop(0, count // 2, two_steps, 0)

    @pl.when(count % 2 == 1)
    def _():
        step(count - 1, even, None)


def ready_kernel(layer, *refs):
    counts_ref, low, middle, high = refs[:4]
    weights = (None, None, *refs[4:7])
    refs = refs[7:]
    if layer == 0:
        feats, refs = refs[:4], refs[4:]
        pairs, order_out, more, order, done = refs
    else:
        order, feats = refs[0], refs[1:]
    parts = [ref[...].reshape(own_atoms // 3, -1) for ref in (low, middle, high)]
    third = own_atoms // 3
    if layer == 0:
        geo = [p[:, 4 * chan :] + own_table(n) for n, p in enumerate(parts)]
        geo = jnp.concatenate(geo, axis=0)
        order[...], total = compaction(geo[:, 3:4].astype(f32), own_span)
        keep = pltpu.make_async_copy(order, order_out, done.at[0])
        keep.start()
    x = None
    for n in range(3):
        y = dot(order[:, n * third : (n + 1) * third], parts[n][:, : 4 * chan])
        x = y if n == 0 else x + y
    features(layer, x.astype(bf16), slice(0, own_span), weights, feats)
    if layer == 0:
        row = rows_of(dot(order[...], geo).astype(bf16))
        more[0] = jnp.where(jnp.sum(total) > own_main + 0.5, 1, 0)
        first = counts_ref[0]
        mine = columns_of(
            jnp.concatenate([middle[q, 1][:, 4 * chan :] for q in range(2)], axis=0)
        )
        place = lax.broadcasted_iota(jnp.int32, (2 * slots, 1), 0)
        moved = pltpu.roll(mine, lax.rem(first + slots, 2 * slots), 0)
        mine = jnp.where(place < first, mine, moved)
        number = jnp.where(place < first, place + 1, place - first + (slots + 1))
        shift = jnp.where(place < first, 0.0, -cutoff)
        geometry(row, mine, number, shift, pairs, slice(0, 2 * slots))
        keep.wait()


def own_kernel(layer, *refs):
    counts_ref, weights, feats, pairs, more, delta = refs[0], refs[1:3], refs[3:7], *refs[7:10]
    refs = refs[10:]
    if layer == 0:
        pairs_out, done, refs = refs[0], refs[-1], refs[1:-1]
        keep = pltpu.make_async_copy(pairs, pairs_out, done.at[0])
        keep.start()
    edges = refs
    count = (counts_ref[0] + counts_ref[1] + block - 1) // block
    delta[...] = jnp.zeros_like(delta)

    def add(part):
        messages(
            layer,
            count,
            lambda b: (b * block, part.start),
            part,
            weights,
            pairs,
            feats,
            edges,
            delta,
        )

    add(slice(0, own_main))

    @pl.when(more[0] > 0)
    def _():
        add(slice(own_main, own_span))

    if layer == 0:
        keep.wait()


def side_kernel(layer, last, *refs):
    counts_ref, low, high, own_ref, before = refs[:5]
    weights = refs[5:10]
    refs = refs[10:]
    if last:
        read_in_ref, read_out_ref = refs[:2]
        refs = refs[2:]
    if layer > 0:
        (pairs, order, more), refs = refs[:3], refs[3:]
    if last:
        (scalar_ref, vector_ref, energy_ref), refs = refs[:3], refs[3:]
    else:
        state_ref, refs = refs[0], refs[1:]
    if layer == 0:
        (pairs, order_out, more), refs = refs[:3], refs[3:]
        order, done = refs[13:]
    feats, edges, delta = refs[:4], refs[4:12], refs[12]
    delta[...] = jnp.zeros_like(delta)
    main, rest = slice(0, side_main), slice(side_main, side_span)
    atoms = [ref[...].reshape(side_atoms, -1) for ref in (low, high)]
    if layer == 0:
        total = []
        for q in range(2):
            geo = atoms[q][:, 4 * chan :] + side_table()
            order[q], number = compaction(geo[:, 3:4].astype(f32), side_span)
            total.append(jnp.sum(number))
            row = rows_of(dot(order[q], geo).astype(bf16))
            mine = columns_of(own_ref[q][:, 4 * chan :])
            at = slice(q * slots, (q + 1) * slots)
            number = lax.broadcasted_iota(jnp.int32, (slots, 1), 0) + (q * slots + 1)
            geometry(row, mine, number, (-cutoff, cutoff)[q], pairs, at)
        more[0] = jnp.where(jnp.maximum(total[0], total[1]) > side_main + 0.5, 1, 0)
        keep = pltpu.make_async_copy(order, order_out, done.at[0])
        keep.start()
    below = (counts_ref[0] + block - 1) // block
    above = (counts_ref[1] + block - 1) // block

    def add(part):
        for q in range(2):
            x = dot(order[q, part, :], atoms[q][:, : 4 * chan])
            rows = slice(q * side_span + part.start, q * side_span + part.stop)
            features(layer, x.astype(bf16), rows, weights, feats)

        def place(b):
            q = jnp.where(b >= below, 1, 0)
            return b * block + q * (slots - below * block), q * side_span + part.start

        messages(layer, below + above, place, part, weights, pairs, feats, edges, delta)

    add(main)

    @pl.when(more[0] > 0)
    def _():
        add(rest)

    slot = lax.broadcasted_iota(jnp.int32, (2 * slots, 1), 0)
    limit = jnp.where(slot < slots, counts_ref[0], counts_ref[1] + slots)
    live = flag(slot < limit)
    mine = own_ref[...].reshape(2 * slots, -1)[:, : 4 * chan].astype(f32)
    packed = before[0 : 2 * slots, :]
    moved = pltpu.roll(packed, slots - counts_ref[0], 0)
    change = delta[0 : 2 * slots, :] + jnp.where(slot < slots, packed, moved)
    state = ((mine + message_scale * change) * live).astype(bf16)
    if layer == 0:
        keep.wait()
    if not last:
        state_ref[...] = state
    else:
        for q in range(2):
            at = slice(q * slots, (q + 1) * slots)
            scalar_ref[q] = state[at, :chan]
            for k in range(3):
                vector_ref[q, k] = state[at, (k + 1) * chan : (k + 2) * chan]
        x = dot(state[:, :chan], read_in_ref[...])
        each = half_silu(0.5 * x) * read_out_ref[...] * live
        energy_ref[...] = jnp.broadcast_to(jnp.sum(each, keepdims=True), energy_ref.shape)


vmem = pl.BlockSpec(memory_space=pltpu.VMEM)
smem = pl.BlockSpec(memory_space=pltpu.SMEM)
hbm = pl.BlockSpec(memory_space=pltpu.HBM)


def scratch(rows, main):
    return [
        pltpu.VMEM((rows, 4 * chan), bf16),
        *[pltpu.VMEM((rows, 2 * chan), bf16)] * 3,
        *[pltpu.VMEM((block * hidden, main), bf16)] * 8,
    ]


def cost(atoms):
    return pl.CostEstimate(
        flops=2 * 2 * slots * atoms * 81920, bytes_accessed=4000000, transcendentals=4000000
    )


params = pltpu.CompilerParams(vmem_limit_bytes=24 * 1024 * 1024)
delta_shape = jax.ShapeDtypeStruct((room, 4 * chan), f32)


def kept_shapes(span, order):
    return (
        jax.ShapeDtypeStruct((12, room, span), f32),
        jax.ShapeDtypeStruct(order, bf16),
        jax.ShapeDtypeStruct((2,), jnp.int32),
    )


kept_specs = (vmem, vmem, smem)


def feature_shapes(rows):
    return [jax.ShapeDtypeStruct((rows, width * chan), bf16) for width in (4, 2, 2, 2)]


def ready_call(layer, counts, ys, weights, order):
    operands = [counts, *ys, *weights[2:]] + ([] if layer == 0 else [order])
    shapes, outs, held = feature_shapes(own_span), [vmem] * 4, []
    if layer == 0:
        pairs, order, more = kept_shapes(own_span, (own_span, own_atoms))
        shapes += [pairs, pltpu.HBM(order.shape, order.dtype), more]
        outs += [vmem, hbm, smem]
        held = [pltpu.VMEM(order.shape, order.dtype), pltpu.SemaphoreType.DMA((1,))]
    return pl.pallas_call(
        functools.partial(ready_kernel, layer),
        out_shape=shapes,
        in_specs=[smem] + [vmem] * (len(operands) - 1),
        out_specs=outs,
        scratch_shapes=held,
        compiler_params=params,
        name=f"ready_part_{layer}",
    )(*operands)


def own_call(layer, counts, weights, feats, pairs, more):
    operands = [counts, *weights[:2], *feats, pairs, more]
    shapes, outs = [delta_shape], [vmem]
    held = [pltpu.VMEM((block * hidden, own_main), bf16)] * 8
    if layer == 0:
        shapes.append(pltpu.HBM(pairs.shape, pairs.dtype))
        outs.append(hbm)
        held.append(pltpu.SemaphoreType.DMA((1,)))
    return pl.pallas_call(
        functools.partial(own_kernel, layer),
        out_shape=shapes,
        in_specs=[smem] + [vmem] * (len(operands) - 2) + [smem],
        out_specs=outs,
        scratch_shapes=held,
        compiler_params=params,
        cost_estimate=cost(own_atoms),
        name=f"own_part_{layer}",
    )(*operands)


def side_call(layer, last, counts, low, high, own, delta, weights, readout, kept):
    operands = [counts, low, high, own, delta, *weights]
    specs = [smem] + [vmem] * (len(operands) - 1)
    shapes, outs = (jax.ShapeDtypeStruct((2 * slots, 4 * chan), bf16),), (vmem,)
    if last:
        operands += readout
        specs += [vmem] * 2
        shapes = (
            jax.ShapeDtypeStruct((2, slots, chan), bf16),
            jax.ShapeDtypeStruct((2, 3, slots, chan), bf16),
            jax.ShapeDtypeStruct((chan, chan), f32),
        )
        outs = (vmem,) * 3
    held = scratch(2 * side_span, side_main) + [pltpu.VMEM(delta_shape.shape, f32)]
    if layer == 0:
        pairs, order, more = kept_shapes(side_span, (2, side_span, side_atoms))
        shapes += (pairs, pltpu.HBM(order.shape, order.dtype), more)
        outs += (vmem, hbm, smem)
        held += [pltpu.VMEM(order.shape, order.dtype), pltpu.SemaphoreType.DMA((1,))]
    else:
        operands += kept
        specs += kept_specs
    return pl.pallas_call(
        functools.partial(side_kernel, layer, last),
        out_shape=shapes,
        in_specs=specs,
        out_specs=outs,
        scratch_shapes=held,
        compiler_params=params,
        cost_estimate=cost(side_atoms),
        name=f"side_part_{layer}",
    )(*operands)


def pack_kernel(counts_in, position_in, scalar_in, vector_in, out_ref, counts_ref, place, done):
    copies = [(counts_in, counts_ref), (position_in, place)]
    for q in range(2):
        copies.append((scalar_in.at[q], out_ref.at[q, :, pl.ds(0, chan)]))
        for k in range(3):
            at = pl.ds((k + 1) * chan, chan)
            copies.append((vector_in.at[q, k], out_ref.at[q, :, at]))
    copies = [pltpu.make_async_copy(*c, done.at[n]) for n, c in enumerate(copies)]
    for copy in copies:
        copy.start()
    for copy in copies:
        copy.wait()
    row, lane = iotas((2, slots))
    live = flag(lane < jnp.where(row == 0, counts_ref[0], counts_ref[1]))
    rest = jnp.concatenate([place[q, k] for k in range(3) for q in range(2)] + [live], axis=0)
    addends = []
    for _ in range(3):
        addends.append(rest.astype(bf16).astype(f32))
        rest = rest - addends[-1]
    addends = jnp.concatenate(addends, axis=0).astype(bf16)
    row, lane = iotas((24, chan))
    target = (row // 8) * 8 + (row % 8) // 2
    for q in range(2):
        spread = flag((lane == target) & (row % 2 == q)).astype(bf16)
        geo = lax.dot_general(
            addends, spread, (((0,), (0,)), ((), ())), preferred_element_type=f32
        )
        out_ref[q, :, 4 * chan :] = geo.astype(bf16)


def pack_call(*operands):
    operands = [pltpu.with_memory_space_constraint(x, pltpu.HBM) for x in operands]
    return pl.pallas_call(
        pack_kernel,
        out_shape=jax.ShapeDtypeStruct((2, slots, 5 * chan), bf16),
        in_specs=[hbm] * 4,
        out_specs=vmem,
        scratch_shapes=[
            pltpu.SMEM((2,), jnp.int32),
            pltpu.VMEM((2, 3, 1, slots), f32),
            pltpu.SemaphoreType.DMA((10,)),
        ],
        compiler_params=pltpu.CompilerParams(vmem_limit_bytes=4 * 1024 * 1024),
        name="pack",
    )(*operands)


def shifted(value, axis, step):
    count = lax.axis_size(axis)
    return lax.ppermute(value, axis, [((i + step) % count, i) for i in range(count)])


def radial_rows(radial_in, radial_bias):
    layers = radial_in.shape[0]
    eye = jnp.asarray(np.eye(block) * 0.5, bf16)
    spread = radial_in.transpose(0, 2, 1)[:, None, :, :, None] * eye[:, None, None, :]
    spread = spread.reshape(layers, block * hidden, 8 * block)
    bias = jnp.stack([p * jnp.asarray(0.5, bf16) for p in pieces(radial_bias)], axis=2)
    bias = jnp.broadcast_to(bias[:, None], (layers, block, hidden, 3))
    bias = bias.reshape(layers, block * hidden, 3)
    return jnp.pad(
        jnp.concatenate([spread, bias], axis=2), ((0, 0), (0, 0), (0, depth - 8 * block - 3))
    )


def on_device(
    positions,
    counts,
    scalars,
    vectors,
    radial_in,
    radial_bias,
    radial_out,
    atom_in,
    atom_bias,
    atom_out,
    readout_in,
    readout_out,
):
    counts = counts.reshape(2)
    own = pack_call(
        counts,
        positions.reshape(2, 3, 1, slots),
        scalars.reshape(2, slots, chan),
        vectors.reshape(2, slots, 3, chan).transpose(0, 2, 1, 3),
    )
    layers = radial_in.shape[0]
    side_kept = ()
    for layer in range(layers):
        last = layer == layers - 1
        y = jnp.stack([shifted(own, "gz", -1), own, shifted(own, "gz", 1)], axis=1)
        if layer == 0:
            y, radial_in, radial_bias = lax.optimization_barrier((y, radial_in, radial_bias))
            rin = radial_rows(radial_in, radial_bias)
            weights = [rin, radial_out, atom_in, atom_bias, atom_out]
        ys = [shifted(y, "gy", -1), y, shifted(y, "gy", 1)]
        if layer == 0:
            *feats, pairs, order, more = ready_call(layer, counts, ys, weights, None)
        else:
            feats = ready_call(layer, counts, ys, weights, order)
        low, high = jnp.stack([v[1] for v in ys]), jnp.stack([v[0] for v in ys])
        low, high, feats = lax.optimization_barrier((low, high, feats))
        low, high = shifted(low, "gx", -1), shifted(high, "gx", 1)
        delta, *kept = own_call(layer, counts, weights, feats, pairs, more)
        if layer == 0:
            pairs = kept[0]
        readout = [readout_in, readout_out[None, :]]
        state, *kept = side_call(
            layer, last, counts, low, high, own, delta, weights, readout, side_kept
        )
        if last:
            vector_state, energy = kept
        else:
            side_kept = side_kept or kept
            own = state.reshape(2, slots, 4 * chan)
    scalar_state = state.reshape(scalars.shape)
    vector_state = vector_state.transpose(0, 2, 1, 3).reshape(vectors.shape)
    every = lax.all_to_all(energy, ("gx", "gy", "gz"), 0, 0, tiled=True)
    energy = jnp.sum(every, axis=0)[:1]
    return scalar_state, vector_state, energy


def solution(mesh):
    in_specs = (
        P("gx", "gy", "gz", None, None),
        P("gx", "gy", "gz"),
        P("gx", "gy", "gz", None, None),
        P("gx", "gy", "gz", None, None, None),
        P(),
        P(),
        P(),
        P(),
        P(),
        P(),
        P(),
        P(),
    )
    out_specs = (P("gx", "gy", "gz", None, None), P("gx", "gy", "gz", None, None, None), P())
    return jax.shard_map(
        on_device, mesh=mesh, in_specs=in_specs, out_specs=out_specs, check_vma=False
    )
```

```python
import functools
import math

import jax
import jax.numpy as jnp
import numpy as np
from jax import lax
from jax.experimental import pallas as pl
from jax.experimental.pallas import tpu as pltpu
from jax.sharding import PartitionSpec as P

cutoff = 5.0
message_scale = 0.5
slots = 32
chan = 128
hidden = 64
block = 8
room = 2 * slots + block
depth = 80
own_atoms, own_main, own_span = 576, 512, 640
side_atoms, side_main, side_span = 288, 256, 384
f32 = jnp.float32
bf16 = jnp.bfloat16
across = (((1,), (1,)), ((), ()))


def pieces(value):
    high = lax.reduce_precision(value, 8, 7)
    rest = value - high
    middle = lax.reduce_precision(rest, 8, 7)
    low = lax.reduce_precision(rest - middle, 8, 7)
    return high.astype(bf16), middle.astype(bf16), low.astype(bf16)


def dot(a, b):
    return jnp.dot(a, b, preferred_element_type=f32)


def half_silu(y):
    return y + y * jnp.tanh(y)


def iotas(shape):
    return lax.broadcasted_iota(jnp.int32, shape, 0), lax.broadcasted_iota(jnp.int32, shape, 1)


def flag(condition):
    return jnp.where(condition, 1.0, 0.0)


def rows_of(geo):
    row, lane = iotas((8, chan))
    pick = flag((lane == row) | (lane == row + 8) | (lane == row + 16)).astype(bf16)
    return lax.dot_general(pick, geo, across, preferred_element_type=f32)


def columns_of(geo):
    row, lane = iotas((chan, chan))
    pick = flag((lane == row) | (lane + 8 == row) | (lane + 16 == row)).astype(bf16)
    return dot(geo, pick)


def own_table(y):
    row, lane = iotas((own_atoms // 3, chan))
    plane = flag(row >= 3 * slots)
    row = jnp.where(row >= 3 * slots, row - 3 * slots, row)
    z = flag(row >= slots) + flag(row >= 2 * slots) - 1.0
    table = jnp.where(lane == 4, plane * cutoff, 0.0) + jnp.where(lane == 6, z * cutoff, 0.0)
    table += jnp.where(lane == 5, (y - 1) * cutoff, 0.0)
    if y == 1:
        name = (row - slots + 1).astype(f32) + plane * slots
        table += jnp.where((lane == 7) & (z == 0.0), name, 0.0)
    return table.astype(bf16)


def side_table():
    row, lane = iotas((side_atoms, chan))
    y = flag(row >= 3 * slots) + flag(row >= 6 * slots) - 1.0
    row = row.astype(f32) - (y + 1.0) * (3 * slots)
    z = flag(row >= slots) + flag(row >= 2 * slots) - 1.0
    table = jnp.where(lane == 5, y * cutoff, 0.0) + jnp.where(lane == 6, z * cutoff, 0.0)
    return table.astype(bf16)


def compaction(live, span):
    atoms = live.shape[0]
    ranks = []
    total = jnp.zeros((1, 1), f32)
    for at in range(0, atoms, chan):
        part = live[at : at + chan]
        row, lane = iotas((part.shape[0], part.shape[0]))
        before = jnp.sum(jnp.where(row < lane, part, 0.0), axis=0, keepdims=True)
        own = jnp.sum(jnp.where(row == lane, part, 0.0), axis=0, keepdims=True)
        ranks.append(jnp.where(own > 0.5, before + total, -1.0))
        total = total + jnp.sum(part, axis=0, keepdims=True)
    rank = jnp.concatenate(ranks, axis=1)
    row = lax.broadcasted_iota(jnp.int32, (span, atoms), 0).astype(f32)
    return flag(row == rank).astype(bf16), total


def geometry(row, mine, number, shift, pairs_ref, at):
    dist2 = None
    disp = []
    for k in range(3):
        offset = row[4 + k : 5 + k] + shift if k == 0 else row[4 + k : 5 + k]
        d = (row[k : k + 1] + offset) - mine[:, k : k + 1]
        disp.append(d)
        dist2 = d * d if k == 0 else dist2 + d * d
    live = row[3:4]
    itself = flag(row[7:8] == number.astype(f32))
    dist2 = dist2 + itself + (1.0 - live)
    inverse = lax.rsqrt(dist2)
    dist = dist2 * inverse
    phase = 0.5 - dist * (1.0 / cutoff)
    square = phase * phase
    series = 0.0
    for k in range(6, -1, -1):
        series = series * square + 0.5 * (-1.0) ** k * math.pi ** (2 * k + 1) / math.factorial(2 * k + 1)
    smooth = jnp.where(dist < cutoff, 0.5 + phase * series, 0.0)
    weight = smooth * live * (1.0 - itself)
    scaled = weight * inverse
    pairs_ref[8, at, :] = weight
    for k in range(3):
        pairs_ref[9 + k, at, :] = scaled * disp[k]
    sharp = 0.5 * (7.0 / cutoff) ** 2 / math.log(2.0)
    for k in range(8):
        away = dist - k * (cutoff / 7.0)
        pairs_ref[k, at, :] = jnp.exp2(away * away * -sharp)


def features(layer, x, part, weights, feats):
    _, _, ain_ref, abias_ref, aout_ref = weights
    s = x[:, :chan]
    bias = abias_ref[layer : layer + 1, :]
    hid = half_silu(0.5 * (dot(s, ain_ref[layer]) + bias)).astype(bf16)
    gates = dot(hid, aout_ref[layer]).astype(bf16)
    ga, gb = gates[:, :chan], gates[:, chan : 2 * chan]
    gc, gg = gates[:, 2 * chan : 3 * chan], gates[:, 3 * chan :]
    vec = [x[:, (k + 1) * chan : (k + 2) * chan] for k in range(3)]
    feats[0][part, :] = jnp.concatenate([ga] + [gb * v for v in vec], axis=1)
    for k in range(3):
        feats[1 + k][part, :] = jnp.concatenate([gc, gg * vec[k]], axis=1)


def messages(layer, count, place, window, weights, pairs_ref, feats, edges, delta, fill=None):
    rin_ref, rout_ref = weights[:2]
    width = window.stop - window.start
    even, odd = edges[:4], edges[4:]

    def rows_at(b):
        return pl.ds(pl.multiple_of(place(b)[0], block), block)

    def hidden_of(b):
        slab = pairs_ref[0:8, rows_at(b), window].reshape(8 * block, width)
        slab = jnp.concatenate([slab, jnp.ones((depth - 8 * block, width), f32)], axis=0)
        return dot(rin_ref[layer], slab.astype(bf16)), pairs_ref[8:12, rows_at(b), window]

    def edge(r, y, w, out):
        part = slice(r * hidden, (r + 1) * hidden)
        s = half_silu(y[part]).astype(bf16).reshape(4, 16, width)
        for g in range(4):
            line = jnp.broadcast_to(w[g][r : r + 1, :], (16, width)).astype(bf16)
            out[g][part, :width] = (s * line[None]).reshape(hidden, width)

    def product(n, used, atoms):
        if n < 2:
            return dot(used[0][:, :width], feats[0][atoms, 2 * n * chan : 2 * (n + 1) * chan])
        return dot(used[n - 1][:, :width], feats[n - 1][atoms, :])

    def gather(n, result, radial, sums):
        groups = ((0, 1), (1, 1), (2, 3), (2, 3), (2, 3))[n]
        targets = ((0, 1), (2, 3), (1, 0), (2, 0), (3, 0))[n]
        for half in range(2):
            value = result[:, half * chan : (half + 1) * chan].reshape(block, hidden, chan)
            value = jnp.sum(value * radial[groups[half]], axis=1)
            t = targets[half]
            sums[t] = value if sums[t] is None else sums[t] + value

    def step(b, used, following):
        radial = [rout_ref[layer, :, g * chan : (g + 1) * chan].astype(f32)[None] for g in range(4)]
        sums = [None] * 4
        atoms = pl.ds(pl.multiple_of(place(b)[1], chan), width)
        if following is not None:
            y, w = hidden_of(b + 1)
        made, previous = 0, None
        for n in range(5):
            result = product(n, used, atoms)
            while following is not None and made < block and made * 5 < (n + 1) * block:
                edge(made, y, w, following)
                made += 1
            if n > 0:
                gather(n - 1, previous, radial, sums)
            previous = result
        gather(4, previous, radial, sums)
        for g in range(4):
            delta[rows_at(b), g * chan : (g + 1) * chan] += sums[g]

    if fill is not None and layer == 0:
        fill()
    y, w = hidden_of(0)
    for r in range(block):
        edge(r, y, w, even)
    if fill is not None and layer > 0:
        fill()

    def two_steps(t, carry):
        step(2 * t, even, odd)
        step(2 * t + 1, odd, even)
        return carry

    lax.fori_loop(0, count // 2, two_steps, 0)

    @pl.when(count % 2 == 1)
    def _():
        step(count - 1, even, None)


def packed_features(layer, ys, order, part, weights, feats):
    third = own_atoms // 3
    x = None
    for n, ref in enumerate(ys):
        atoms = ref[...].reshape(third, -1)[:, : 4 * chan]
        y = dot(order[part, n * third : (n + 1) * third], atoms)
        x = y if n == 0 else x + y
    features(layer, x.astype(bf16), part, weights, feats)


def geometry_kernel(counts_ref, low, middle, high, pairs, order, more):
    geo = [
        ref[...].reshape(own_atoms // 3, -1)[:, 4 * chan :] + own_table(n)
        for n, ref in enumerate((low, middle, high))
    ]
    geo = jnp.concatenate(geo, axis=0)
    order[...], total = compaction(geo[:, 3:4].astype(f32), own_span)
    row = rows_of(dot(order[...], geo).astype(bf16))
    more[0] = jnp.where(jnp.sum(total) > own_main + 0.5, 1, 0)
    first = counts_ref[0]
    mine = columns_of(jnp.concatenate([middle[q, 1][:, 4 * chan :] for q in range(2)], axis=0))
    place = lax.broadcasted_iota(jnp.int32, (2 * slots, 1), 0)
    moved = pltpu.roll(mine, lax.rem(first + slots, 2 * slots), 0)
    mine = jnp.where(place < first, mine, moved)
    number = jnp.where(place < first, place + 1, place - first + (slots + 1))
    shift = jnp.where(place < first, 0.0, -cutoff)
    geometry(row, mine, number, shift, pairs, slice(0, 2 * slots))


def feature_kernel(layer, low, middle, high, ain_ref, abias_ref, aout_ref, order, *feats):
    weights = (None, None, ain_ref, abias_ref, aout_ref)
    packed_features(layer, (low, middle, high), order, slice(0, own_span), weights, feats)


def own_kernel(layer, *refs):
    counts_ref, weights, refs = refs[0], refs[1:6], refs[6:]
    if layer == 0:
        ys, order, refs = refs[:3], refs[3], refs[4:]
        pairs, more, delta, pairs_out, order_out = refs[:5]
        feats, edges, done = refs[5:9], refs[9:17], refs[17]
        keep = [
            pltpu.make_async_copy(pairs, pairs_out, done.at[0]),
            pltpu.make_async_copy(order, order_out, done.at[1]),
        ]
        for copy in keep:
            copy.start()
    else:
        feats, (pairs, more, delta), edges = refs[:4], refs[4:7], refs[7:]
    count = (counts_ref[0] + counts_ref[1] + block - 1) // block
    delta[...] = jnp.zeros_like(delta)

    def add(part):
        def fill():
            packed_features(layer, ys, order, part, weights, feats)

        messages(
            layer,
            count,
            lambda b: (b * block, part.start),
            part,
            weights,
            pairs,
            feats,
            edges,
            delta,
            fill if layer == 0 else None,
        )

    add(slice(0, own_main))

    @pl.when(more[0] > 0)
    def _():
        add(slice(own_main, own_span))

    if layer == 0:
        for copy in keep:
            copy.wait()


def side_kernel(layer, last, *refs):
    counts_ref, low, high, own_ref, before = refs[:5]
    weights = refs[5:10]
    refs = refs[10:]
    if last:
        read_in_ref, read_out_ref = refs[:2]
        refs = refs[2:]
    if layer > 0:
        (pairs, order, more), refs = refs[:3], refs[3:]
    if last:
        (scalar_ref, vector_ref, energy_ref), refs = refs[:3], refs[3:]
    else:
        state_ref, refs = refs[0], refs[1:]
    if layer == 0:
        (pairs, order_out, more), refs = refs[:3], refs[3:]
        order, done = refs[13:]
    feats, edges, delta = refs[:4], refs[4:12], refs[12]
    delta[...] = jnp.zeros_like(delta)
    main, rest = slice(0, side_main), slice(side_main, side_span)
    atoms = [ref[...].reshape(side_atoms, -1) for ref in (low, high)]
    if layer == 0:
        total = []
        for q in range(2):
            geo = atoms[q][:, 4 * chan :] + side_table()
            order[q], number = compaction(geo[:, 3:4].astype(f32), side_span)
            total.append(jnp.sum(number))
            row = rows_of(dot(order[q], geo).astype(bf16))
            mine = columns_of(own_ref[q][:, 4 * chan :])
            at = slice(q * slots, (q + 1) * slots)
            number = lax.broadcasted_iota(jnp.int32, (slots, 1), 0) + (q * slots + 1)
            geometry(row, mine, number, (-cutoff, cutoff)[q], pairs, at)
        more[0] = jnp.where(jnp.maximum(total[0], total[1]) > side_main + 0.5, 1, 0)
        keep = pltpu.make_async_copy(order, order_out, done.at[0])
        keep.start()
    below = (counts_ref[0] + block - 1) // block
    above = (counts_ref[1] + block - 1) // block

    def add(part):
        def fill():
            for q in range(2):
                x = dot(order[q, part, :], atoms[q][:, : 4 * chan])
                rows = slice(q * side_span + part.start, q * side_span + part.stop)
                features(layer, x.astype(bf16), rows, weights, feats)

        def place(b):
            q = jnp.where(b >= below, 1, 0)
            return b * block + q * (slots - below * block), q * side_span + part.start

        messages(layer, below + above, place, part, weights, pairs, feats, edges, delta, fill)

    add(main)

    @pl.when(more[0] > 0)
    def _():
        add(rest)

    slot = lax.broadcasted_iota(jnp.int32, (2 * slots, 1), 0)
    limit = jnp.where(slot < slots, counts_ref[0], counts_ref[1] + slots)
    live = flag(slot < limit)
    mine = own_ref[...].reshape(2 * slots, -1)[:, : 4 * chan].astype(f32)
    packed = before[0 : 2 * slots, :]
    moved = pltpu.roll(packed, slots - counts_ref[0], 0)
    change = delta[0 : 2 * slots, :] + jnp.where(slot < slots, packed, moved)
    state = ((mine + message_scale * change) * live).astype(bf16)
    if layer == 0:
        keep.wait()
    if not last:
        state_ref[...] = state
    else:
        for q in range(2):
            at = slice(q * slots, (q + 1) * slots)
            scalar_ref[q] = state[at, :chan]
            for k in range(3):
                vector_ref[q, k] = state[at, (k + 1) * chan : (k + 2) * chan]
        x = dot(state[:, :chan], read_in_ref[...])
        each = half_silu(0.5 * x) * read_out_ref[...] * live
        energy_ref[...] = jnp.broadcast_to(jnp.sum(each, keepdims=True), energy_ref.shape)


vmem = pl.BlockSpec(memory_space=pltpu.VMEM)
smem = pl.BlockSpec(memory_space=pltpu.SMEM)
hbm = pl.BlockSpec(memory_space=pltpu.HBM)


def scratch(rows, main):
    return [
        pltpu.VMEM((rows, 4 * chan), bf16),
        *[pltpu.VMEM((rows, 2 * chan), bf16)] * 3,
        *[pltpu.VMEM((block * hidden, main), bf16)] * 8,
    ]


def cost(atoms):
    return pl.CostEstimate(
        flops=2 * 2 * slots * atoms * 81920, bytes_accessed=4000000, transcendentals=4000000
    )


params = pltpu.CompilerParams(vmem_limit_bytes=24 * 1024 * 1024)
delta_shape = jax.ShapeDtypeStruct((room, 4 * chan), f32)


def kept_shapes(span, order):
    return (
        jax.ShapeDtypeStruct((12, room, span), f32),
        jax.ShapeDtypeStruct(order, bf16),
        jax.ShapeDtypeStruct((2,), jnp.int32),
    )


kept_specs = (vmem, vmem, smem)


def feature_shapes(rows):
    return [jax.ShapeDtypeStruct((rows, width * chan), bf16) for width in (4, 2, 2, 2)]


def geometry_call(counts, ys):
    return pl.pallas_call(
        geometry_kernel,
        out_shape=kept_shapes(own_span, (own_span, own_atoms)),
        in_specs=[smem] + [vmem] * 3,
        out_specs=kept_specs,
        compiler_params=params,
        name="geometry_part",
    )(counts, *ys)


def feature_call(layer, ys, weights, order):
    return pl.pallas_call(
        functools.partial(feature_kernel, layer),
        out_shape=feature_shapes(own_span),
        in_specs=[vmem] * 7,
        out_specs=[vmem] * 4,
        compiler_params=params,
        name=f"feature_part_{layer}",
    )(*ys, *weights[2:], order)


def own_call(layer, counts, weights, given, pairs, more):
    operands = [counts, *weights, *given, pairs, more]
    shapes, outs = [delta_shape], [vmem]
    held = [pltpu.VMEM((block * hidden, own_main), bf16)] * 8
    if layer == 0:
        shapes += [pltpu.HBM(x.shape, x.dtype) for x in (pairs, given[3])]
        outs += [hbm, hbm]
        held = [pltpu.VMEM(f.shape, f.dtype) for f in feature_shapes(own_span)] + held
        held.append(pltpu.SemaphoreType.DMA((2,)))
    return pl.pallas_call(
        functools.partial(own_kernel, layer),
        out_shape=shapes,
        in_specs=[smem] + [vmem] * (len(operands) - 2) + [smem],
        out_specs=outs,
        scratch_shapes=held,
        compiler_params=params,
        cost_estimate=cost(own_atoms),
        name=f"own_part_{layer}",
    )(*operands)


def side_call(layer, last, counts, low, high, own, delta, weights, readout, kept):
    operands = [counts, low, high, own, delta, *weights]
    specs = [smem] + [vmem] * (len(operands) - 1)
    shapes, outs = (jax.ShapeDtypeStruct((2 * slots, 4 * chan), bf16),), (vmem,)
    if last:
        operands += readout
        specs += [vmem] * 2
        shapes = (
            jax.ShapeDtypeStruct((2, slots, chan), bf16),
            jax.ShapeDtypeStruct((2, 3, slots, chan), bf16),
            jax.ShapeDtypeStruct((chan, chan), f32),
        )
        outs = (vmem,) * 3
    held = scratch(2 * side_span, side_main) + [pltpu.VMEM(delta_shape.shape, f32)]
    if layer == 0:
        pairs, order, more = kept_shapes(side_span, (2, side_span, side_atoms))
        shapes += (pairs, pltpu.HBM(order.shape, order.dtype), more)
        outs += (vmem, hbm, smem)
        held += [pltpu.VMEM(order.shape, order.dtype), pltpu.SemaphoreType.DMA((1,))]
    else:
        operands += kept
        specs += kept_specs
    return pl.pallas_call(
        functools.partial(side_kernel, layer, last),
        out_shape=shapes,
        in_specs=specs,
        out_specs=outs,
        scratch_shapes=held,
        compiler_params=params,
        cost_estimate=cost(side_atoms),
        name=f"side_part_{layer}",
    )(*operands)


def pack_kernel(counts_in, position_in, scalar_in, vector_in, out_ref, counts_ref, place, done):
    copies = [(counts_in, counts_ref), (position_in, place)]
    for q in range(2):
        copies.append((scalar_in.at[q], out_ref.at[q, :, pl.ds(0, chan)]))
        for k in range(3):
            at = pl.ds((k + 1) * chan, chan)
            copies.append((vector_in.at[q, k], out_ref.at[q, :, at]))
    copies = [pltpu.make_async_copy(*c, done.at[n]) for n, c in enumerate(copies)]
    for copy in copies:
        copy.start()
    for copy in copies:
        copy.wait()
    row, lane = iotas((2, slots))
    live = flag(lane < jnp.where(row == 0, counts_ref[0], counts_ref[1]))
    rest = jnp.concatenate([place[q, k] for k in range(3) for q in range(2)] + [live], axis=0)
    addends = []
    for _ in range(3):
        addends.append(rest.astype(bf16).astype(f32))
        rest = rest - addends[-1]
    addends = jnp.concatenate(addends, axis=0).astype(bf16)
    row, lane = iotas((24, chan))
    target = (row // 8) * 8 + (row % 8) // 2
    for q in range(2):
        spread = flag((lane == target) & (row % 2 == q)).astype(bf16)
        geo = lax.dot_general(
            addends, spread, (((0,), (0,)), ((), ())), preferred_element_type=f32
        )
        out_ref[q, :, 4 * chan :] = geo.astype(bf16)


def pack_call(*operands):
    operands = [pltpu.with_memory_space_constraint(x, pltpu.HBM) for x in operands]
    return pl.pallas_call(
        pack_kernel,
        out_shape=jax.ShapeDtypeStruct((2, slots, 5 * chan), bf16),
        in_specs=[hbm] * 4,
        out_specs=vmem,
        scratch_shapes=[
            pltpu.SMEM((2,), jnp.int32),
            pltpu.VMEM((2, 3, 1, slots), f32),
            pltpu.SemaphoreType.DMA((10,)),
        ],
        compiler_params=pltpu.CompilerParams(vmem_limit_bytes=4 * 1024 * 1024),
        name="pack",
    )(*operands)


def shifted(value, axis, step):
    count = lax.axis_size(axis)
    return lax.ppermute(value, axis, [((i + step) % count, i) for i in range(count)])


def radial_rows(radial_in, radial_bias):
    layers = radial_in.shape[0]
    eye = jnp.asarray(np.eye(block) * 0.5, bf16)
    spread = radial_in.transpose(0, 2, 1)[:, None, :, :, None] * eye[:, None, None, :]
    spread = spread.reshape(layers, block * hidden, 8 * block)
    bias = jnp.stack([p * jnp.asarray(0.5, bf16) for p in pieces(radial_bias)], axis=2)
    bias = jnp.broadcast_to(bias[:, None], (layers, block, hidden, 3))
    bias = bias.reshape(layers, block * hidden, 3)
    return jnp.pad(
        jnp.concatenate([spread, bias], axis=2), ((0, 0), (0, 0), (0, depth - 8 * block - 3))
    )


def on_device(
    positions,
    counts,
    scalars,
    vectors,
    radial_in,
    radial_bias,
    radial_out,
    atom_in,
    atom_bias,
    atom_out,
    readout_in,
    readout_out,
):
    counts = counts.reshape(2)
    own = pack_call(
        counts,
        positions.reshape(2, 3, 1, slots),
        scalars.reshape(2, slots, chan),
        vectors.reshape(2, slots, 3, chan).transpose(0, 2, 1, 3),
    )
    layers = radial_in.shape[0]
    side_kept = ()
    for layer in range(layers):
        last = layer == layers - 1
        y = jnp.stack([shifted(own, "gz", -1), own, shifted(own, "gz", 1)], axis=1)
        if layer == 0:
            y, radial_in, radial_bias = lax.optimization_barrier((y, radial_in, radial_bias))
            rin = radial_rows(radial_in, radial_bias)
            weights = [rin, radial_out, atom_in, atom_bias, atom_out]
        ys = [shifted(y, "gy", -1), y, shifted(y, "gy", 1)]
        low, high = jnp.stack([v[1] for v in ys]), jnp.stack([v[0] for v in ys])
        if layer == 0:
            pairs, order, more = geometry_call(counts, ys)
            low, high, pairs = lax.optimization_barrier((low, high, pairs))
            given = [*ys, order]
        else:
            given = feature_call(layer, ys, weights, order)
            low, high, given = lax.optimization_barrier((low, high, given))
        low, high = shifted(low, "gx", -1), shifted(high, "gx", 1)
        delta, *kept = own_call(layer, counts, weights, given, pairs, more)
        if layer == 0:
            pairs, order = kept
        readout = [readout_in, readout_out[None, :]]
        state, *kept = side_call(
            layer, last, counts, low, high, own, delta, weights, readout, side_kept
        )
        if last:
            vector_state, energy = kept
        else:
            side_kept = side_kept or kept
            own = state.reshape(2, slots, 4 * chan)
    scalar_state = state.reshape(scalars.shape)
    vector_state = vector_state.transpose(0, 2, 1, 3).reshape(vectors.shape)
    every = lax.all_to_all(energy, ("gx", "gy", "gz"), 0, 0, tiled=True)
    energy = jnp.sum(every, axis=0)[:1]
    return scalar_state, vector_state, energy


def solution(mesh):
    in_specs = (
        P("gx", "gy", "gz", None, None),
        P("gx", "gy", "gz"),
        P("gx", "gy", "gz", None, None),
        P("gx", "gy", "gz", None, None, None),
        P(),
        P(),
        P(),
        P(),
        P(),
        P(),
        P(),
        P(),
    )
    out_specs = (P("gx", "gy", "gz", None, None), P("gx", "gy", "gz", None, None, None), P())
    return jax.shard_map(
        on_device, mesh=mesh, in_specs=in_specs, out_specs=out_specs, check_vma=False
    )
```

```python
import functools
import math

import jax
import jax.numpy as jnp
import numpy as np
from jax import lax
from jax.experimental import pallas as pl
from jax.experimental.pallas import tpu as pltpu
from jax.sharding import PartitionSpec as P

cutoff = 5.0
message_scale = 0.5
slots = 32
chan = 128
hidden = 64
block = 8
room = 2 * slots + block
depth = 80
own_atoms, own_main, own_span = 576, 512, 640
side_atoms, side_main, side_span = 288, 256, 384
f32 = jnp.float32
bf16 = jnp.bfloat16
across = (((1,), (1,)), ((), ()))


def pieces(value):
    high = lax.reduce_precision(value, 8, 7)
    rest = value - high
    middle = lax.reduce_precision(rest, 8, 7)
    low = lax.reduce_precision(rest - middle, 8, 7)
    return high.astype(bf16), middle.astype(bf16), low.astype(bf16)


def dot(a, b):
    return jnp.dot(a, b, preferred_element_type=f32)


def half_silu(y):
    return y + y * jnp.tanh(y)


def iotas(shape):
    return lax.broadcasted_iota(jnp.int32, shape, 0), lax.broadcasted_iota(jnp.int32, shape, 1)


def flag(condition):
    return jnp.where(condition, 1.0, 0.0)


def rows_of(geo):
    row, lane = iotas((8, chan))
    pick = flag((lane == row) | (lane == row + 8) | (lane == row + 16)).astype(bf16)
    return lax.dot_general(pick, geo, across, preferred_element_type=f32)


def columns_of(geo):
    row, lane = iotas((chan, chan))
    pick = flag((lane == row) | (lane + 8 == row) | (lane + 16 == row)).astype(bf16)
    return dot(geo, pick)


def own_table(y):
    row, lane = iotas((own_atoms // 3, chan))
    plane = flag(row >= 3 * slots)
    row = jnp.where(row >= 3 * slots, row - 3 * slots, row)
    z = flag(row >= slots) + flag(row >= 2 * slots) - 1.0
    table = jnp.where(lane == 4, plane * cutoff, 0.0) + jnp.where(lane == 6, z * cutoff, 0.0)
    table += jnp.where(lane == 5, (y - 1) * cutoff, 0.0)
    if y == 1:
        name = (row - slots + 1).astype(f32) + plane * slots
        table += jnp.where((lane == 7) & (z == 0.0), name, 0.0)
    return table.astype(bf16)


def side_table():
    row, lane = iotas((side_atoms, chan))
    y = flag(row >= 3 * slots) + flag(row >= 6 * slots) - 1.0
    row = row.astype(f32) - (y + 1.0) * (3 * slots)
    z = flag(row >= slots) + flag(row >= 2 * slots) - 1.0
    table = jnp.where(lane == 5, y * cutoff, 0.0) + jnp.where(lane == 6, z * cutoff, 0.0)
    return table.astype(bf16)


def compaction(live, span):
    atoms = live.shape[0]
    ranks = []
    total = jnp.zeros((1, 1), f32)
    for at in range(0, atoms, chan):
        part = live[at : at + chan]
        row, lane = iotas((part.shape[0], part.shape[0]))
        before = jnp.sum(jnp.where(row < lane, part, 0.0), axis=0, keepdims=True)
        own = jnp.sum(jnp.where(row == lane, part, 0.0), axis=0, keepdims=True)
        ranks.append(jnp.where(own > 0.5, before + total, -1.0))
        total = total + jnp.sum(part, axis=0, keepdims=True)
    rank = jnp.concatenate(ranks, axis=1)
    row = lax.broadcasted_iota(jnp.int32, (span, atoms), 0).astype(f32)
    return flag(row == rank).astype(bf16), total


def geometry(row, mine, number, shift, pairs_ref, at):
    dist2 = None
    disp = []
    for k in range(3):
        offset = row[4 + k : 5 + k] + shift if k == 0 else row[4 + k : 5 + k]
        d = (row[k : k + 1] + offset) - mine[:, k : k + 1]
        disp.append(d)
        dist2 = d * d if k == 0 else dist2 + d * d
    live = row[3:4]
    itself = flag(row[7:8] == number.astype(f32))
    dist2 = dist2 + itself + (1.0 - live)
    inverse = lax.rsqrt(dist2)
    dist = dist2 * inverse
    phase = 0.5 - dist * (1.0 / cutoff)
    square = phase * phase
    series = 0.0
    for k in range(6, -1, -1):
        series = series * square + 0.5 * (-1.0) ** k * math.pi ** (2 * k + 1) / math.factorial(2 * k + 1)
    smooth = jnp.where(dist < cutoff, 0.5 + phase * series, 0.0)
    weight = smooth * live * (1.0 - itself)
    scaled = weight * inverse
    pairs_ref[8, at, :] = weight
    for k in range(3):
        pairs_ref[9 + k, at, :] = scaled * disp[k]
    sharp = 0.5 * (7.0 / cutoff) ** 2 / math.log(2.0)
    for k in range(8):
        away = dist - k * (cutoff / 7.0)
        pairs_ref[k, at, :] = jnp.exp2(away * away * -sharp)


def features(layer, x, part, weights, feats):
    _, _, ain_ref, abias_ref, aout_ref = weights
    s = x[:, :chan]
    bias = abias_ref[layer : layer + 1, :]
    hid = half_silu(0.5 * (dot(s, ain_ref[layer]) + bias)).astype(bf16)
    gates = dot(hid, aout_ref[layer]).astype(bf16)
    ga, gb = gates[:, :chan], gates[:, chan : 2 * chan]
    gc, gg = gates[:, 2 * chan : 3 * chan], gates[:, 3 * chan :]
    vec = [x[:, (k + 1) * chan : (k + 2) * chan] for k in range(3)]
    feats[0][part, :] = jnp.concatenate([ga] + [gb * v for v in vec], axis=1)
    for k in range(3):
        feats[1 + k][part, :] = jnp.concatenate([gc, gg * vec[k]], axis=1)


def messages(layer, count, place, window, weights, pairs_ref, feats, edges, delta, fill=None):
    rin_ref, rout_ref = weights[:2]
    width = window.stop - window.start
    even, odd = edges[:4], edges[4:]

    def rows_at(b):
        return pl.ds(pl.multiple_of(place(b)[0], block), block)

    def hidden_of(b):
        slab = pairs_ref[0:8, rows_at(b), window].reshape(8 * block, width)
        slab = jnp.concatenate([slab, jnp.ones((depth - 8 * block, width), f32)], axis=0)
        return dot(rin_ref[layer], slab.astype(bf16)), pairs_ref[8:12, rows_at(b), window]

    def edge(r, y, w, out):
        part = slice(r * hidden, (r + 1) * hidden)
        s = half_silu(y[part]).astype(bf16).reshape(4, 16, width)
        for g in range(4):
            line = jnp.broadcast_to(w[g][r : r + 1, :], (16, width)).astype(bf16)
            out[g][part, :width] = (s * line[None]).reshape(hidden, width)

    def product(n, used, atoms):
        if n < 2:
            return dot(used[0][:, :width], feats[0][atoms, 2 * n * chan : 2 * (n + 1) * chan])
        return dot(used[n - 1][:, :width], feats[n - 1][atoms, :])

    def gather(n, result, radial, sums):
        groups = ((0, 1), (1, 1), (2, 3), (2, 3), (2, 3))[n]
        targets = ((0, 1), (2, 3), (1, 0), (2, 0), (3, 0))[n]
        for half in range(2):
            value = result[:, half * chan : (half + 1) * chan].reshape(block, hidden, chan)
            value = jnp.sum(value * radial[groups[half]], axis=1)
            t = targets[half]
            sums[t] = value if sums[t] is None else sums[t] + value

    def step(b, used, following):
        radial = [rout_ref[layer, :, g * chan : (g + 1) * chan].astype(f32)[None] for g in range(4)]
        sums = [None] * 4
        atoms = pl.ds(pl.multiple_of(place(b)[1], chan), width)
        if following is not None:
            y, w = hidden_of(b + 1)
        made, previous = 0, None
        for n in range(5):
            result = product(n, used, atoms)
            while following is not None and made < block and made * 5 < (n + 1) * block:
                edge(made, y, w, following)
                made += 1
            if n > 0:
                gather(n - 1, previous, radial, sums)
            previous = result
        gather(4, previous, radial, sums)
        for g in range(4):
            delta[rows_at(b), g * chan : (g + 1) * chan] += sums[g]

    if fill is not None and layer == 0:
        fill()
    y, w = hidden_of(0)
    for r in range(block):
        edge(r, y, w, even)
    if fill is not None and layer > 0:
        fill()

    def two_steps(t, carry):
        step(2 * t, even, odd)
        step(2 * t + 1, odd, even)
        return carry

    lax.fori_loop(0, count // 2, two_steps, 0)

    @pl.when(count % 2 == 1)
    def _():
        step(count - 1, even, None)


def packed_features(layer, ys, order, part, weights, feats):
    third = own_atoms // 3
    x = None
    for n, ref in enumerate(ys):
        atoms = ref[...].reshape(third, -1)[:, : 4 * chan]
        y = dot(order[part, n * third : (n + 1) * third], atoms)
        x = y if n == 0 else x + y
    features(layer, x.astype(bf16), part, weights, feats)


def geometry_kernel(counts_ref, low, middle, high, pairs, order, more):
    geo = [
        ref[...].reshape(own_atoms // 3, -1)[:, 4 * chan :] + own_table(n)
        for n, ref in enumerate((low, middle, high))
    ]
    geo = jnp.concatenate(geo, axis=0)
    order[...], total = compaction(geo[:, 3:4].astype(f32), own_span)
    row = rows_of(dot(order[...], geo).astype(bf16))
    more[0] = jnp.where(jnp.sum(total) > own_main + 0.5, 1, 0)
    first = counts_ref[0]
    mine = columns_of(jnp.concatenate([middle[q, 1][:, 4 * chan :] for q in range(2)], axis=0))
    place = lax.broadcasted_iota(jnp.int32, (2 * slots, 1), 0)
    moved = pltpu.roll(mine, lax.rem(first + slots, 2 * slots), 0)
    mine = jnp.where(place < first, mine, moved)
    number = jnp.where(place < first, place + 1, place - first + (slots + 1))
    shift = jnp.where(place < first, 0.0, -cutoff)
    geometry(row, mine, number, shift, pairs, slice(0, 2 * slots))


def feature_kernel(layer, low, middle, high, ain_ref, abias_ref, aout_ref, order, *feats):
    weights = (None, None, ain_ref, abias_ref, aout_ref)
    packed_features(layer, (low, middle, high), order, slice(0, own_span), weights, feats)


def own_kernel(layer, *refs):
    counts_ref, weights, refs = refs[0], refs[1:6], refs[6:]
    if layer == 0:
        ys, order, refs = refs[:3], refs[3], refs[4:]
        pairs, more, delta, pairs_out, order_out = refs[:5]
        feats, edges, done = refs[5:9], refs[9:17], refs[17]
        keep = [
            pltpu.make_async_copy(pairs, pairs_out, done.at[0]),
            pltpu.make_async_copy(order, order_out, done.at[1]),
        ]
        for copy in keep:
            copy.start()
    else:
        feats, (pairs, more, delta), edges = refs[:4], refs[4:7], refs[7:]
    count = (counts_ref[0] + counts_ref[1] + block - 1) // block
    delta[...] = jnp.zeros_like(delta)

    def add(part):
        def fill():
            packed_features(layer, ys, order, part, weights, feats)

        messages(
            layer,
            count,
            lambda b: (b * block, part.start),
            part,
            weights,
            pairs,
            feats,
            edges,
            delta,
            fill if layer == 0 else None,
        )

    add(slice(0, own_main))

    @pl.when(more[0] > 0)
    def _():
        add(slice(own_main, own_span))

    if layer == 0:
        for copy in keep:
            copy.wait()


def side_kernel(layer, last, *refs):
    counts_ref, *around = refs[:5]
    own_ref, before = refs[5:7]
    weights = refs[7:12]
    refs = refs[12:]
    if last:
        read_in_ref, read_out_ref = refs[:2]
        refs = refs[2:]
    if layer > 0:
        (pairs, order, more), refs = refs[:3], refs[3:]
    if last:
        (scalar_ref, vector_ref, energy_ref), refs = refs[:3], refs[3:]
    else:
        state_ref, refs = refs[0], refs[1:]
    if layer == 0:
        (pairs, order_out, more), refs = refs[:3], refs[3:]
        order, done = refs[13:]
    feats, edges, delta = refs[:4], refs[4:12], refs[12]
    delta[...] = jnp.zeros_like(delta)
    main, rest = slice(0, side_main), slice(side_main, side_span)
    third = side_atoms // 3
    atoms = []
    for middle, outer in (around[:2], around[2:]):
        rows = [ref.reshape(third, -1) for ref in (outer[0], middle[...], outer[1])]
        atoms.append(jnp.concatenate(rows, axis=0))
    if layer == 0:
        total = []
        for q in range(2):
            geo = atoms[q][:, 4 * chan :] + side_table()
            order[q], number = compaction(geo[:, 3:4].astype(f32), side_span)
            total.append(jnp.sum(number))
            row = rows_of(dot(order[q], geo).astype(bf16))
            mine = columns_of(own_ref[q][:, 4 * chan :])
            at = slice(q * slots, (q + 1) * slots)
            number = lax.broadcasted_iota(jnp.int32, (slots, 1), 0) + (q * slots + 1)
            geometry(row, mine, number, (-cutoff, cutoff)[q], pairs, at)
        more[0] = jnp.where(jnp.maximum(total[0], total[1]) > side_main + 0.5, 1, 0)
        keep = pltpu.make_async_copy(order, order_out, done.at[0])
        keep.start()
    below = (counts_ref[0] + block - 1) // block
    above = (counts_ref[1] + block - 1) // block

    def add(part):
        def fill():
            for q in range(2):
                x = dot(order[q, part, :], atoms[q][:, : 4 * chan])
                rows = slice(q * side_span + part.start, q * side_span + part.stop)
                features(layer, x.astype(bf16), rows, weights, feats)

        def place(b):
            q = jnp.where(b >= below, 1, 0)
            return b * block + q * (slots - below * block), q * side_span + part.start

        messages(layer, below + above, place, part, weights, pairs, feats, edges, delta, fill)

    add(main)

    @pl.when(more[0] > 0)
    def _():
        add(rest)

    slot = lax.broadcasted_iota(jnp.int32, (2 * slots, 1), 0)
    limit = jnp.where(slot < slots, counts_ref[0], counts_ref[1] + slots)
    live = flag(slot < limit)
    mine = own_ref[...].reshape(2 * slots, -1)[:, : 4 * chan].astype(f32)
    packed = before[0 : 2 * slots, :]
    moved = pltpu.roll(packed, slots - counts_ref[0], 0)
    change = delta[0 : 2 * slots, :] + jnp.where(slot < slots, packed, moved)
    state = ((mine + message_scale * change) * live).astype(bf16)
    if layer == 0:
        keep.wait()
    if not last:
        state_ref[...] = state
    else:
        for q in range(2):
            at = slice(q * slots, (q + 1) * slots)
            scalar_ref[q] = state[at, :chan]
            for k in range(3):
                vector_ref[q, k] = state[at, (k + 1) * chan : (k + 2) * chan]
        x = dot(state[:, :chan], read_in_ref[...])
        each = half_silu(0.5 * x) * read_out_ref[...] * live
        energy_ref[...] = jnp.broadcast_to(jnp.sum(each, keepdims=True), energy_ref.shape)


vmem = pl.BlockSpec(memory_space=pltpu.VMEM)
smem = pl.BlockSpec(memory_space=pltpu.SMEM)
hbm = pl.BlockSpec(memory_space=pltpu.HBM)


def scratch(rows, main):
    return [
        pltpu.VMEM((rows, 4 * chan), bf16),
        *[pltpu.VMEM((rows, 2 * chan), bf16)] * 3,
        *[pltpu.VMEM((block * hidden, main), bf16)] * 8,
    ]


def cost(atoms):
    return pl.CostEstimate(
        flops=2 * 2 * slots * atoms * 81920, bytes_accessed=4000000, transcendentals=4000000
    )


params = pltpu.CompilerParams(vmem_limit_bytes=24 * 1024 * 1024)
delta_shape = jax.ShapeDtypeStruct((room, 4 * chan), f32)


def kept_shapes(span, order):
    return (
        jax.ShapeDtypeStruct((12, room, span), f32),
        jax.ShapeDtypeStruct(order, bf16),
        jax.ShapeDtypeStruct((2,), jnp.int32),
    )


kept_specs = (vmem, vmem, smem)


def feature_shapes(rows):
    return [jax.ShapeDtypeStruct((rows, width * chan), bf16) for width in (4, 2, 2, 2)]


def geometry_call(counts, ys):
    return pl.pallas_call(
        geometry_kernel,
        out_shape=kept_shapes(own_span, (own_span, own_atoms)),
        in_specs=[smem] + [vmem] * 3,
        out_specs=kept_specs,
        compiler_params=params,
        name="geometry_part",
    )(counts, *ys)


def feature_call(layer, ys, weights, order):
    return pl.pallas_call(
        functools.partial(feature_kernel, layer),
        out_shape=feature_shapes(own_span),
        in_specs=[vmem] * 7,
        out_specs=[vmem] * 4,
        compiler_params=params,
        name=f"feature_part_{layer}",
    )(*ys, *weights[2:], order)


def own_call(layer, counts, weights, given, pairs, more):
    operands = [counts, *weights, *given, pairs, more]
    shapes, outs = [delta_shape], [vmem]
    held = [pltpu.VMEM((block * hidden, own_main), bf16)] * 8
    if layer == 0:
        shapes += [pltpu.HBM(x.shape, x.dtype) for x in (pairs, given[3])]
        outs += [hbm, hbm]
        held = [pltpu.VMEM(f.shape, f.dtype) for f in feature_shapes(own_span)] + held
        held.append(pltpu.SemaphoreType.DMA((2,)))
    return pl.pallas_call(
        functools.partial(own_kernel, layer),
        out_shape=shapes,
        in_specs=[smem] + [vmem] * (len(operands) - 2) + [smem],
        out_specs=outs,
        scratch_shapes=held,
        compiler_params=params,
        cost_estimate=cost(own_atoms),
        name=f"own_part_{layer}",
    )(*operands)


def side_call(layer, last, counts, around, own, delta, weights, readout, kept):
    operands = [counts, *around, own, delta, *weights]
    specs = [smem] + [vmem] * (len(operands) - 1)
    shapes, outs = (jax.ShapeDtypeStruct((2 * slots, 4 * chan), bf16),), (vmem,)
    if last:
        operands += readout
        specs += [vmem] * 2
        shapes = (
            jax.ShapeDtypeStruct((2, slots, chan), bf16),
            jax.ShapeDtypeStruct((2, 3, slots, chan), bf16),
            jax.ShapeDtypeStruct((chan, chan), f32),
        )
        outs = (vmem,) * 3
    held = scratch(2 * side_span, side_main) + [pltpu.VMEM(delta_shape.shape, f32)]
    if layer == 0:
        pairs, order, more = kept_shapes(side_span, (2, side_span, side_atoms))
        shapes += (pairs, pltpu.HBM(order.shape, order.dtype), more)
        outs += (vmem, hbm, smem)
        held += [pltpu.VMEM(order.shape, order.dtype), pltpu.SemaphoreType.DMA((1,))]
    else:
        operands += kept
        specs += kept_specs
    return pl.pallas_call(
        functools.partial(side_kernel, layer, last),
        out_shape=shapes,
        in_specs=specs,
        out_specs=outs,
        scratch_shapes=held,
        compiler_params=params,
        cost_estimate=cost(side_atoms),
        name=f"side_part_{layer}",
    )(*operands)


def pack_kernel(counts_in, position_in, scalar_in, vector_in, out_ref, counts_ref, place, done):
    copies = [(counts_in, counts_ref), (position_in, place)]
    for q in range(2):
        copies.append((scalar_in.at[q], out_ref.at[q, :, pl.ds(0, chan)]))
        for k in range(3):
            at = pl.ds((k + 1) * chan, chan)
            copies.append((vector_in.at[q, k], out_ref.at[q, :, at]))
    copies = [pltpu.make_async_copy(*c, done.at[n]) for n, c in enumerate(copies)]
    for copy in copies:
        copy.start()
    for copy in copies:
        copy.wait()
    row, lane = iotas((2, slots))
    live = flag(lane < jnp.where(row == 0, counts_ref[0], counts_ref[1]))
    rest = jnp.concatenate([place[q, k] for k in range(3) for q in range(2)] + [live], axis=0)
    addends = []
    for _ in range(3):
        addends.append(rest.astype(bf16).astype(f32))
        rest = rest - addends[-1]
    addends = jnp.concatenate(addends, axis=0).astype(bf16)
    row, lane = iotas((24, chan))
    target = (row // 8) * 8 + (row % 8) // 2
    for q in range(2):
        spread = flag((lane == target) & (row % 2 == q)).astype(bf16)
        geo = lax.dot_general(
            addends, spread, (((0,), (0,)), ((), ())), preferred_element_type=f32
        )
        out_ref[q, :, 4 * chan :] = geo.astype(bf16)


def pack_call(*operands):
    operands = [pltpu.with_memory_space_constraint(x, pltpu.HBM) for x in operands]
    return pl.pallas_call(
        pack_kernel,
        out_shape=jax.ShapeDtypeStruct((2, slots, 5 * chan), bf16),
        in_specs=[hbm] * 4,
        out_specs=vmem,
        scratch_shapes=[
            pltpu.SMEM((2,), jnp.int32),
            pltpu.VMEM((2, 3, 1, slots), f32),
            pltpu.SemaphoreType.DMA((10,)),
        ],
        compiler_params=pltpu.CompilerParams(vmem_limit_bytes=4 * 1024 * 1024),
        name="pack",
    )(*operands)


def shifted(value, axis, step):
    count = lax.axis_size(axis)
    return lax.ppermute(value, axis, [((i + step) % count, i) for i in range(count)])


def radial_rows(radial_in, radial_bias):
    layers = radial_in.shape[0]
    eye = jnp.asarray(np.eye(block) * 0.5, bf16)
    spread = radial_in.transpose(0, 2, 1)[:, None, :, :, None] * eye[:, None, None, :]
    spread = spread.reshape(layers, block * hidden, 8 * block)
    bias = jnp.stack([p * jnp.asarray(0.5, bf16) for p in pieces(radial_bias)], axis=2)
    bias = jnp.broadcast_to(bias[:, None], (layers, block, hidden, 3))
    bias = bias.reshape(layers, block * hidden, 3)
    return jnp.pad(
        jnp.concatenate([spread, bias], axis=2), ((0, 0), (0, 0), (0, depth - 8 * block - 3))
    )


def on_device(
    positions,
    counts,
    scalars,
    vectors,
    radial_in,
    radial_bias,
    radial_out,
    atom_in,
    atom_bias,
    atom_out,
    readout_in,
    readout_out,
):
    counts = counts.reshape(2)
    own = pack_call(
        counts,
        positions.reshape(2, 3, 1, slots),
        scalars.reshape(2, slots, chan),
        vectors.reshape(2, slots, 3, chan).transpose(0, 2, 1, 3),
    )
    layers = radial_in.shape[0]
    side_kept = ()
    for layer in range(layers):
        last = layer == layers - 1
        y = jnp.stack([shifted(own, "gz", -1), own, shifted(own, "gz", 1)], axis=1)
        if layer == 0:
            y, radial_in, radial_bias = lax.optimization_barrier((y, radial_in, radial_bias))
            rin = radial_rows(radial_in, radial_bias)
            weights = [rin, radial_out, atom_in, atom_bias, atom_out]
        ys = [shifted(y, "gy", -1), y, shifted(y, "gy", 1)]
        around = [shifted(y[1], "gx", -1), shifted(y[0], "gx", 1)]
        low, high = (jnp.stack([ys[0][p], ys[2][p]]) for p in (1, 0))
        if layer == 0:
            pairs, order, more = geometry_call(counts, ys)
            low, high, pairs = lax.optimization_barrier((low, high, pairs))
            given = [*ys, order]
        else:
            given = feature_call(layer, ys, weights, order)
            low, high, given = lax.optimization_barrier((low, high, given))
        around = [around[0], shifted(low, "gx", -1), around[1], shifted(high, "gx", 1)]
        delta, *kept = own_call(layer, counts, weights, given, pairs, more)
        if layer == 0:
            pairs, order = kept
        readout = [readout_in, readout_out[None, :]]
        state, *kept = side_call(
            layer, last, counts, around, own, delta, weights, readout, side_kept
        )
        if last:
            vector_state, energy = kept
        else:
            side_kept = side_kept or kept
            own = state.reshape(2, slots, 4 * chan)
    scalar_state = state.reshape(scalars.shape)
    vector_state = vector_state.transpose(0, 2, 1, 3).reshape(vectors.shape)
    every = lax.all_to_all(energy, ("gx", "gy", "gz"), 0, 0, tiled=True)
    energy = jnp.sum(every, axis=0)[:1]
    return scalar_state, vector_state, energy


def solution(mesh):
    in_specs = (
        P("gx", "gy", "gz", None, None),
        P("gx", "gy", "gz"),
        P("gx", "gy", "gz", None, None),
        P("gx", "gy", "gz", None, None, None),
        P(),
        P(),
        P(),
        P(),
        P(),
        P(),
        P(),
        P(),
    )
    out_specs = (P("gx", "gy", "gz", None, None), P("gx", "gy", "gz", None, None, None), P())
    return jax.shard_map(
        on_device, mesh=mesh, in_specs=in_specs, out_specs=out_specs, check_vma=False
    )
```
